32 devices in a mesh: dp: 8 (over y, x, core), kv: 4 (over z).
Axes of the slice: x: 2, y: 2, z: 4, core: 2. Of those that a mesh axis runs over, the one named last changes fastest.
Arguments:
- tokens_in: bfloat16 [8192, 2048], P('dp'), may hold values from -6 to 6
- attn_gain: float32 [2048], replicated, may hold values from 0.5 to 1.5
- w_query: bfloat16 [2048, 2048], P(None, 'kv'), may hold values from -0.125 to 0.125
- w_key: bfloat16 [2048, 256], P(None, 'kv'), may hold values from -0.125 to 0.125
- w_value: bfloat16 [2048, 256], P(None, 'kv'), may hold values from -0.125 to 0.125
- w_output: bfloat16 [4, 512, 2048], P('kv'), may hold values from -0.5 to 0.5
- mlp_gain: float32 [2048], replicated, may hold values from 0.5 to 1.5
- w_gate: bfloat16 [2048, 5632], P(None, 'kv'), may hold values from -0.125 to 0.125
- w_up: bfloat16 [2048, 5632], P(None, 'kv'), may hold values from -0.125 to 0.125
- w_down: bfloat16 [4, 1408, 2048], P('kv'), may hold values from -0.078125 to 0.078125
- counts: int32 [8], P('dp'), may hold values from 768 to 1024, as said below
- segments: int32 [8192], P('dp'), may hold values from 0 to 8191, as said below
- cotangent: bfloat16 [8192, 2048], P('dp'), may hold values from -6 to 6
Outputs:
- layer_out: bfloat16 [8192, 2048], P(('dp', 'kv'))
- grad_tokens: float32 [8192, 2048], P(('dp', 'kv'))
- grad_attn_gain: float32 [2048], P('dp')
- grad_query_w: float32 [2048, 2048], P('dp', 'kv')
- grad_key_w: float32 [2048, 256], P('dp', 'kv')
- grad_value_w: float32 [2048, 256], P('dp', 'kv')
- grad_output_w: float32 [4, 512, 2048], P('kv', 'dp')
- grad_mlp_gain: float32 [2048], P('dp')
- grad_gate_w: float32 [2048, 5632], P('dp', 'kv')
- grad_up_w: float32 [2048, 5632], P('dp', 'kv')
- grad_down_w: float32 [4, 1408, 2048], P('kv', 'dp')
The draws below stay inside these ranges and needn't reach their ends.
Inputs may be any that keep to these rules, and one draw needn't show every extreme that they name: `counts`: each pack's real tokens come first and its padding last; at most 256 padded tokens a pack; some packs have none. `segments`: ids never fall; every pack of 1024 rows begins a new segment at its first row, and no segment crosses packs; every padded token is a segment of its own, numbered by its index; a real segment is a chat fragment of at most 256 tokens or a whole pack.
All inputs are finite; a program needn't handle non-finite values.
Results may differ from the reference program's by a relative error of at most 0.024.
Values may be sent and summed in bfloat16 or wider, within the bound.
A program may use at most 256 MiB of HBM per device.

```python
import jax
import jax.numpy as jnp
from jax import lax

D = 2048
HD = 64
QPK = 8
FF = 5632
TOK_DEV = 1024
FRAG_MIN = 32
FRAG_MAX = 256
KV_HEADS = 4
HEADS = 32
PAD_MAX = 256
TOKENS = 8192
N_DP = 8


def pack_layout(key):
    chosen = jax.random.randint(jax.random.fold_in(key, 11), (), 0, 7)
    device_ids = jnp.arange(N_DP, dtype=jnp.int32)
    full_doc = device_ids % 8 == chosen
    padding = jax.random.randint(jax.random.fold_in(key, 12), (N_DP,), 0, PAD_MAX + 1)
    padding = jnp.where(device_ids == (chosen + 1) % N_DP, PAD_MAX, padding)
    padding = jnp.where(device_ids == N_DP - 1, jnp.maximum(padding, 1), padding)
    padding = jnp.where(full_doc, 0, padding)
    counts = (TOK_DEV - padding).astype(jnp.int32)
    frag_slots = TOK_DEV // FRAG_MIN + 1
    lengths = jax.random.randint(jax.random.fold_in(key, 13), (N_DP, frag_slots), FRAG_MIN, FRAG_MAX + 1)
    ends_at = jnp.cumsum(lengths, axis=1)
    places = jnp.arange(TOK_DEV, dtype=jnp.int32)
    local_ids = jnp.sum((ends_at[:, None, :] <= places[None, :, None]).astype(jnp.int32), axis=2)
    local_ids = jnp.where(full_doc[:, None], 0, local_ids)
    local_ids = jnp.where(places[None, :] < counts[:, None], local_ids, places[None, :])
    segment_ids = device_ids[:, None] * TOK_DEV + local_ids
    return (counts, segment_ids.reshape(TOKENS).astype(jnp.int32))


def draw_counts(key, part):
    counts, segment_ids = pack_layout(key)
    return counts


def draw_segments(key, part):
    counts, segment_ids = pack_layout(key)
    return segment_ids


def strengthened(drawn, rng, source, target, parts, factor):
    def block_of(position):
        return (jnp.arange(drawn.shape[position]) // (drawn.shape[position] // parts)).reshape((-1,) + (1,) * (drawn.ndim - 1 - position))

    first = jax.random.permutation(rng, parts)[block_of(target)]
    far = (block_of(target) + parts // 2) % parts
    return jnp.where((block_of(source) == first) | (block_of(source) == far), factor * drawn, drawn)


def steps_of(stream_key, shape, split, low, top_value):
    gain, own = 1.0, jax.random.fold_in(stream_key, 6)
    for dim, shards_of in split:
        draws = jnp.exp(jax.random.uniform(jax.random.fold_in(own, dim), (shards_of,), jnp.float32, low / len(split), top_value / len(split)))
        gain = gain * jnp.repeat(draws, shape[dim] // shards_of).reshape([-1 if axis == dim else 1 for axis in range(len(shape))])
    return gain


def normal_values(rng, extent, deviation, limit, shards=(), held_as=jnp.bfloat16):
    drawn = deviation * jax.random.normal(rng, extent, jnp.float32)
    if shards:
        drawn = drawn * steps_of(rng, extent, shards, -0.22, 0.18)
    return jnp.clip(drawn, -limit, limit).astype(held_as)


def bell_draw_with(rng, dims, deviation, reach, shards, heavy, kind=jnp.bfloat16):
    values = deviation * jax.random.normal(rng, dims, jnp.float32)
    if shards:
        values = values * steps_of(rng, dims, shards, -0.22, 0.18)
    return jnp.clip(strengthened(values, jax.random.fold_in(rng, 3), *heavy), -reach, reach).astype(kind)


def setup_inputs(seed: int = 0) -> dict:
    key_list = jax.random.split(jax.random.key(seed), 14)
    tokens_in = bell_draw_with(key_list[0], (TOKENS, D), 1.0, 6.0, ((0, 8),), (0, 1, 8, 2.0))
    attn_gain = jnp.clip(1.0 + 0.1 * jax.random.normal(key_list[1], (D,), jnp.float32), 0.5, 1.5)
    w_query = normal_values(key_list[2], (D, HEADS * HD), D ** -0.5, 0.125, ((1, 4),))
    w_key = normal_values(key_list[3], (D, KV_HEADS * HD), D ** -0.5, 0.125, ((1, 4),))
    w_value = normal_values(key_list[4], (D, KV_HEADS * HD), D ** -0.5, 0.125, ((1, 4),))
    w_output = normal_values(key_list[5], (KV_HEADS, QPK * HD, D), (HEADS * HD // 16) ** -0.5, 0.5, ((0, 4),))
    mlp_gain = jnp.clip(1.0 + 0.1 * jax.random.normal(key_list[6], (D,), jnp.float32), 0.5, 1.5)
    w_gate = normal_values(key_list[7], (D, FF), D ** -0.5, 0.125, ((1, 4),))
    w_up = normal_values(key_list[8], (D, FF), D ** -0.5, 0.125, ((1, 4),))
    w_down = normal_values(key_list[9], (KV_HEADS, FF // KV_HEADS, D), FF ** -0.5, 0.078125, ((0, 4),))
    counts = draw_counts(jax.random.fold_in(key_list[13], 71), 0)
    segments = draw_segments(jax.random.fold_in(key_list[13], 71), 0)
    cotangent = normal_values(key_list[12], (TOKENS, D), 1.0, 6.0, ((0, 8),))
    return dict(tokens_in=tokens_in, attn_gain=attn_gain, w_query=w_query, w_key=w_key, w_value=w_value, w_output=w_output, mlp_gain=mlp_gain, w_gate=w_gate, w_up=w_up, w_down=w_down, counts=counts, segments=segments, cotangent=cotangent)


EPS = 1e-05
EXACT = lax.Precision.HIGHEST

@jax.custom_vjp
def low(v):
    return lax.optimization_barrier(v.astype(jnp.bfloat16)).astype(jnp.float32)

@jax.custom_vjp
def low_back(v):
    return v

def low_keep(v):
    return (low(v), None)

def low_pass(kept, grad):
    return (grad,)

def back_keep(v):
    return (v, None)

def back_low(kept, grad):
    return (low(grad),)
low.defvjp(low_keep, low_pass)
low_back.defvjp(back_keep, back_low)

def norm_rows(values, norm_gain):
    inverse = lax.rsqrt(lax.optimization_barrier(jnp.mean(values * values, axis=1, keepdims=True)) + EPS)
    return values * inverse * norm_gain

def rope_tables(places, head_width):
    half_width = head_width // 2
    frequency = 10000.0 ** (-(jnp.arange(half_width, dtype=jnp.float32) * 2.0 / head_width))
    angles = places.astype(jnp.float32)[:, None] * frequency[None, :]
    cosine = jnp.concatenate([jnp.cos(angles), jnp.cos(angles)], axis=1)
    sinus = jnp.concatenate([jnp.sin(angles), jnp.sin(angles)], axis=1)
    return (cosine, sinus)

def rotate(vectors, cosine, sinus):
    half_width = vectors.shape[-1] // 2
    turned = jnp.concatenate([-vectors[..., half_width:], vectors[..., :half_width]], axis=-1)
    return vectors * cosine[:, None, :] + turned * sinus[:, None, :]

def seg_positions(segment_ids):
    places = jnp.arange(segment_ids.shape[0], dtype=jnp.int32)
    boundary = jnp.concatenate([jnp.ones((1,), jnp.bool_), segment_ids[1:] != segment_ids[:-1]])
    starts_at = lax.cummax(jnp.where(boundary, places, 0), axis=0)
    return places - starts_at

def attend_pack(operands):
    query_mat, key_mat, value_mat, pack_ids = operands
    key_all = jnp.repeat(key_mat, QPK, axis=1)
    value_all = jnp.repeat(value_mat, QPK, axis=1)
    raw_scores = low_back(jnp.einsum('qhd,khd->hqk', query_mat, key_all, precision=EXACT) * HD ** (-0.5))
    places = jnp.arange(TOK_DEV, dtype=jnp.int32)
    allowed = (places[None, :] <= places[:, None]) & (pack_ids[None, :] == pack_ids[:, None])
    masked = jnp.where(allowed[None], raw_scores, -jnp.inf)
    chance = low(jax.nn.softmax(masked, axis=2))
    return jnp.einsum('hqk,khd->qhd', chance, value_all, precision=EXACT)

def reference(tokens_in, attn_gain, w_query, w_key, w_value, w_output, mlp_gain, w_gate, w_up, w_down, counts, segments, cotangent):
    places_all = jnp.arange(TOKENS, dtype=jnp.int32)
    live_rows = (places_all % TOK_DEV < jnp.repeat(counts, TOK_DEV, total_repeat_length=TOKENS)).astype(jnp.float32)
    cosine, sinus = rope_tables(seg_positions(segments), HD)

    def per_pack(tensor):
        return tensor.reshape((N_DP, TOK_DEV) + tensor.shape[1:])

    def layer_forward(tokens_f, gain_one, query_w, key_w, value_w, output_w, gain_two, gate_w, up_w, down_w):
        act_one = low(norm_rows(tokens_f, gain_one))
        query_raw = low_back(jnp.dot(act_one, query_w, precision=EXACT)).reshape(TOKENS, HEADS, HD)
        key_raw = low_back(jnp.dot(act_one, key_w, precision=EXACT)).reshape(TOKENS, KV_HEADS, HD)
        value_mat = low(low_back(jnp.dot(act_one, value_w, precision=EXACT))).reshape(TOKENS, KV_HEADS, HD)
        query_mat = low(rotate(query_raw, cosine, sinus))
        key_mat = low(rotate(key_raw, cosine, sinus))
        attended = lax.map(jax.checkpoint(attend_pack), (per_pack(query_mat), per_pack(key_mat), per_pack(value_mat), per_pack(segments)))
        attn_out = low(low_back(attended.reshape(TOKENS, HEADS * HD)))
        branch = low_back(jnp.dot(attn_out, output_w.reshape(HEADS * HD, D), precision=EXACT))
        resid = tokens_f + branch
        act_two = low(norm_rows(resid, gain_two))
        gate_act = low_back(jnp.dot(act_two, gate_w, precision=EXACT))
        up_act = low_back(jnp.dot(act_two, up_w, precision=EXACT))
        hidden = low(jax.nn.silu(gate_act) * up_act)
        feed = low_back(jnp.dot(hidden, down_w.reshape(FF, D), precision=EXACT))
        return resid + feed
    primals = (tokens_in.astype(jnp.float32), attn_gain.astype(jnp.float32), w_query.astype(jnp.float32), w_key.astype(jnp.float32), w_value.astype(jnp.float32), w_output.astype(jnp.float32), mlp_gain.astype(jnp.float32), w_gate.astype(jnp.float32), w_up.astype(jnp.float32), w_down.astype(jnp.float32))
    layer_out, pullback = jax.vjp(layer_forward, *primals)
    gradients = pullback(cotangent.astype(jnp.float32) * live_rows[:, None])
    return (layer_out.astype(jnp.bfloat16), gradients[0], gradients[1], gradients[2], gradients[3], gradients[4], gradients[5], gradients[6], gradients[7], gradients[8], gradients[9])
```

```python
import jax
import jax.numpy as jnp
from jax import lax
from jax.sharding import PartitionSpec as P

EPS = 1e-05


def norm_rows(values, norm_gain):
    inverse = lax.rsqrt(jnp.mean(values * values, axis=1, keepdims=True) + EPS)
    return values * inverse * norm_gain


def rope_tables(places, head_width):
    half_width = head_width // 2
    frequency = 10000.0 ** (-(jnp.arange(half_width, dtype=jnp.float32) * 2.0 / head_width))
    angles = places.astype(jnp.float32)[:, None] * frequency[None, :]
    cosine = jnp.concatenate([jnp.cos(angles), jnp.cos(angles)], axis=1)
    sinus = jnp.concatenate([jnp.sin(angles), jnp.sin(angles)], axis=1)
    return (cosine, sinus)


def rotate(vectors, cosine, sinus):
    half_width = vectors.shape[-1] // 2
    turned = jnp.concatenate([-vectors[..., half_width:], vectors[..., :half_width]], axis=-1)
    return vectors * cosine[:, None, :] + turned * sinus[:, None, :]


def seg_positions(segment_ids):
    places = jnp.arange(segment_ids.shape[0], dtype=jnp.int32)
    boundary = jnp.concatenate([jnp.ones((1,), jnp.bool_), segment_ids[1:] != segment_ids[:-1]])
    starts_at = lax.cummax(jnp.where(boundary, places, 0), axis=0)
    return places - starts_at


def product_left(first_mat, second_mat):
    return lax.dot_general(
        first_mat, second_mat, (((0,), (0,)), ((), ())), preferred_element_type=jnp.float32
    )


def product_right(first_mat, second_mat):
    return lax.dot_general(
        first_mat, second_mat, (((1,), (1,)), ((), ())), preferred_element_type=jnp.float32
    )


def block_scores(query_mat, key_mat, query_seg, key_seg, query_place, key_place, score_scale):
    raw_scores = (
        jnp.einsum("qhd,kd->hqk", query_mat, key_mat, preferred_element_type=jnp.float32)
        * score_scale
    )
    allowed = (key_place[None, :] <= query_place[:, None]) & (
        key_seg[None, :] == query_seg[:, None]
    )
    return jnp.where(allowed[None], raw_scores, -jnp.inf)


def swiglu(gate_act, up_act):
    return jax.nn.silu(gate_act) * up_act


def gather_weight(shard):
    share = shard.shape[0] // lax.axis_size("dp")
    mine = lax.dynamic_slice_in_dim(shard, lax.axis_index("dp") * share, share, 0)
    return lax.all_gather(lax.all_gather(mine, "kv"), "dp", axis=1, tiled=True)


def per_device(
    tokens_in,
    attn_gain,
    w_query,
    w_key,
    w_value,
    w_output,
    mlp_gain,
    w_gate,
    w_up,
    w_down,
    counts,
    segments,
    cotangent,
):
    row_count = tokens_in.shape[0]
    head_width = w_key.shape[1]
    head_count = w_query.shape[1] // head_width
    row_share = row_count // lax.axis_size("kv")
    own_start = lax.axis_index("kv") * row_share
    score_scale = head_width ** (-0.5)
    block_rows = min(512, row_count)
    places = jnp.arange(row_count, dtype=jnp.int32)

    def own_rows(array):
        return lax.dynamic_slice_in_dim(array, own_start, row_share, 0)

    w_out_full = gather_weight(w_output[0]).reshape(-1, w_output.shape[2])
    w_qkv_full = gather_weight(jnp.concatenate([w_query, w_key, w_value], axis=1))
    tokens_f = tokens_in.astype(jnp.float32)
    cosine, sinus = rope_tables(seg_positions(segments), head_width)
    act_one = norm_rows(tokens_f, attn_gain).astype(jnp.bfloat16)
    query_raw = jnp.dot(act_one, w_query, preferred_element_type=jnp.float32).reshape(
        row_count, head_count, head_width
    )
    key_raw = jnp.dot(act_one, w_key, preferred_element_type=jnp.float32).reshape(
        row_count, 1, head_width
    )
    value_b = jnp.dot(act_one, w_value, preferred_element_type=jnp.float32).astype(jnp.bfloat16)
    query_b = rotate(query_raw, cosine, sinus).astype(jnp.bfloat16)
    key_b = rotate(key_raw, cosine, sinus)[:, 0, :].astype(jnp.bfloat16)
    outputs = []
    logsums = []
    for begin_row in range(0, row_count, block_rows):
        end_row = begin_row + block_rows
        scores = block_scores(
            query_b[begin_row:end_row],
            key_b[:end_row],
            segments[begin_row:end_row],
            segments[:end_row],
            places[begin_row:end_row],
            places[:end_row],
            score_scale,
        )
        highest = jnp.max(scores, axis=2, keepdims=True)
        logsum = highest + jnp.log(jnp.sum(jnp.exp(scores - highest), axis=2, keepdims=True))
        chance_b = jnp.exp(scores - logsum).astype(jnp.bfloat16)
        outputs.append(
            jnp.einsum(
                "hqk,kd->qhd", chance_b, value_b[:end_row], preferred_element_type=jnp.float32
            )
        )
        logsums.append(logsum)
    attn_out = (
        jnp.concatenate(outputs, axis=0)
        .reshape(row_count, head_count * head_width)
        .astype(jnp.bfloat16)
    )
    attn_full = lax.all_gather(attn_out, "kv", axis=1, tiled=True)
    resid_full = tokens_f + jnp.dot(attn_full, w_out_full, preferred_element_type=jnp.float32)
    resid_mine = own_rows(resid_full)
    act_two = norm_rows(resid_full, mlp_gain).astype(jnp.bfloat16)
    gate_act = jnp.dot(act_two, w_gate, preferred_element_type=jnp.float32)
    up_act = jnp.dot(act_two, w_up, preferred_element_type=jnp.float32)
    hidden = swiglu(gate_act, up_act).astype(jnp.bfloat16)
    feed_part = jnp.dot(hidden, w_down[0], preferred_element_type=jnp.float32)
    live_rows = (places < counts[0]).astype(jnp.float32)
    grad_out = cotangent.astype(jnp.float32) * live_rows[:, None]
    grad_out_b = grad_out.astype(jnp.bfloat16)
    grad_hidden = product_right(grad_out_b, w_down[0])
    grad_down = product_left(hidden, grad_out_b)
    swiglu_out, swiglu_back = jax.vjp(swiglu, gate_act, up_act)
    grad_gate, grad_up = swiglu_back(grad_hidden)
    grad_gate = grad_gate.astype(jnp.bfloat16)
    grad_up = grad_up.astype(jnp.bfloat16)
    grad_wgate = product_left(act_two, grad_gate)
    grad_wup = product_left(act_two, grad_up)
    grad_act_two = product_right(grad_gate, w_gate) + product_right(grad_up, w_up)
    grad_two_mine = lax.psum_scatter(
        grad_act_two.astype(jnp.bfloat16), "kv", scatter_dimension=0, tiled=True
    ).astype(jnp.float32)
    norm_out, second_back = jax.vjp(norm_rows, resid_mine, mlp_gain)
    grad_resid, gain_two = second_back(grad_two_mine)
    grad_resid_mine = own_rows(grad_out) + grad_resid
    grad_branch = grad_resid_mine.astype(jnp.bfloat16)
    grad_attn_rows = product_right(grad_branch, w_out_full).astype(jnp.bfloat16)
    grad_attn = lax.all_to_all(grad_attn_rows, "kv", 1, 0, tiled=True).reshape(
        row_count, head_count, head_width
    )
    grad_woutput = product_left(own_rows(attn_full), grad_branch)
    layer_out = (
        resid_mine
        + lax.psum_scatter(
            feed_part.astype(jnp.bfloat16), "kv", scatter_dimension=0, tiled=True
        ).astype(jnp.float32)
    ).astype(jnp.bfloat16)
    grad_query_parts = []
    grad_key_r = jnp.zeros((row_count, head_width), jnp.float32)
    grad_value_r = jnp.zeros((row_count, head_width), jnp.float32)
    for block_index, begin_row in enumerate(range(0, row_count, block_rows)):
        end_row = begin_row + block_rows
        remain = row_count - end_row
        scores = block_scores(
            query_b[begin_row:end_row],
            key_b[:end_row],
            segments[begin_row:end_row],
            segments[:end_row],
            places[begin_row:end_row],
            places[:end_row],
            score_scale,
        )
        chance = jnp.exp(scores - logsums[block_index])
        grad_probs = jnp.einsum(
            "qhd,kd->hqk",
            grad_attn[begin_row:end_row],
            value_b[:end_row],
            preferred_element_type=jnp.float32,
        )
        centre = jnp.sum(chance * grad_probs, axis=2, keepdims=True)
        grad_scores = (chance * (grad_probs - centre)).astype(jnp.bfloat16)
        grad_query_parts.append(
            jnp.einsum(
                "hqk,kd->qhd", grad_scores, key_b[:end_row], preferred_element_type=jnp.float32
            )
            * score_scale
        )
        key_term = (
            jnp.einsum(
                "hqk,qhd->kd",
                grad_scores,
                query_b[begin_row:end_row],
                preferred_element_type=jnp.float32,
            )
            * score_scale
        )
        grad_key_r = grad_key_r + jnp.pad(key_term, ((0, remain), (0, 0)))
        value_term = jnp.einsum(
            "hqk,qhd->kd",
            chance.astype(jnp.bfloat16),
            grad_attn[begin_row:end_row],
            preferred_element_type=jnp.float32,
        )
        grad_value_r = grad_value_r + jnp.pad(value_term, ((0, remain), (0, 0)))
    query_rot, query_back = jax.vjp(lambda vectors: rotate(vectors, cosine, sinus), query_raw)
    grad_query = (
        query_back(jnp.concatenate(grad_query_parts, axis=0))[0]
        .reshape(row_count, head_count * head_width)
        .astype(jnp.bfloat16)
    )
    key_rot, key_back = jax.vjp(lambda vectors: rotate(vectors, cosine, sinus), key_raw)
    grad_key = (
        key_back(grad_key_r[:, None, :])[0].reshape(row_count, head_width).astype(jnp.bfloat16)
    )
    grad_value = grad_value_r.astype(jnp.bfloat16)
    grad_wquery = product_left(act_one, grad_query)
    grad_wkey = product_left(act_one, grad_key)
    grad_wvalue = product_left(act_one, grad_value)
    grad_qkv = jnp.concatenate([grad_query, grad_key, grad_value], axis=1)
    group_count = lax.axis_size("kv")
    grad_qkv_rows = lax.all_to_all(
        grad_qkv.reshape(group_count, row_share, -1), "kv", 0, 0, tiled=True
    )
    grad_one_mine = jnp.einsum(
        "grc,gdc->rd", grad_qkv_rows, w_qkv_full, preferred_element_type=jnp.float32
    )
    first_out, first_back = jax.vjp(norm_rows, own_rows(tokens_f), attn_gain)
    grad_first, gain_one = first_back(grad_one_mine)
    grad_tokens = grad_resid_mine + grad_first
    (
        sent_query,
        sent_key,
        sent_value,
        sent_output,
        sent_one,
        sent_gate,
        sent_up,
        sent_down,
        sent_two,
    ) = (
        lax.psum_scatter(
            grad_wquery.astype(jnp.bfloat16), "dp", scatter_dimension=0, tiled=True
        ).astype(jnp.float32),
        lax.psum_scatter(
            grad_wkey.astype(jnp.bfloat16), "dp", scatter_dimension=0, tiled=True
        ).astype(jnp.float32),
        lax.psum_scatter(
            grad_wvalue.astype(jnp.bfloat16), "dp", scatter_dimension=0, tiled=True
        ).astype(jnp.float32),
        lax.psum_scatter(
            lax.psum_scatter(
                grad_woutput.reshape(group_count, -1, w_output.shape[2]).astype(jnp.bfloat16),
                "dp",
                scatter_dimension=1,
                tiled=True,
            ),
            "kv",
            scatter_dimension=0,
            tiled=True,
        ).astype(jnp.float32),
        lax.psum_scatter(lax.psum(gain_one, "kv"), "dp", scatter_dimension=0, tiled=True),
        lax.psum_scatter(
            grad_wgate.astype(jnp.bfloat16), "dp", scatter_dimension=0, tiled=True
        ).astype(jnp.float32),
        lax.psum_scatter(
            grad_wup.astype(jnp.bfloat16), "dp", scatter_dimension=0, tiled=True
        ).astype(jnp.float32),
        lax.psum_scatter(
            grad_down[None].astype(jnp.bfloat16), "dp", scatter_dimension=1, tiled=True
        ).astype(jnp.float32),
        lax.psum_scatter(lax.psum(gain_two, "kv"), "dp", scatter_dimension=0, tiled=True),
    )
    return (
        layer_out,
        grad_tokens,
        sent_one,
        sent_query,
        sent_key,
        sent_value,
        sent_output,
        sent_two,
        sent_gate,
        sent_up,
        sent_down,
    )


def solution(mesh):
    return jax.shard_map(
        per_device,
        mesh=mesh,
        in_specs=(
            P("dp", None),
            P(),
            P(None, "kv"),
            P(None, "kv"),
            P(None, "kv"),
            P("kv", None, None),
            P(),
            P(None, "kv"),
            P(None, "kv"),
            P("kv", None, None),
            P("dp"),
            P("dp"),
            P("dp", None),
        ),
        out_specs=(
            P(("dp", "kv"), None),
            P(("dp", "kv"), None),
            P("dp"),
            P("dp", "kv"),
            P("dp", "kv"),
            P("dp", "kv"),
            P("kv", "dp", None),
            P("dp"),
            P("dp", "kv"),
            P("dp", "kv"),
            P("kv", "dp", None),
        ),
        check_vma=False,
    )
```

```python
import functools

import jax
import jax.numpy as jnp
from jax import lax
from jax.experimental import pallas as pl
from jax.experimental.pallas import tpu as pltpu
from jax.sharding import PartitionSpec as P

EPS = 1e-05
MESH = pl.DeviceIdType.MESH
VMEM_LIMIT = 60 * 1024 * 1024


def norm_rows(values, norm_gain):
    inverse = lax.rsqrt(jnp.mean(values * values, axis=1, keepdims=True) + EPS)
    return values * inverse * norm_gain


def rope_tables(places, head_width):
    half_width = head_width // 2
    frequency = 10000.0 ** (-(jnp.arange(half_width, dtype=jnp.float32) * 2.0 / head_width))
    angles = places.astype(jnp.float32)[:, None] * frequency[None, :]
    cosine = jnp.concatenate([jnp.cos(angles), jnp.cos(angles)], axis=1)
    sinus = jnp.concatenate([jnp.sin(angles), jnp.sin(angles)], axis=1)
    return (cosine, sinus)


def rotate(vectors, cosine, sinus):
    half_width = vectors.shape[-1] // 2
    turned = jnp.concatenate([-vectors[..., half_width:], vectors[..., :half_width]], axis=-1)
    return vectors * cosine[:, None, :] + turned * sinus[:, None, :]


def seg_positions(segment_ids):
    places = jnp.arange(segment_ids.shape[0], dtype=jnp.int32)
    boundary = jnp.concatenate([jnp.ones((1,), jnp.bool_), segment_ids[1:] != segment_ids[:-1]])
    starts_at = lax.cummax(jnp.where(boundary, places, 0), axis=0)
    return places - starts_at


def product_left(first_mat, second_mat):
    return lax.dot_general(
        first_mat, second_mat, (((0,), (0,)), ((), ())), preferred_element_type=jnp.float32
    )


def product_right(first_mat, second_mat):
    return lax.dot_general(
        first_mat, second_mat, (((1,), (1,)), ((), ())), preferred_element_type=jnp.float32
    )


def block_scores(query_mat, key_mat, query_seg, key_seg, query_place, key_place, score_scale):
    raw_scores = (
        jnp.einsum("qhd,kd->hqk", query_mat, key_mat, preferred_element_type=jnp.float32)
        * score_scale
    )
    allowed = (key_place[None, :] <= query_place[:, None]) & (
        key_seg[None, :] == query_seg[:, None]
    )
    return jnp.where(allowed[None], raw_scores, -jnp.inf)


def swiglu(gate_act, up_act):
    return jax.nn.silu(gate_act) * up_act


def gather_weight(shard):
    share = shard.shape[0] // lax.axis_size("dp")
    mine = lax.dynamic_slice_in_dim(shard, lax.axis_index("dp") * share, share, 0)
    return lax.all_gather(lax.all_gather(mine, "kv"), "dp", axis=1, tiled=True)


def row_halves(rows):
    upper = -(-rows // 32) * 16
    return ((0, upper), (upper, rows - upper))


def product_scatter_kernel(count, dp, *refs):
    lhs, rhs, outs = refs[:count], refs[count : 2 * count], refs[2 * count : 3 * count]
    sent, held = refs[3 * count : 4 * count], refs[4 * count : 5 * count]
    late = (refs[5 * count : 6 * count], refs[6 * count : 7 * count])
    first_send, first_recv, late_send, late_recv = refs[7 * count :]
    me = lax.axis_index("dp")
    upper = me // 2
    bits = dp.bit_length() - 1
    slots = dp // 2

    def bit(place):
        return (me // 2**place) % 2

    def partner(place):
        return me + 2**place * (1 - 2 * bit(place))

    def first_copy(a, t):
        return pltpu.make_async_remote_copy(
            src_ref=sent[a].at[t],
            dst_ref=held[a].at[t],
            send_sem=first_send.at[a, t],
            recv_sem=first_recv.at[a, t],
            device_id={"dp": partner(0)},
            device_id_type=MESH,
        )

    def stage_bit(half, stage):
        return stage - 1 if half == 0 else bits - 1 - stage

    def slot_of(half, stage, index, value):
        if half == 0:
            return index * 2**stage + value * 2 ** (stage - 1) + upper % 2 ** (stage - 1)
        top = 2 ** (bits - stage)
        return index + value * (top // 2) + (upper // top) * top

    def late_copy(a, half, stage, index, slot):
        start, size = row_halves(lhs[a].shape[1])[half]
        place = stage_bit(half, stage) + 1
        buffer = slots - 2 ** (bits - stage) + index
        return pltpu.make_async_remote_copy(
            src_ref=held[a].at[slot, pl.ds(start, size)],
            dst_ref=late[half][a].at[buffer],
            send_sem=late_send.at[a, half, buffer],
            recv_sem=late_recv.at[a, half, buffer],
            device_id={"dp": partner(place)},
            device_id_type=MESH,
        )

    def product(a, chunk):
        return jnp.dot(lhs[a][chunk], rhs[a][...], preferred_element_type=jnp.float32)

    def other_chunks(a):
        def step(t, carry):
            sent[a][t] = product(a, 2 * t + 1 - bit(0)).astype(jnp.bfloat16)
            first_copy(a, t).start()
            return carry

        lax.fori_loop(0, slots, step, 0)

    def own_chunks(a):
        def step(e, carry):
            t = 0
            for place in range(bits - 1):
                t = t + 2**place * ((e // 2**place + 1 + upper // 2**place) % 2)
            own = product(a, 2 * t + bit(0))
            first_copy(a, t).wait_recv()
            held[a][t] = (held[a][t].astype(jnp.float32) + own).astype(jnp.bfloat16)

            @pl.when(e % 2 == 0)
            def _():
                late_copy(a, 0, 1, t // 2, t).start()

            @pl.when(e < slots // 2)
            def _():
                late_copy(a, 1, 1, t % (slots // 2), t).start()

            return carry

        lax.fori_loop(0, slots, step, 0)

    def later(a, stage):
        for half in range(2):
            start, size = row_halves(lhs[a].shape[1])[half]
            keep_bit = bit(stage_bit(half, stage) + 1)
            if stage < bits - 1:
                follow = stage_bit(half, stage + 1)
            for index in range(2 ** (bits - 1 - stage)):
                slot = slot_of(half, stage, index, keep_bit)
                late_copy(a, half, stage, index, slot).wait_recv()
                total = held[a][slot, pl.ds(start, size)].astype(jnp.float32) + late[half][a][
                    slots - 2 ** (bits - stage) + index
                ].astype(jnp.float32)
                if stage == bits - 1:
                    outs[a][pl.ds(start, size)] = total
                else:
                    held[a][slot, pl.ds(start, size)] = total.astype(jnp.bfloat16)
            if stage < bits - 1:
                for index in range(2 ** (bits - 2 - stage)):
                    slot = slot_of(half, stage + 1, index, 1 - bit(follow + 1))
                    late_copy(a, half, stage + 1, index, slot).start()

    barrier = pltpu.get_barrier_semaphore()
    for place in range(bits):
        pl.semaphore_signal(
            barrier, inc=1, device_id={"dp": partner(place)}, device_id_type=MESH
        )
    pl.semaphore_wait(barrier, bits)
    pending = []
    for a in range(count):
        other_chunks(a)
        own_chunks(a)
        pending.append((a, 1))
        if a > 0:
            done, stage = pending.pop(0)
            later(done, stage)
            if stage < bits - 1:
                pending.append((done, stage + 1))
    while pending:
        done, stage = pending.pop(0)
        later(done, stage)
        if stage < bits - 1:
            pending.append((done, stage + 1))
    for a in range(count):
        for t in range(slots):
            first_copy(a, t).wait_send()
        for half in range(2):
            for stage in range(1, bits):
                for index in range(2 ** (bits - 1 - stage)):
                    late_copy(a, half, stage, index, 0).wait_send()


def product_scatter(pairs, collective_id):
    count = len(pairs)
    dp = pairs[0][0].shape[0]
    slots = dp // 2
    dims = [(lhs.shape[1], rhs.shape[1]) for lhs, rhs in pairs]
    flops = sum(2 * lhs.size * rhs.shape[1] for lhs, rhs in pairs)
    moved = sum(2 * (lhs.size + rhs.size) for lhs, rhs in pairs)
    vmem = pl.BlockSpec(memory_space=pltpu.VMEM)
    return pl.pallas_call(
        functools.partial(product_scatter_kernel, count, dp),
        out_shape=[jax.ShapeDtypeStruct(dim, jnp.float32) for dim in dims],
        in_specs=[vmem] * (2 * count),
        out_specs=[vmem] * count,
        scratch_shapes=[pltpu.VMEM((slots,) + dim, jnp.bfloat16) for dim in dims] * 2
        + [
            pltpu.VMEM((slots - 1, row_halves(rows)[half][1], columns), jnp.bfloat16)
            for half in range(2)
            for rows, columns in dims
        ]
        + [pltpu.SemaphoreType.DMA((count, slots))] * 2
        + [pltpu.SemaphoreType.DMA((count, 2, slots - 1))] * 2,
        compiler_params=pltpu.CompilerParams(
            collective_id=collective_id, has_side_effects=True, vmem_limit_bytes=VMEM_LIMIT
        ),
        cost_estimate=pl.CostEstimate(flops=flops * 3, bytes_accessed=moved, transcendentals=0),
    )(*[lhs for lhs, _ in pairs], *[rhs for _, rhs in pairs])


def row_chunks(matrix, count):
    chunks = matrix.T.reshape(count, matrix.shape[1] // count, matrix.shape[0])
    return jnp.pad(chunks, ((0, 0), (0, -chunks.shape[1] % 16), (0, 0)))


def per_device(
    tokens_in,
    attn_gain,
    w_query,
    w_key,
    w_value,
    w_output,
    mlp_gain,
    w_gate,
    w_up,
    w_down,
    counts,
    segments,
    cotangent,
):
    row_count = tokens_in.shape[0]
    head_width = w_key.shape[1]
    head_count = w_query.shape[1] // head_width
    row_share = row_count // lax.axis_size("kv")
    own_start = lax.axis_index("kv") * row_share
    score_scale = head_width ** (-0.5)
    block_rows = min(512, row_count)
    places = jnp.arange(row_count, dtype=jnp.int32)

    def own_rows(array):
        return lax.dynamic_slice_in_dim(array, own_start, row_share, 0)

    w_out_full = gather_weight(w_output[0]).reshape(-1, w_output.shape[2])
    w_qkv_full = gather_weight(jnp.concatenate([w_query, w_key, w_value], axis=1))
    tokens_f = tokens_in.astype(jnp.float32)
    cosine, sinus = rope_tables(seg_positions(segments), head_width)
    act_one = norm_rows(tokens_f, attn_gain).astype(jnp.bfloat16)
    query_raw = jnp.dot(act_one, w_query, preferred_element_type=jnp.float32).reshape(
        row_count, head_count, head_width
    )
    key_raw = jnp.dot(act_one, w_key, preferred_element_type=jnp.float32).reshape(
        row_count, 1, head_width
    )
    value_b = jnp.dot(act_one, w_value, preferred_element_type=jnp.float32).astype(jnp.bfloat16)
    query_b = rotate(query_raw, cosine, sinus).astype(jnp.bfloat16)
    key_b = rotate(key_raw, cosine, sinus)[:, 0, :].astype(jnp.bfloat16)
    outputs = []
    logsums = []
    for begin_row in range(0, row_count, block_rows):
        end_row = begin_row + block_rows
        scores = block_scores(
            query_b[begin_row:end_row],
            key_b[:end_row],
            segments[begin_row:end_row],
            segments[:end_row],
            places[begin_row:end_row],
            places[:end_row],
            score_scale,
        )
        highest = jnp.max(scores, axis=2, keepdims=True)
        logsum = highest + jnp.log(jnp.sum(jnp.exp(scores - highest), axis=2, keepdims=True))
        chance_b = jnp.exp(scores - logsum).astype(jnp.bfloat16)
        outputs.append(
            jnp.einsum(
                "hqk,kd->qhd", chance_b, value_b[:end_row], preferred_element_type=jnp.float32
            )
        )
        logsums.append(logsum)
    attn_out = (
        jnp.concatenate(outputs, axis=0)
        .reshape(row_count, head_count * head_width)
        .astype(jnp.bfloat16)
    )
    attn_full = lax.all_gather(attn_out, "kv", axis=1, tiled=True)
    resid_full = tokens_f + jnp.dot(attn_full, w_out_full, preferred_element_type=jnp.float32)
    resid_mine = own_rows(resid_full)
    act_two = norm_rows(resid_full, mlp_gain).astype(jnp.bfloat16)
    gate_act = jnp.dot(act_two, w_gate, preferred_element_type=jnp.float32)
    up_act = jnp.dot(act_two, w_up, preferred_element_type=jnp.float32)
    hidden = swiglu(gate_act, up_act).astype(jnp.bfloat16)
    feed_part = jnp.dot(hidden, w_down[0], preferred_element_type=jnp.float32)
    live_rows = (places < counts[0]).astype(jnp.float32)
    grad_out = cotangent.astype(jnp.float32) * live_rows[:, None]
    grad_out_b = grad_out.astype(jnp.bfloat16)
    grad_hidden = product_right(grad_out_b, w_down[0])
    swiglu_out, swiglu_back = jax.vjp(swiglu, gate_act, up_act)
    grad_gate, grad_up = swiglu_back(grad_hidden)
    grad_gate = grad_gate.astype(jnp.bfloat16)
    grad_up = grad_up.astype(jnp.bfloat16)
    pack_count = lax.axis_size("dp")
    act_chunks = row_chunks(act_two, pack_count)
    sent_gate, sent_up, sent_down = product_scatter(
        [
            (act_chunks, grad_gate),
            (act_chunks, grad_up),
            (row_chunks(hidden, pack_count), grad_out_b),
        ],
        1,
    )
    sent_down = sent_down[: hidden.shape[1] // pack_count][None]
    grad_act_two = product_right(grad_gate, w_gate) + product_right(grad_up, w_up)
    grad_two_mine = lax.psum_scatter(
        grad_act_two.astype(jnp.bfloat16), "kv", scatter_dimension=0, tiled=True
    ).astype(jnp.float32)
    norm_out, second_back = jax.vjp(norm_rows, resid_mine, mlp_gain)
    grad_resid, gain_two = second_back(grad_two_mine)
    grad_resid_mine = own_rows(grad_out) + grad_resid
    grad_branch = grad_resid_mine.astype(jnp.bfloat16)
    grad_attn_rows = product_right(grad_branch, w_out_full).astype(jnp.bfloat16)
    grad_attn = lax.all_to_all(grad_attn_rows, "kv", 1, 0, tiled=True).reshape(
        row_count, head_count, head_width
    )
    grad_woutput = product_left(own_rows(attn_full), grad_branch)
    layer_out = (
        resid_mine
        + lax.psum_scatter(
            feed_part.astype(jnp.bfloat16), "kv", scatter_dimension=0, tiled=True
        ).astype(jnp.float32)
    ).astype(jnp.bfloat16)
    grad_query_parts = []
    grad_key_r = jnp.zeros((row_count, head_width), jnp.float32)
    grad_value_r = jnp.zeros((row_count, head_width), jnp.float32)
    for block_index, begin_row in enumerate(range(0, row_count, block_rows)):
        end_row = begin_row + block_rows
        remain = row_count - end_row
        scores = block_scores(
            query_b[begin_row:end_row],
            key_b[:end_row],
            segments[begin_row:end_row],
            segments[:end_row],
            places[begin_row:end_row],
            places[:end_row],
            score_scale,
        )
        chance = jnp.exp(scores - logsums[block_index])
        grad_probs = jnp.einsum(
            "qhd,kd->hqk",
            grad_attn[begin_row:end_row],
            value_b[:end_row],
            preferred_element_type=jnp.float32,
        )
        centre = jnp.sum(chance * grad_probs, axis=2, keepdims=True)
        grad_scores = (chance * (grad_probs - centre)).astype(jnp.bfloat16)
        grad_query_parts.append(
            jnp.einsum(
                "hqk,kd->qhd", grad_scores, key_b[:end_row], preferred_element_type=jnp.float32
            )
            * score_scale
        )
        key_term = (
            jnp.einsum(
                "hqk,qhd->kd",
                grad_scores,
                query_b[begin_row:end_row],
                preferred_element_type=jnp.float32,
            )
            * score_scale
        )
        grad_key_r = grad_key_r + jnp.pad(key_term, ((0, remain), (0, 0)))
        value_term = jnp.einsum(
            "hqk,qhd->kd",
            chance.astype(jnp.bfloat16),
            grad_attn[begin_row:end_row],
            preferred_element_type=jnp.float32,
        )
        grad_value_r = grad_value_r + jnp.pad(value_term, ((0, remain), (0, 0)))
    query_rot, query_back = jax.vjp(lambda vectors: rotate(vectors, cosine, sinus), query_raw)
    grad_query = (
        query_back(jnp.concatenate(grad_query_parts, axis=0))[0]
        .reshape(row_count, head_count * head_width)
        .astype(jnp.bfloat16)
    )
    key_rot, key_back = jax.vjp(lambda vectors: rotate(vectors, cosine, sinus), key_raw)
    grad_key = (
        key_back(grad_key_r[:, None, :])[0].reshape(row_count, head_width).astype(jnp.bfloat16)
    )
    grad_value = grad_value_r.astype(jnp.bfloat16)
    grad_wquery = product_left(act_one, grad_query)
    grad_wkey = product_left(act_one, grad_key)
    grad_wvalue = product_left(act_one, grad_value)
    grad_qkv = jnp.concatenate([grad_query, grad_key, grad_value], axis=1)
    group_count = lax.axis_size("kv")
    grad_qkv_rows = lax.all_to_all(
        grad_qkv.reshape(group_count, row_share, -1), "kv", 0, 0, tiled=True
    )
    grad_one_mine = jnp.einsum(
        "grc,gdc->rd", grad_qkv_rows, w_qkv_full, preferred_element_type=jnp.float32
    )
    first_out, first_back = jax.vjp(norm_rows, own_rows(tokens_f), attn_gain)
    grad_first, gain_one = first_back(grad_one_mine)
    grad_tokens = grad_resid_mine + grad_first
    (
        sent_query,
        sent_key,
        sent_value,
        sent_output,
        sent_one,
        sent_two,
    ) = (
        lax.psum_scatter(
            grad_wquery.astype(jnp.bfloat16), "dp", scatter_dimension=0, tiled=True
        ).astype(jnp.float32),
        lax.psum_scatter(
            grad_wkey.astype(jnp.bfloat16), "dp", scatter_dimension=0, tiled=True
        ).astype(jnp.float32),
        lax.psum_scatter(
            grad_wvalue.astype(jnp.bfloat16), "dp", scatter_dimension=0, tiled=True
        ).astype(jnp.float32),
        lax.psum_scatter(
            lax.psum_scatter(
                grad_woutput.reshape(group_count, -1, w_output.shape[2]).astype(jnp.bfloat16),
                "dp",
                scatter_dimension=1,
                tiled=True,
            ),
            "kv",
            scatter_dimension=0,
            tiled=True,
        ).astype(jnp.float32),
        lax.psum_scatter(lax.psum(gain_one, "kv"), "dp", scatter_dimension=0, tiled=True),
        lax.psum_scatter(lax.psum(gain_two, "kv"), "dp", scatter_dimension=0, tiled=True),
    )
    return (
        layer_out,
        grad_tokens,
        sent_one,
        sent_query,
        sent_key,
        sent_value,
        sent_output,
        sent_two,
        sent_gate,
        sent_up,
        sent_down,
    )


def solution(mesh):
    return jax.shard_map(
        per_device,
        mesh=mesh,
        in_specs=(
            P("dp", None),
            P(),
            P(None, "kv"),
            P(None, "kv"),
            P(None, "kv"),
            P("kv", None, None),
            P(),
            P(None, "kv"),
            P(None, "kv"),
            P("kv", None, None),
            P("dp"),
            P("dp"),
            P("dp", None),
        ),
        out_specs=(
            P(("dp", "kv"), None),
            P(("dp", "kv"), None),
            P("dp"),
            P("dp", "kv"),
            P("dp", "kv"),
            P("dp", "kv"),
            P("kv", "dp", None),
            P("dp"),
            P("dp", "kv"),
            P("dp", "kv"),
            P("kv", "dp", None),
        ),
        check_vma=False,
    )
```

```python
import functools

import jax
import jax.numpy as jnp
from jax import lax
from jax.experimental import pallas as pl
from jax.experimental.pallas import tpu as pltpu
from jax.sharding import PartitionSpec as P

EPS = 1e-05
MESH = pl.DeviceIdType.MESH
VMEM_LIMIT = 60 * 1024 * 1024


def norm_rows(values, norm_gain):
    inverse = lax.rsqrt(jnp.mean(values * values, axis=1, keepdims=True) + EPS)
    return values * inverse * norm_gain


def rope_tables(places, head_width):
    half_width = head_width // 2
    frequency = 10000.0 ** (-(jnp.arange(half_width, dtype=jnp.float32) * 2.0 / head_width))
    angles = places.astype(jnp.float32)[:, None] * frequency[None, :]
    cosine = jnp.concatenate([jnp.cos(angles), jnp.cos(angles)], axis=1)
    sinus = jnp.concatenate([jnp.sin(angles), jnp.sin(angles)], axis=1)
    return (cosine, sinus)


def rotate(vectors, cosine, sinus):
    half_width = vectors.shape[-1] // 2
    turned = jnp.concatenate([-vectors[..., half_width:], vectors[..., :half_width]], axis=-1)
    return vectors * cosine[:, None, :] + turned * sinus[:, None, :]


def seg_positions(segment_ids):
    places = jnp.arange(segment_ids.shape[0], dtype=jnp.int32)
    boundary = jnp.concatenate([jnp.ones((1,), jnp.bool_), segment_ids[1:] != segment_ids[:-1]])
    starts_at = lax.cummax(jnp.where(boundary, places, 0), axis=0)
    return places - starts_at


def product_left(first_mat, second_mat):
    return lax.dot_general(
        first_mat, second_mat, (((0,), (0,)), ((), ())), preferred_element_type=jnp.float32
    )


def product_right(first_mat, second_mat):
    return lax.dot_general(
        first_mat, second_mat, (((1,), (1,)), ((), ())), preferred_element_type=jnp.float32
    )


def block_scores(query_mat, key_mat, query_seg, key_seg, query_place, key_place, score_scale):
    raw_scores = (
        jnp.einsum("qhd,kd->hqk", query_mat, key_mat, preferred_element_type=jnp.float32)
        * score_scale
    )
    allowed = (key_place[None, :] <= query_place[:, None]) & (
        key_seg[None, :] == query_seg[:, None]
    )
    return jnp.where(allowed[None], raw_scores, -jnp.inf)


def swiglu(gate_act, up_act):
    return jax.nn.silu(gate_act) * up_act


def gather_share(shard):
    share = shard.shape[0] // lax.axis_size("dp")
    mine = lax.dynamic_slice_in_dim(shard, lax.axis_index("dp") * share, share, 0)
    return lax.all_gather(mine, "kv")


def other_groups(array):
    count = lax.axis_size("kv")
    doubled = jnp.concatenate([array, array], axis=0)
    return lax.dynamic_slice_in_dim(doubled, lax.axis_index("kv") + 1, count - 1, 0)


def row_halves(rows):
    upper = -(-rows // 32) * 16
    return ((0, upper), (upper, rows - upper))


def product_scatter_kernel(count, dp, *refs):
    lhs, rhs, outs = refs[:count], refs[count : 2 * count], refs[2 * count : 3 * count]
    sent, held = refs[3 * count : 4 * count], refs[4 * count : 5 * count]
    late = (refs[5 * count : 6 * count], refs[6 * count : 7 * count])
    first_send, first_recv, late_send, late_recv = refs[7 * count :]
    me = lax.axis_index("dp")
    upper = me // 2
    bits = dp.bit_length() - 1
    slots = dp // 2

    def bit(place):
        return (me // 2**place) % 2

    def partner(place):
        return me + 2**place * (1 - 2 * bit(place))

    def first_copy(a, t):
        return pltpu.make_async_remote_copy(
            src_ref=sent[a].at[t],
            dst_ref=held[a].at[t],
            send_sem=first_send.at[a, t],
            recv_sem=first_recv.at[a, t],
            device_id={"dp": partner(0)},
            device_id_type=MESH,
        )

    def stage_bit(half, stage):
        return stage - 1 if half == 0 else bits - 1 - stage

    def slot_of(half, stage, index, value):
        if half == 0:
            return index * 2**stage + value * 2 ** (stage - 1) + upper % 2 ** (stage - 1)
        top = 2 ** (bits - stage)
        return index + value * (top // 2) + (upper // top) * top

    def late_copy(a, half, stage, index, slot):
        start, size = row_halves(lhs[a].shape[1])[half]
        place = stage_bit(half, stage) + 1
        buffer = slots - 2 ** (bits - stage) + index
        return pltpu.make_async_remote_copy(
            src_ref=held[a].at[slot, pl.ds(start, size)],
            dst_ref=late[half][a].at[buffer],
            send_sem=late_send.at[a, half, buffer],
            recv_sem=late_recv.at[a, half, buffer],
            device_id={"dp": partner(place)},
            device_id_type=MESH,
        )

    def product(a, chunk):
        return jnp.dot(lhs[a][chunk], rhs[a][...], preferred_element_type=jnp.float32)

    def other_chunks(a):
        def step(t, carry):
            sent[a][t] = product(a, 2 * t + 1 - bit(0)).astype(jnp.bfloat16)
            first_copy(a, t).start()
            return carry

        lax.fori_loop(0, slots, step, 0)

    def own_chunks(a):
        def step(e, carry):
            t = 0
            for place in range(bits - 1):
                t = t + 2**place * ((e // 2**place + 1 + upper // 2**place) % 2)
            own = product(a, 2 * t + bit(0))
            first_copy(a, t).wait_recv()
            held[a][t] = (held[a][t].astype(jnp.float32) + own).astype(jnp.bfloat16)

            @pl.when(e % 2 == 0)
            def _():
                late_copy(a, 0, 1, t // 2, t).start()

            @pl.when(e < slots // 2)
            def _():
                late_copy(a, 1, 1, t % (slots // 2), t).start()

            return carry

        lax.fori_loop(0, slots, step, 0)

    def later(a, stage):
        for half in range(2):
            start, size = row_halves(lhs[a].shape[1])[half]
            keep_bit = bit(stage_bit(half, stage) + 1)
            if stage < bits - 1:
                follow = stage_bit(half, stage + 1)
            for index in range(2 ** (bits - 1 - stage)):
                slot = slot_of(half, stage, index, keep_bit)
                late_copy(a, half, stage, index, slot).wait_recv()
                total = held[a][slot, pl.ds(start, size)].astype(jnp.float32) + late[half][a][
                    slots - 2 ** (bits - stage) + index
                ].astype(jnp.float32)
                if stage == bits - 1:
                    outs[a][pl.ds(start, size)] = total
                else:
                    held[a][slot, pl.ds(start, size)] = total.astype(jnp.bfloat16)
            if stage < bits - 1:
                for index in range(2 ** (bits - 2 - stage)):
                    slot = slot_of(half, stage + 1, index, 1 - bit(follow + 1))
                    late_copy(a, half, stage + 1, index, slot).start()

    barrier = pltpu.get_barrier_semaphore()
    for place in range(bits):
        pl.semaphore_signal(
            barrier, inc=1, device_id={"dp": partner(place)}, device_id_type=MESH
        )
    pl.semaphore_wait(barrier, bits)
    pending = []
    for a in range(count):
        other_chunks(a)
        own_chunks(a)
        pending.append((a, 1))
        if a > 0:
            done, stage = pending.pop(0)
            later(done, stage)
            if stage < bits - 1:
                pending.append((done, stage + 1))
    while pending:
        done, stage = pending.pop(0)
        later(done, stage)
        if stage < bits - 1:
            pending.append((done, stage + 1))
    for a in range(count):
        for t in range(slots):
            first_copy(a, t).wait_send()
        for half in range(2):
            for stage in range(1, bits):
                for index in range(2 ** (bits - 1 - stage)):
                    late_copy(a, half, stage, index, 0).wait_send()


def product_scatter(pairs, collective_id):
    count = len(pairs)
    dp = pairs[0][0].shape[0]
    slots = dp // 2
    dims = [(lhs.shape[1], rhs.shape[1]) for lhs, rhs in pairs]
    flops = sum(2 * lhs.size * rhs.shape[1] for lhs, rhs in pairs)
    moved = sum(2 * (lhs.size + rhs.size) for lhs, rhs in pairs)
    vmem = pl.BlockSpec(memory_space=pltpu.VMEM)
    return pl.pallas_call(
        functools.partial(product_scatter_kernel, count, dp),
        out_shape=[jax.ShapeDtypeStruct(dim, jnp.float32) for dim in dims],
        in_specs=[vmem] * (2 * count),
        out_specs=[vmem] * count,
        scratch_shapes=[pltpu.VMEM((slots,) + dim, jnp.bfloat16) for dim in dims] * 2
        + [
            pltpu.VMEM((slots - 1, row_halves(rows)[half][1], columns), jnp.bfloat16)
            for half in range(2)
            for rows, columns in dims
        ]
        + [pltpu.SemaphoreType.DMA((count, slots))] * 2
        + [pltpu.SemaphoreType.DMA((count, 2, slots - 1))] * 2,
        compiler_params=pltpu.CompilerParams(
            collective_id=collective_id, has_side_effects=True, vmem_limit_bytes=VMEM_LIMIT
        ),
        cost_estimate=pl.CostEstimate(flops=flops * 3, bytes_accessed=moved, transcendentals=0),
    )(*[lhs for lhs, _ in pairs], *[rhs for _, rhs in pairs])


def times(first, second):
    return jnp.dot(first, second, preferred_element_type=jnp.float32)


def times_t(first, second):
    return lax.dot_general(
        first, second, (((1,), (1,)), ((), ())), preferred_element_type=jnp.float32
    )


class Spread:
    def __init__(self, buffer, send_sem, recv_sem, dp, split):
        self.buffer, self.send_sem, self.recv_sem = buffer, send_sem, recv_sem
        self.me = lax.axis_index("dp")
        self.bits = dp.bit_length() - 1
        columns = buffer.shape[3]
        self.columns = ((0, split), (split, columns - split))

    def flipped(self, places):
        device = self.me
        for place in places:
            device = device + 2**place * (1 - 2 * ((self.me // 2**place) % 2))
        return device

    def copies(self, stage, arriving):
        result = []
        for half in range(2):
            order = list(range(1, self.bits))
            order = (order if half == 0 else order[::-1]) + [0]
            for subset in range(2**stage):
                places = [order[b] for b in range(stage) if subset >> b & 1]
                if arriving:
                    places = places + [order[stage]]
                part = self.buffer.at[:, self.flipped(places), :, pl.ds(*self.columns[half])]
                number = 2**stage - 1 + subset
                result.append(
                    pltpu.make_async_remote_copy(
                        src_ref=part,
                        dst_ref=part,
                        send_sem=self.send_sem.at[half, number],
                        recv_sem=self.recv_sem.at[half, number],
                        device_id={"dp": self.flipped([order[stage]])},
                        device_id_type=MESH,
                    )
                )
        return result

    def start(self, stage):
        for copy in self.copies(stage, False):
            copy.start()

    def wait_recv(self, stage):
        for copy in self.copies(stage, True):
            copy.wait_recv()

    def wait_send(self):
        for stage in range(self.bits):
            for copy in self.copies(stage, False):
                copy.wait_send()


def greet(dp, groups):
    pack, group = lax.axis_index("dp"), lax.axis_index("kv")
    bits = dp.bit_length() - 1
    barrier = pltpu.get_barrier_semaphore()
    for place in range(bits):
        other = pack + 2**place * (1 - 2 * ((pack // 2**place) % 2))
        pl.semaphore_signal(barrier, inc=1, device_id={"dp": other}, device_id_type=MESH)
    for step in range(1, groups):
        other = (group + step) % groups
        pl.semaphore_signal(barrier, inc=1, device_id={"kv": other}, device_id_type=MESH)
    pl.semaphore_wait(barrier, bits + groups - 1)


def feed_forward_kernel(dp, groups, *refs):
    (
        attn_hbm, attn_ref, part_ref, own_hbm, gate_hbm, up_hbm, down_hbm, cot_hbm, live_hbm,
        tokens_ref, gain_ref, live_ref,
        act_out, hidden_out, gate_out, up_out, back_out, feed_out, resid_out, rows_out, all_out,
        attn_in, all_ref, own_ref, w_gate, w_up, w_down, cot_ref, live_all, grad_hidden, resid_ref,
        load_sem, send_sem, recv_sem, spread_send, spread_recv, out_sem,
    ) = refs
    block = pl.program_id(0)
    blocks = groups
    group = lax.axis_index("kv")
    pack = lax.axis_index("dp")
    rows = tokens_ref.shape[0]
    others = groups - 1
    spread = Spread(all_ref, spread_send, spread_recv, dp, all_ref.shape[3] // 2)
    loads = [
        pltpu.make_async_copy(source, target, load_sem.at[index])
        for index, (source, target) in enumerate(
            (
                (down_hbm, w_down),
                (cot_hbm, cot_ref),
                (live_hbm, live_all),
                (own_hbm, own_ref),
                (gate_hbm, w_gate),
                (up_hbm, w_up),
            )
        )
    ]

    def attn_copy(part, step, slot):
        span = pl.ds(part * rows, rows)
        return pltpu.make_async_remote_copy(
            src_ref=attn_hbm.at[span],
            dst_ref=attn_in.at[slot, span],
            send_sem=send_sem.at[part, slot],
            recv_sem=recv_sem.at[part, slot],
            device_id={"kv": (group + 1 + step) % groups},
            device_id_type=MESH,
        )

    def hidden_gradient(part):
        span = pl.ds(part * rows, rows)
        masked = (cot_ref[span].astype(jnp.float32) * live_all[span]).astype(jnp.bfloat16)
        grad_hidden[span] = times_t(masked, w_down[...]).astype(jnp.bfloat16)

    @pl.when(block == 0)
    def _():
        for load in loads:
            load.start()
        all_ref[:, pack] = part_ref[...]
        greet(dp, groups)
        for step in range(others):
            attn_copy(0, step, others - 1 - step).start()
        spread.start(0)
        for part in range(1, blocks):
            for step in range(others):
                attn_copy(part, step, others - 1 - step).start()
        for load in loads[:3]:
            load.wait()
        stages = dp.bit_length() - 1
        for stage in range(stages):
            if stage < blocks:
                hidden_gradient(stage)
            spread.wait_recv(stage)
            if stage + 1 < stages:
                spread.start(stage + 1)
        for part in range(stages, blocks):
            hidden_gradient(part)
        for load in loads[3:]:
            load.wait()

    for slot in range(others):
        attn_copy(block, 0, slot).wait_recv()
    span = pl.ds(pl.multiple_of(block * rows, rows), rows)
    width = own_ref.shape[0]
    total = tokens_ref[...].astype(jnp.float32) + times(attn_ref[...], own_ref[...])
    for slot in range(others):
        total = total + times(attn_in[slot, span], all_ref[slot].reshape(width, -1))
    resid_ref[...] = total
    inverse = lax.rsqrt(jnp.mean(total * total, axis=1, keepdims=True) + EPS)
    act = (total * inverse * gain_ref[...]).astype(jnp.bfloat16)
    act_out[...] = act.T
    gate = times(act, w_gate[...])
    up = times(act, w_up[...])
    chance = jax.nn.sigmoid(gate)
    swish = gate * chance
    hidden = swish * up
    feed_out[...] = times(hidden.astype(jnp.bfloat16), w_down[...]).astype(jnp.bfloat16)
    hidden_out[...] = (hidden * live_ref[...]).astype(jnp.bfloat16).T
    grad = grad_hidden[span].astype(jnp.float32)
    gate_b = (grad * up * chance * (1.0 + gate * (1.0 - chance))).astype(jnp.bfloat16)
    up_b = (grad * swish).astype(jnp.bfloat16)
    gate_out[...] = gate_b
    up_out[...] = up_b
    back_out[...] = (times_t(gate_b, w_gate[...]) + times_t(up_b, w_up[...])).astype(jnp.bfloat16)

    @pl.when(block == group)
    def _():
        copy = pltpu.make_async_copy(resid_ref, resid_out, out_sem.at[0])
        copy.start()
        copy.wait()

    @pl.when(block == blocks - 1)
    def _():
        mine = pl.ds(pl.multiple_of(group * rows, rows), rows)
        copies = [
            pltpu.make_async_copy(attn_in.at[:, mine], rows_out, out_sem.at[1]),
            pltpu.make_async_copy(all_ref, all_out, out_sem.at[2]),
        ]
        for copy in copies:
            copy.start()
        for part in range(blocks):
            for slot in range(others):
                attn_copy(part, others - 1 - slot, slot).wait_send()
        spread.wait_send()
        for copy in copies:
            copy.wait()


def feed_forward(attn, part, w_own, w_gate, w_up, w_down, cotangent, live, tokens, gain, sizes, collective_id):
    dp, groups = sizes
    count, features = tokens.shape
    rows = count // groups
    width, hidden = w_own.shape[0], w_gate.shape[1]
    share = part.shape[1]
    others = groups - 1
    any_spec = pl.BlockSpec(memory_space=pl.ANY)
    by_row = lambda columns: pl.BlockSpec((rows, columns), lambda i: (i, 0))
    by_column = lambda height: pl.BlockSpec((height, rows), lambda i: (0, i))
    flops = 2 * count * features * (groups * width + 6 * hidden)
    return pl.pallas_call(
        functools.partial(feed_forward_kernel, dp, groups),
        grid=(groups,),
        out_shape=[
            jax.ShapeDtypeStruct((features, count), jnp.bfloat16),
            jax.ShapeDtypeStruct((hidden, count), jnp.bfloat16),
            jax.ShapeDtypeStruct((count, hidden), jnp.bfloat16),
            jax.ShapeDtypeStruct((count, hidden), jnp.bfloat16),
            jax.ShapeDtypeStruct((count, features), jnp.bfloat16),
            jax.ShapeDtypeStruct((count, features), jnp.bfloat16),
            jax.ShapeDtypeStruct((rows, features), jnp.float32),
            jax.ShapeDtypeStruct((others, rows, width), jnp.bfloat16),
            jax.ShapeDtypeStruct((others, dp, share, features), jnp.bfloat16),
        ],
        in_specs=[
            any_spec,
            by_row(width),
            pl.BlockSpec(memory_space=pltpu.VMEM),
            any_spec, any_spec, any_spec, any_spec, any_spec, any_spec,
            by_row(features),
            pl.BlockSpec(memory_space=pltpu.VMEM),
            by_row(1),
        ],
        out_specs=[
            by_column(features), by_column(hidden), by_row(hidden), by_row(hidden),
            by_row(features), by_row(features), any_spec, any_spec, any_spec,
        ],
        scratch_shapes=[
            pltpu.VMEM((others, count, width), jnp.bfloat16),
            pltpu.VMEM((others, dp, share, features), jnp.bfloat16),
            pltpu.VMEM((width, features), jnp.bfloat16),
            pltpu.VMEM((features, hidden), jnp.bfloat16),
            pltpu.VMEM((features, hidden), jnp.bfloat16),
            pltpu.VMEM((hidden, features), jnp.bfloat16),
            pltpu.VMEM((count, features), jnp.bfloat16),
            pltpu.VMEM((count, 1), jnp.float32),
            pltpu.VMEM((count, hidden), jnp.bfloat16),
            pltpu.VMEM((rows, features), jnp.float32),
            pltpu.SemaphoreType.DMA((6,)),
            pltpu.SemaphoreType.DMA((groups, others)),
            pltpu.SemaphoreType.DMA((groups, others)),
            pltpu.SemaphoreType.DMA((2, dp - 1)),
            pltpu.SemaphoreType.DMA((2, dp - 1)),
            pltpu.SemaphoreType.DMA((3,)),
        ],
        compiler_params=pltpu.CompilerParams(
            collective_id=collective_id, has_side_effects=True, vmem_limit_bytes=VMEM_LIMIT
        ),
        cost_estimate=pl.CostEstimate(flops=flops, bytes_accessed=40 * count * features, transcendentals=0),
    )(attn, attn, part, w_own, w_gate, w_up, w_down, cotangent, live, tokens, gain, live)


def by_group(ring):
    count = lax.axis_size("kv")
    doubled = jnp.concatenate([ring, ring], axis=0)
    return lax.dynamic_slice_in_dim(doubled, count - lax.axis_index("kv"), count, 0)


def row_chunks(matrix, count):
    chunks = matrix.reshape(count, matrix.shape[0] // count, matrix.shape[1])
    return jnp.pad(chunks, ((0, 0), (0, -chunks.shape[1] % 16), (0, 0)))


def per_device(
    tokens_in,
    attn_gain,
    w_query,
    w_key,
    w_value,
    w_output,
    mlp_gain,
    w_gate,
    w_up,
    w_down,
    counts,
    segments,
    cotangent,
):
    row_count = tokens_in.shape[0]
    head_width = w_key.shape[1]
    head_count = w_query.shape[1] // head_width
    row_share = row_count // lax.axis_size("kv")
    own_start = lax.axis_index("kv") * row_share
    score_scale = head_width ** (-0.5)
    block_rows = min(512, row_count)
    places = jnp.arange(row_count, dtype=jnp.int32)

    def own_rows(array):
        return lax.dynamic_slice_in_dim(array, own_start, row_share, 0)

    pack_count, group_count = lax.axis_size("dp"), lax.axis_size("kv")
    w_out_part = other_groups(gather_share(w_output[0]))
    w_qkv_part, w_out_part = lax.optimization_barrier(
        (jnp.concatenate([w_query, w_key, w_value], axis=1), w_out_part)
    )
    w_qkv_full = lax.all_gather(gather_share(w_qkv_part), "dp", axis=1, tiled=True)
    tokens_f = tokens_in.astype(jnp.float32)
    cosine, sinus = rope_tables(seg_positions(segments), head_width)
    act_one = norm_rows(tokens_f, attn_gain).astype(jnp.bfloat16)
    query_raw = jnp.dot(act_one, w_query, preferred_element_type=jnp.float32).reshape(
        row_count, head_count, head_width
    )
    key_raw = jnp.dot(act_one, w_key, preferred_element_type=jnp.float32).reshape(
        row_count, 1, head_width
    )
    value_b = jnp.dot(act_one, w_value, preferred_element_type=jnp.float32).astype(jnp.bfloat16)
    query_b = rotate(query_raw, cosine, sinus).astype(jnp.bfloat16)
    key_b = rotate(key_raw, cosine, sinus)[:, 0, :].astype(jnp.bfloat16)
    outputs = []
    logsums = []
    for begin_row in range(0, row_count, block_rows):
        end_row = begin_row + block_rows
        scores = block_scores(
            query_b[begin_row:end_row],
            key_b[:end_row],
            segments[begin_row:end_row],
            segments[:end_row],
            places[begin_row:end_row],
            places[:end_row],
            score_scale,
        )
        highest = jnp.max(scores, axis=2, keepdims=True)
        logsum = highest + jnp.log(jnp.sum(jnp.exp(scores - highest), axis=2, keepdims=True))
        chance_b = jnp.exp(scores - logsum).astype(jnp.bfloat16)
        outputs.append(
            jnp.einsum(
                "hqk,kd->qhd", chance_b, value_b[:end_row], preferred_element_type=jnp.float32
            )
        )
        logsums.append(logsum)
    attn_out = (
        jnp.concatenate(outputs, axis=0)
        .reshape(row_count, head_count * head_width)
        .astype(jnp.bfloat16)
    )
    live_rows = (places < counts[0]).astype(jnp.float32)[:, None]
    (
        act_flipped,
        hidden_flipped,
        grad_gate,
        grad_up,
        grad_act_two,
        feed_part,
        resid_mine,
        attn_others,
        w_out_others,
    ) = feed_forward(
        attn_out,
        w_out_part,
        w_output[0],
        w_gate,
        w_up,
        w_down[0],
        cotangent,
        live_rows,
        tokens_in,
        mlp_gain[None],
        (pack_count, group_count),
        1,
    )
    act_chunks = row_chunks(act_flipped, pack_count)
    sent_gate, sent_up, sent_down = product_scatter(
        [
            (act_chunks, grad_gate),
            (act_chunks, grad_up),
            (row_chunks(hidden_flipped, pack_count), cotangent),
        ],
        2,
    )
    sent_down = sent_down[: w_down.shape[1] // pack_count][None]
    grad_two_mine = lax.psum_scatter(grad_act_two, "kv", scatter_dimension=0, tiled=True)
    grad_two_mine, feed_part, sent_down = lax.optimization_barrier(
        (grad_two_mine, feed_part, sent_down)
    )
    grad_out_mine = own_rows(cotangent).astype(jnp.float32) * own_rows(live_rows)
    norm_out, second_back = jax.vjp(norm_rows, resid_mine, mlp_gain)
    grad_resid, gain_two = second_back(grad_two_mine.astype(jnp.float32))
    grad_resid_mine = grad_out_mine + grad_resid
    grad_branch = grad_resid_mine.astype(jnp.bfloat16)
    attn_ring = jnp.concatenate([own_rows(attn_out)[None], attn_others], axis=0)
    w_out_ring = jnp.concatenate(
        [w_output, w_out_others.reshape(group_count - 1, w_output.shape[1], -1)], axis=0
    )
    grad_attn_ring = jnp.einsum(
        "rd,gcd->grc", grad_branch, w_out_ring, preferred_element_type=jnp.float32
    ).astype(jnp.bfloat16)
    grad_attn = lax.all_to_all(by_group(grad_attn_ring), "kv", 0, 0, tiled=True).reshape(
        row_count, head_count, head_width
    )
    grad_woutput = by_group(
        jnp.einsum("grc,rd->gcd", attn_ring, grad_branch, preferred_element_type=jnp.float32).astype(
            jnp.bfloat16
        )
    )
    layer_out = (
        resid_mine
        + lax.psum_scatter(feed_part, "kv", scatter_dimension=0, tiled=True).astype(jnp.float32)
    ).astype(jnp.bfloat16)
    grad_query_parts = []
    grad_key_r = jnp.zeros((row_count, head_width), jnp.float32)
    grad_value_r = jnp.zeros((row_count, head_width), jnp.float32)
    for block_index, begin_row in enumerate(range(0, row_count, block_rows)):
        end_row = begin_row + block_rows
        remain = row_count - end_row
        scores = block_scores(
            query_b[begin_row:end_row],
            key_b[:end_row],
            segments[begin_row:end_row],
            segments[:end_row],
            places[begin_row:end_row],
            places[:end_row],
            score_scale,
        )
        chance = jnp.exp(scores - logsums[block_index])
        grad_probs = jnp.einsum(
            "qhd,kd->hqk",
            grad_attn[begin_row:end_row],
            value_b[:end_row],
            preferred_element_type=jnp.float32,
        )
        centre = jnp.sum(chance * grad_probs, axis=2, keepdims=True)
        grad_scores = (chance * (grad_probs - centre)).astype(jnp.bfloat16)
        grad_query_parts.append(
            jnp.einsum(
                "hqk,kd->qhd", grad_scores, key_b[:end_row], preferred_element_type=jnp.float32
            )
            * score_scale
        )
        key_term = (
            jnp.einsum(
                "hqk,qhd->kd",
                grad_scores,
                query_b[begin_row:end_row],
                preferred_element_type=jnp.float32,
            )
            * score_scale
        )
        grad_key_r = grad_key_r + jnp.pad(key_term, ((0, remain), (0, 0)))
        value_term = jnp.einsum(
            "hqk,qhd->kd",
            chance.astype(jnp.bfloat16),
            grad_attn[begin_row:end_row],
            preferred_element_type=jnp.float32,
        )
        grad_value_r = grad_value_r + jnp.pad(value_term, ((0, remain), (0, 0)))
    query_rot, query_back = jax.vjp(lambda vectors: rotate(vectors, cosine, sinus), query_raw)
    grad_query = (
        query_back(jnp.concatenate(grad_query_parts, axis=0))[0]
        .reshape(row_count, head_count * head_width)
        .astype(jnp.bfloat16)
    )
    key_rot, key_back = jax.vjp(lambda vectors: rotate(vectors, cosine, sinus), key_raw)
    grad_key = (
        key_back(grad_key_r[:, None, :])[0].reshape(row_count, head_width).astype(jnp.bfloat16)
    )
    grad_value = grad_value_r.astype(jnp.bfloat16)
    grad_wquery = product_left(act_one, grad_query)
    grad_wkey = product_left(act_one, grad_key)
    grad_wvalue = product_left(act_one, grad_value)
    grad_qkv = jnp.concatenate([grad_query, grad_key, grad_value], axis=1)
    grad_qkv_rows = lax.all_to_all(
        grad_qkv.reshape(group_count, row_share, -1), "kv", 0, 0, tiled=True
    )
    grad_one_mine = jnp.einsum(
        "grc,gdc->rd", grad_qkv_rows, w_qkv_full, preferred_element_type=jnp.float32
    )
    first_out, first_back = jax.vjp(norm_rows, own_rows(tokens_f), attn_gain)
    grad_first, gain_one = first_back(grad_one_mine)
    grad_tokens = grad_resid_mine + grad_first
    (
        sent_query,
        sent_key,
        sent_value,
        sent_output,
        sent_one,
        sent_two,
    ) = (
        lax.psum_scatter(
            grad_wquery.astype(jnp.bfloat16), "dp", scatter_dimension=0, tiled=True
        ).astype(jnp.float32),
        lax.psum_scatter(
            grad_wkey.astype(jnp.bfloat16), "dp", scatter_dimension=0, tiled=True
        ).astype(jnp.float32),
        lax.psum_scatter(
            grad_wvalue.astype(jnp.bfloat16), "dp", scatter_dimension=0, tiled=True
        ).astype(jnp.float32),
        lax.psum_scatter(
            lax.psum_scatter(
                grad_woutput,
                "dp",
                scatter_dimension=1,
                tiled=True,
            ),
            "kv",
            scatter_dimension=0,
            tiled=True,
        ).astype(jnp.float32),
        lax.psum_scatter(lax.psum(gain_one, "kv"), "dp", scatter_dimension=0, tiled=True),
        lax.psum_scatter(lax.psum(gain_two, "kv"), "dp", scatter_dimension=0, tiled=True),
    )
    return (
        layer_out,
        grad_tokens,
        sent_one,
        sent_query,
        sent_key,
        sent_value,
        sent_output,
        sent_two,
        sent_gate,
        sent_up,
        sent_down,
    )


def solution(mesh):
    return jax.shard_map(
        per_device,
        mesh=mesh,
        in_specs=(
            P("dp", None),
            P(),
            P(None, "kv"),
            P(None, "kv"),
            P(None, "kv"),
            P("kv", None, None),
            P(),
            P(None, "kv"),
            P(None, "kv"),
            P("kv", None, None),
            P("dp"),
            P("dp"),
            P("dp", None),
        ),
        out_specs=(
            P(("dp", "kv"), None),
            P(("dp", "kv"), None),
            P("dp"),
            P("dp", "kv"),
            P("dp", "kv"),
            P("dp", "kv"),
            P("kv", "dp", None),
            P("dp"),
            P("dp", "kv"),
            P("dp", "kv"),
            P("kv", "dp", None),
        ),
        check_vma=False,
    )
```

```python
import functools

import jax
import jax.numpy as jnp
from jax import lax
from jax.experimental import pallas as pl
from jax.experimental.pallas import tpu as pltpu
from jax.sharding import PartitionSpec as P

EPS = 1e-05
LOG2E = 1.4426950408889634
MESH = pl.DeviceIdType.MESH
VMEM_LIMIT = 60 * 1024 * 1024


def row_halves(rows):
    upper = -(-rows // 32) * 16
    return ((0, upper), (upper, rows - upper))


def times(first, second):
    return jnp.dot(first, second, preferred_element_type=jnp.float32)


def times_t(first, second):
    return lax.dot_general(
        first, second, (((1,), (1,)), ((), ())), preferred_element_type=jnp.float32
    )


def to_group(step, groups, source, target, sems):
    return pltpu.make_async_remote_copy(
        src_ref=source,
        dst_ref=target,
        send_sem=sems.at[0, step - 1],
        recv_sem=sems.at[1, step - 1],
        device_id={"kv": (lax.axis_index("kv") + step) % groups},
        device_id_type=MESH,
    )


class Spread:
    def __init__(self, buffer, send_sem, recv_sem, dp):
        self.buffer, self.send_sem, self.recv_sem = buffer, send_sem, recv_sem
        self.me = lax.axis_index("dp")
        self.bits = dp.bit_length() - 1
        columns = buffer.shape[3]
        split = -(-columns // 256) * 128
        self.columns = ((0, split), (split, columns - split))

    def flipped(self, places):
        device = self.me
        for place in places:
            device = device + 2**place * (1 - 2 * ((self.me // 2**place) % 2))
        return device

    def copies(self, stage, arriving):
        result = []
        for half in range(2):
            order = list(range(1, self.bits))
            order = (order if half == 0 else order[::-1]) + [0]
            for subset in range(2**stage):
                places = [order[b] for b in range(stage) if subset >> b & 1]
                if arriving:
                    places = places + [order[stage]]
                part = self.buffer.at[:, self.flipped(places), :, pl.ds(*self.columns[half])]
                number = 2**stage - 1 + subset
                result.append(
                    pltpu.make_async_remote_copy(
                        src_ref=part,
                        dst_ref=part,
                        send_sem=self.send_sem.at[half, number],
                        recv_sem=self.recv_sem.at[half, number],
                        device_id={"dp": self.flipped([order[stage]])},
                        device_id_type=MESH,
                    )
                )
        return result

    def start(self, stage):
        for copy in self.copies(stage, False):
            copy.start()

    def wait_recv(self, stage):
        for copy in self.copies(stage, True):
            copy.wait_recv()

    def wait_send(self):
        for stage in range(self.bits):
            for copy in self.copies(stage, False):
                copy.wait_send()


def greet(dp, groups):
    pack, group = lax.axis_index("dp"), lax.axis_index("kv")
    bits = dp.bit_length() - 1
    barrier = pltpu.get_barrier_semaphore()
    for place in range(bits):
        other = pack + 2**place * (1 - 2 * ((pack // 2**place) % 2))
        pl.semaphore_signal(barrier, inc=1, device_id={"dp": other}, device_id_type=MESH)
    for step in range(1, groups):
        other = (group + step) % groups
        pl.semaphore_signal(barrier, inc=1, device_id={"kv": other}, device_id_type=MESH)
    pl.semaphore_wait(barrier, bits + groups - 1)


def attention_kernel(groups, head_width, *refs):
    (
        tokens_ref, gain_ref, query_w, pair_w, seg_column, seg_row, frequency, part_hbm,
        attn_out, act_out, query_out, key_out, value_out, logsum_out,
        cosine_out, sine_a_out, sine_b_out, cosine_t_out, sine_t_out, parts_out,
        query_m, value_t, part_sems,
    ) = refs
    rows = tokens_ref.shape[0] // groups
    width, span_w = query_w.shape[1], key_out.shape[1]
    heads, pair, half = span_w // head_width, 2 * head_width, head_width // 2
    scale = head_width**-0.5 * LOG2E

    def part_copy(step):
        return to_group(step, groups, part_hbm, parts_out.at[groups - 1 - step], part_sems)

    greet(1, groups)
    for step in range(1, groups):
        part_copy(step).start()
    lanes = lax.broadcasted_iota(jnp.int32, (rows, pair), 1)
    low_half = lanes % head_width < half
    head_lanes = lax.broadcasted_iota(jnp.int32, (rows, span_w), 1) // head_width

    for block in range(groups):
        part = pl.ds(block * rows, rows)
        values = tokens_ref[part].astype(jnp.float32)
        inverse = lax.rsqrt(jnp.mean(values * values, axis=1, keepdims=True) + EPS)
        act = (values * inverse * gain_ref[...]).astype(jnp.bfloat16)
        act_out[:, part] = act.T
        query_raw = times(act, query_w[...])
        pair_raw = times(act, pair_w[...])
        before = (seg_row[...] < seg_column[part]).astype(jnp.float32)
        places = (
            lax.broadcasted_iota(jnp.int32, (rows, 1), 0) + block * rows
        ).astype(jnp.float32) - jnp.sum(before, axis=1, keepdims=True)
        angles = places * frequency[...]
        cosine, sine = jnp.cos(angles), jnp.sin(angles)
        sine_a, sine_b = jnp.where(low_half, -sine, 0.0), jnp.where(low_half, 0.0, sine)
        cosine_out[part], sine_a_out[part], sine_b_out[part] = cosine, sine_a, sine_b
        cosine_t_out[:, part] = cosine.T[:half]
        sine_t_out[:, part] = sine.T[:half]

        def rotated(vectors):
            return (
                vectors * cosine
                + pltpu.roll(vectors, pair - half, 1) * sine_a
                + pltpu.roll(vectors, half, 1) * sine_b
            ).astype(jnp.bfloat16)

        for start in range(0, width, pair):
            query_out[part, pl.ds(start, pair)] = rotated(query_raw[:, start : start + pair])
        other = pltpu.roll(pair_raw, head_width, 1)
        keys_two = rotated(jnp.where(lanes < head_width, pair_raw, other))
        values_two = jnp.where(lanes < head_width, other, pair_raw)
        key_out[part] = jnp.concatenate([keys_two] * (span_w // pair), axis=1)
        value_out[part] = jnp.concatenate(
            [values_two.astype(jnp.bfloat16)] * (span_w // pair), axis=1
        )
        value_t[:, part] = values_two.T[:head_width].astype(jnp.bfloat16)
        query_seg = seg_row[:, part]
        query_place = lax.broadcasted_iota(jnp.int32, (rows, rows), 1) + block * rows

        def span(number, carry):
            columns = pl.ds(pl.multiple_of(number * span_w, span_w), span_w)
            query = query_out[part, columns]
            for head in range(heads):
                query_m[pl.ds(head * rows, rows)] = jnp.where(head_lanes == head, query, 0)

            def keys(step, carry):
                highest, total, output = carry
                piece = block - step
                key_part = pl.ds(pl.multiple_of(piece * rows, rows), rows)
                key_place = lax.broadcasted_iota(jnp.int32, (rows, rows), 0) + piece * rows
                allowed = (seg_column[key_part] == query_seg) & (key_place <= query_place)
                bias = jnp.where(allowed, 0.0, -jnp.inf)
                scores = times_t(key_out[key_part], query_m[...]) * scale
                scores = scores + jnp.concatenate([bias] * heads, axis=1)
                top = jnp.maximum(highest, jnp.max(scores, axis=0, keepdims=True))
                shrink = jnp.exp2(highest - top)
                chance = jnp.exp2(scores - top)
                total = total * shrink + jnp.sum(chance, axis=0, keepdims=True)
                output = output * shrink + times(value_t[:, key_part], chance.astype(jnp.bfloat16))
                return top, total, output

            first = (
                jnp.full((1, heads * rows), -jnp.inf, jnp.float32),
                jnp.zeros((1, heads * rows), jnp.float32),
                jnp.zeros((head_width, heads * rows), jnp.float32),
            )
            highest, total, output = lax.fori_loop(0, block + 1, keys, first)
            output = output / total
            stacked = jnp.concatenate(
                [output[:, head * rows : (head + 1) * rows] for head in range(heads)], axis=0
            )
            attn_out[part, columns] = stacked.T.astype(jnp.bfloat16)
            logsum_out[number * groups + block] = highest + jnp.log(total) * LOG2E
            return carry

        lax.fori_loop(0, width // span_w, span, 0)
    for step in range(1, groups):
        part_copy(step).wait()


def attention(tokens, gain, query_w, pair_w, segments, part, groups, collective_id):
    count, features = tokens.shape
    width, head_width = query_w.shape[1], pair_w.shape[1] // 2
    span_w = 256
    rows, heads, half = count // groups, span_w // head_width, head_width // 2
    frequency = 10000.0 ** (-(jnp.arange(half, dtype=jnp.float32) * 2.0 / head_width))
    vmem = pl.BlockSpec(memory_space=pltpu.VMEM)
    any_spec = pl.BlockSpec(memory_space=pl.ANY)
    bf16, f32 = jnp.bfloat16, jnp.float32
    return pl.pallas_call(
        functools.partial(attention_kernel, groups, head_width),
        out_shape=[
            jax.ShapeDtypeStruct((count, width), bf16),
            jax.ShapeDtypeStruct((features, count), bf16),
            jax.ShapeDtypeStruct((count, width), bf16),
            jax.ShapeDtypeStruct((count, span_w), bf16),
            jax.ShapeDtypeStruct((count, span_w), bf16),
            jax.ShapeDtypeStruct((width // span_w * groups, 1, heads * rows), f32),
            jax.ShapeDtypeStruct((count, 2 * head_width), f32),
            jax.ShapeDtypeStruct((count, 2 * head_width), f32),
            jax.ShapeDtypeStruct((count, 2 * head_width), f32),
            jax.ShapeDtypeStruct((half, count), f32),
            jax.ShapeDtypeStruct((half, count), f32),
            jax.ShapeDtypeStruct((groups - 1,) + part.shape, bf16),
        ],
        in_specs=[vmem] * 7 + [any_spec],
        out_specs=[vmem] * 11 + [any_spec],
        scratch_shapes=[
            pltpu.VMEM((heads * rows, span_w), bf16),
            pltpu.VMEM((head_width, count), bf16),
            pltpu.SemaphoreType.DMA((2, groups - 1)),
        ],
        compiler_params=pltpu.CompilerParams(
            collective_id=collective_id, has_side_effects=True, vmem_limit_bytes=VMEM_LIMIT
        ),
        cost_estimate=pl.CostEstimate(
            flops=4 * count * features * width, bytes_accessed=8 * tokens.size, transcendentals=0
        ),
    )(
        tokens,
        gain,
        query_w,
        pair_w,
        segments[:, None],
        segments[None],
        jnp.tile(frequency, 4)[None],
        part,
    )


def feed_forward_kernel(dp, groups, *refs):
    (
        attn_hbm, attn_ref, part_ref, own_hbm, gate_hbm, up_hbm, down_hbm, cot_hbm, live_hbm,
        tokens_ref, gain_ref, live_ref,
        act_out, hidden_out, gate_out, up_out, back_out, feed_out, resid_out, rows_out, all_out,
        attn_in, all_ref, own_ref, w_gate, w_up, w_down, cot_ref, live_all, grad_hidden, resid_ref,
        load_sem, send_sem, recv_sem, spread_send, spread_recv, out_sem,
    ) = refs
    block = pl.program_id(0)
    blocks = groups
    group = lax.axis_index("kv")
    pack = lax.axis_index("dp")
    rows = tokens_ref.shape[0]
    others = groups - 1
    spread = Spread(all_ref, spread_send, spread_recv, dp)
    loads = [
        pltpu.make_async_copy(source, target, load_sem.at[index])
        for index, (source, target) in enumerate(
            (
                (down_hbm, w_down),
                (cot_hbm, cot_ref),
                (live_hbm, live_all),
                (own_hbm, own_ref),
                (gate_hbm, w_gate),
                (up_hbm, w_up),
            )
        )
    ]

    def attn_copy(part, step, slot, source, place):
        span = pl.ds(part * rows, rows)
        return pltpu.make_async_remote_copy(
            src_ref=source.at[span],
            dst_ref=attn_in.at[slot, span],
            send_sem=send_sem.at[part, place],
            recv_sem=recv_sem.at[part, slot],
            device_id={"kv": (group + step) % groups},
            device_id_type=MESH,
        )

    def send_rows(part):
        for step in range(1, groups):
            copy = attn_copy(part, step, others - step, attn_hbm, step - 1)
            if step in relayed:
                pl.when((group == 0) | (group == 3))(copy.start)
            else:
                copy.start()

    relayed = (2,) if groups == 4 else ()
    relays = ((1, 0, 3), (2, 2, 1)) if groups == 4 else ()

    def wait_rows(part, slot):
        attn_copy(part, 1, slot, attn_hbm, 0).wait_recv()

    def pass_on(part):
        for holder, slot, step in relays:

            @pl.when(group == holder)
            def _():
                wait_rows(part, slot)
                attn_copy(part, step, 1, attn_in.at[slot], 1).start()

    def wait_block(part):
        for slot in range(others):
            holders = [holder for holder, place, _ in relays if place == slot]
            if holders:

                @pl.when(group != holders[0])
                def _():
                    wait_rows(part, slot)
            else:
                wait_rows(part, slot)

    def hidden_gradient(part):
        span = pl.ds(part * rows, rows)
        masked = (cot_ref[span].astype(jnp.float32) * live_all[span]).astype(jnp.bfloat16)
        grad_hidden[span] = times_t(masked, w_down[...]).astype(jnp.bfloat16)

    @pl.when(block == 0)
    def _():
        for load in loads:
            load.start()
        all_ref[:, pack] = part_ref[...]
        greet(dp, groups)
        send_rows(0)
        spread.start(0)
        for part in range(1, blocks):
            send_rows(part)
        for load in loads[:3]:
            load.wait()
        stages = dp.bit_length() - 1
        for stage in range(stages):
            if stage < blocks:
                hidden_gradient(stage)
            spread.wait_recv(stage)
            if stage + 1 < stages:
                spread.start(stage + 1)
            if stage < 2:
                pass_on(stage)
        for part in range(stages, blocks):
            hidden_gradient(part)
        for load in loads[3:]:
            load.wait()

    wait_block(block)
    span = pl.ds(pl.multiple_of(block * rows, rows), rows)
    width = own_ref.shape[0]
    total = tokens_ref[...].astype(jnp.float32) + times(attn_ref[...], own_ref[...])
    for slot in range(others):
        total = total + times_t(attn_in[slot, span], all_ref[slot].reshape(-1, width))
    resid_ref[...] = total
    inverse = lax.rsqrt(jnp.mean(total * total, axis=1, keepdims=True) + EPS)
    act = (total * inverse * gain_ref[...]).astype(jnp.bfloat16)
    act_out[...] = act.T
    gate = times(act, w_gate[...])
    up = times(act, w_up[...])
    chance = jax.nn.sigmoid(gate)
    swish = gate * chance
    hidden = swish * up
    feed_out[...] = times(hidden.astype(jnp.bfloat16), w_down[...]).astype(jnp.bfloat16)
    hidden_out[...] = (hidden * live_ref[...]).astype(jnp.bfloat16).T
    grad = grad_hidden[span].astype(jnp.float32)
    gate_b = (grad * up * chance * (1.0 + gate * (1.0 - chance))).astype(jnp.bfloat16)
    up_b = (grad * swish).astype(jnp.bfloat16)
    gate_out[...] = gate_b
    up_out[...] = up_b
    back_out[...] = (times_t(gate_b, w_gate[...]) + times_t(up_b, w_up[...])).astype(jnp.bfloat16)

    @pl.when(block == group)
    def _():
        copy = pltpu.make_async_copy(resid_ref, resid_out, out_sem.at[0])
        copy.start()
        copy.wait()

    @pl.when(block < blocks - 2)
    def _():
        pass_on(block + 2)

    @pl.when(block == blocks - 1)
    def _():
        mine = pl.ds(pl.multiple_of(group * rows, rows), rows)
        copies = [
            pltpu.make_async_copy(attn_in.at[:, mine], rows_out, out_sem.at[1]),
            pltpu.make_async_copy(all_ref, all_out, out_sem.at[2]),
        ]
        for copy in copies:
            copy.start()
        for part in range(blocks):
            for place in range(others):
                attn_copy(part, 1, 0, attn_hbm, place).wait_send()
        spread.wait_send()
        for copy in copies:
            copy.wait()


def feed_forward(attn, part, w_own, w_gate, w_up, w_down, cotangent, live, tokens, gain, sizes, collective_id):
    dp, groups = sizes
    count, features = tokens.shape
    rows = count // groups
    width, hidden = w_own.shape[0], w_gate.shape[1]
    share = part.shape[1]
    others = groups - 1
    any_spec = pl.BlockSpec(memory_space=pl.ANY)
    by_row = lambda columns: pl.BlockSpec((rows, columns), lambda i: (i, 0))
    by_column = lambda height: pl.BlockSpec((height, rows), lambda i: (0, i))
    flops = 2 * count * features * (groups * width + 6 * hidden)
    return pl.pallas_call(
        functools.partial(feed_forward_kernel, dp, groups),
        grid=(groups,),
        out_shape=[
            jax.ShapeDtypeStruct((features, count), jnp.bfloat16),
            jax.ShapeDtypeStruct((hidden, count), jnp.bfloat16),
            jax.ShapeDtypeStruct((count, hidden), jnp.bfloat16),
            jax.ShapeDtypeStruct((count, hidden), jnp.bfloat16),
            jax.ShapeDtypeStruct((count, features), jnp.bfloat16),
            jax.ShapeDtypeStruct((count, features), jnp.bfloat16),
            jax.ShapeDtypeStruct((rows, features), jnp.float32),
            jax.ShapeDtypeStruct((others, rows, width), jnp.bfloat16),
            jax.ShapeDtypeStruct((others, dp, share, width), jnp.bfloat16),
        ],
        in_specs=[
            any_spec,
            by_row(width),
            pl.BlockSpec(memory_space=pltpu.VMEM),
            any_spec, any_spec, any_spec, any_spec, any_spec, any_spec,
            by_row(features),
            pl.BlockSpec(memory_space=pltpu.VMEM),
            by_row(1),
        ],
        out_specs=[
            by_column(features), by_column(hidden), by_row(hidden), by_row(hidden),
            by_row(features), by_row(features), any_spec, any_spec, any_spec,
        ],
        scratch_shapes=[
            pltpu.VMEM((others, count, width), jnp.bfloat16),
            pltpu.VMEM((others, dp, share, width), jnp.bfloat16),
            pltpu.VMEM((width, features), jnp.bfloat16),
            pltpu.VMEM((features, hidden), jnp.bfloat16),
            pltpu.VMEM((features, hidden), jnp.bfloat16),
            pltpu.VMEM((hidden, features), jnp.bfloat16),
            pltpu.VMEM((count, features), jnp.bfloat16),
            pltpu.VMEM((count, 1), jnp.float32),
            pltpu.VMEM((count, hidden), jnp.bfloat16),
            pltpu.VMEM((rows, features), jnp.float32),
            pltpu.SemaphoreType.DMA((6,)),
            pltpu.SemaphoreType.DMA((groups, others)),
            pltpu.SemaphoreType.DMA((groups, others)),
            pltpu.SemaphoreType.DMA((2, dp - 1)),
            pltpu.SemaphoreType.DMA((2, dp - 1)),
            pltpu.SemaphoreType.DMA((3,)),
        ],
        compiler_params=pltpu.CompilerParams(
            collective_id=collective_id, has_side_effects=True, vmem_limit_bytes=VMEM_LIMIT
        ),
        cost_estimate=pl.CostEstimate(flops=flops, bytes_accessed=40 * count * features, transcendentals=0),
    )(attn, attn, part, w_own, w_gate, w_up, w_down, cotangent, live, tokens, gain, live)


class Scatter:
    def __init__(self, dp, product, store, sent, held, late, sems):
        self.product, self.store, self.sent, self.held, self.late = product, store, sent, held, late
        self.first_send, self.first_recv, self.late_send, self.late_recv = sems
        self.me = lax.axis_index("dp")
        self.upper = self.me // 2
        self.bits = dp.bit_length() - 1
        self.slots = dp // 2
        self.halves = row_halves(held.shape[1])

    def bit(self, place):
        return (self.me // 2**place) % 2

    def partner(self, place):
        return self.me + 2**place * (1 - 2 * self.bit(place))

    def first_copy(self, t):
        return pltpu.make_async_remote_copy(
            src_ref=self.sent.at[t],
            dst_ref=self.held.at[t],
            send_sem=self.first_send.at[t],
            recv_sem=self.first_recv.at[t],
            device_id={"dp": self.partner(0)},
            device_id_type=MESH,
        )

    def stage_bit(self, half, stage):
        return stage - 1 if half == 0 else self.bits - 1 - stage

    def slot_of(self, half, stage, index, value):
        if half == 0:
            low = 2 ** (stage - 1)
            return index * 2**stage + value * low + self.upper % low
        top = 2 ** (self.bits - stage)
        return index + value * (top // 2) + (self.upper // top) * top

    def late_copy(self, half, stage, index, slot):
        start, size = self.halves[half]
        buffer = self.slots - 2 ** (self.bits - stage) + index
        return pltpu.make_async_remote_copy(
            src_ref=self.held.at[slot, pl.ds(start, size)],
            dst_ref=self.late[half].at[buffer],
            send_sem=self.late_send.at[half, buffer],
            recv_sem=self.late_recv.at[half, buffer],
            device_id={"dp": self.partner(self.stage_bit(half, stage) + 1)},
            device_id_type=MESH,
        )

    def other_chunks(self):
        def step(t, carry):
            self.sent[t] = self.product(2 * t + 1 - self.bit(0)).astype(jnp.bfloat16)
            self.first_copy(t).start()
            return carry

        lax.fori_loop(0, self.slots, step, 0)

    def own_chunks(self):
        def step(e, carry):
            t = 0
            for place in range(self.bits - 1):
                t = t + 2**place * ((e // 2**place + 1 + self.upper // 2**place) % 2)
            own = self.product(2 * t + self.bit(0))
            self.first_copy(t).wait_recv()
            self.held[t] = (self.held[t].astype(jnp.float32) + own).astype(jnp.bfloat16)

            @pl.when(e % 2 == 0)
            def _():
                self.late_copy(0, 1, t // 2, t).start()

            @pl.when(e < self.slots // 2)
            def _():
                self.late_copy(1, 1, t % (self.slots // 2), t).start()

            return carry

        lax.fori_loop(0, self.slots, step, 0)

    def later(self, stage):
        for half in range(2):
            start, size = self.halves[half]
            keep_bit = self.bit(self.stage_bit(half, stage) + 1)
            for index in range(2 ** (self.bits - 1 - stage)):
                slot = self.slot_of(half, stage, index, keep_bit)
                self.late_copy(half, stage, index, slot).wait_recv()
                buffer = self.slots - 2 ** (self.bits - stage) + index
                total = self.held[slot, pl.ds(start, size)].astype(jnp.float32) + self.late[half][
                    buffer
                ].astype(jnp.float32)
                if stage == self.bits - 1:
                    self.store(start, size, total)
                else:
                    self.held[slot, pl.ds(start, size)] = total.astype(jnp.bfloat16)
            if stage < self.bits - 1:
                follow = self.stage_bit(half, stage + 1) + 1
                for index in range(2 ** (self.bits - 2 - stage)):
                    slot = self.slot_of(half, stage + 1, index, 1 - self.bit(follow))
                    self.late_copy(half, stage + 1, index, slot).start()

    def finish(self):
        for t in range(self.slots):
            self.first_copy(t).wait_send()
        for half in range(2):
            for stage in range(1, self.bits):
                for index in range(2 ** (self.bits - 1 - stage)):
                    self.late_copy(half, stage, index, 0).wait_send()


def scatter_scratch(dp, rows, columns):
    slots = dp // 2
    return (
        [pltpu.VMEM((slots, rows, columns), jnp.bfloat16)] * 2
        + [pltpu.VMEM((slots - 1, size, columns), jnp.bfloat16) for _, size in row_halves(rows)]
        + [pltpu.SemaphoreType.DMA((slots,))] * 2
        + [pltpu.SemaphoreType.DMA((2, slots - 1))] * 2
    )


def scatter_from(dp, product, store, refs):
    return Scatter(dp, product, store, refs[0], refs[1], refs[2:4], refs[4:8])


def product_scatter_kernel(count, dp, groups, *refs):
    lhs, rhs, pass_ref = refs[:count], refs[count : 2 * count], refs[2 * count]
    outs, pass_out = refs[2 * count + 1 : 3 * count + 1], refs[3 * count + 1]
    pass_sems, scratch = refs[3 * count + 2], refs[3 * count + 3 :]

    def pass_copy(step):
        return to_group(step, groups, pass_ref, pass_out.at[groups - 1 - step], pass_sems)

    def member(a):
        def product(chunk):
            return times(lhs[a][chunk], rhs[a][...])

        def store(start, size, total):
            outs[a][pl.ds(start, size)] = total

        return scatter_from(dp, product, store, scratch[8 * a : 8 * a + 8])

    members = [member(a) for a in range(count)]
    stages = dp.bit_length() - 1
    greet(dp, groups)
    for step in range(1, groups):
        pass_copy(step).start()
    pending = []
    for a in range(count):
        members[a].other_chunks()
        members[a].own_chunks()
        pending.append((a, 1))
        if a > 0:
            done, stage = pending.pop(0)
            members[done].later(stage)
            if stage < stages - 1:
                pending.append((done, stage + 1))
    while pending:
        done, stage = pending.pop(0)
        members[done].later(stage)
        if stage < stages - 1:
            pending.append((done, stage + 1))
    for one in members:
        one.finish()
    for step in range(1, groups):
        pass_copy(step).wait()


def product_scatter(pairs, passed, groups, collective_id):
    count = len(pairs)
    dp = pairs[0][0].shape[0]
    dims = [(lhs.shape[1], rhs.shape[1]) for lhs, rhs in pairs]
    flops = sum(2 * lhs.size * rhs.shape[1] for lhs, rhs in pairs)
    moved = sum(2 * (lhs.size + rhs.size) for lhs, rhs in pairs)
    vmem = pl.BlockSpec(memory_space=pltpu.VMEM)
    any_spec = pl.BlockSpec(memory_space=pl.ANY)
    return pl.pallas_call(
        functools.partial(product_scatter_kernel, count, dp, groups),
        out_shape=[jax.ShapeDtypeStruct(dim, jnp.float32) for dim in dims]
        + [jax.ShapeDtypeStruct((groups - 1,) + passed.shape, passed.dtype)],
        in_specs=[vmem] * (2 * count) + [any_spec],
        out_specs=[vmem] * count + [any_spec],
        scratch_shapes=[pltpu.SemaphoreType.DMA((2, groups - 1))]
        + sum([scatter_scratch(dp, *dim) for dim in dims], []),
        compiler_params=pltpu.CompilerParams(
            collective_id=collective_id, has_side_effects=True, vmem_limit_bytes=VMEM_LIMIT
        ),
        cost_estimate=pl.CostEstimate(flops=flops * 3, bytes_accessed=moved, transcendentals=0),
    )(*[lhs for lhs, _ in pairs], *[rhs for _, rhs in pairs], passed)


def norm_back(values, gain, grads):
    inverse = lax.rsqrt(jnp.mean(values * values, axis=1, keepdims=True) + EPS)
    scaled = gain * grads
    mean = jnp.mean(scaled * values, axis=1, keepdims=True)
    by_values = inverse * scaled - values * (inverse * inverse * inverse * mean)
    return by_values, jnp.sum(grads * values * inverse, axis=0, keepdims=True)


def attention_back_kernel(dp, groups, head_width, *refs):
    (
        back_ref, resid_hbm, cot_hbm, live_ref, tokens_hbm, attn_gain, mlp_gain,
        out_own, out_others, rows_ref, query_ref, key_ref, value_ref, logsum_ref, attn_ref,
        seg_column, seg_row, cosine_t, sine_t, cosine, sine_a, sine_b, qkv_own, pair_own, qkv_parts,
        tokens_out, gains_out, output_out, grad_out, qkv_all,
        cot_ref, tokens_ref, chunk_ref, weights, query_m, attn_m, key_t, query_t, key_sum, value_sum,
        attn_send, attn_grad, arrived, out_total, out_send, out_recv, branch_ref,
        load_sem, last_sem, attn_sems, grad_sems, out_sems, spread_send, spread_recv, *scatter_refs,
    ) = refs
    group, pack, others = lax.axis_index("kv"), lax.axis_index("dp"), groups - 1
    rows = branch_ref.shape[0]
    width = query_ref.shape[1]
    span_w = key_ref.shape[1]
    pair, half, heads = 2 * head_width, head_width // 2, span_w // head_width
    scale = head_width**-0.5
    mine = pl.ds(pl.multiple_of(group * rows, rows), rows)
    out_part = pl.ds(0, width)

    def load(index, source, target):
        return pltpu.make_async_copy(source, target, load_sem.at[index])

    first_loads = [
        load(0, resid_hbm, tokens_out),
        load(1, cot_hbm.at[mine], cot_ref),
        load(2, out_others, weights.at[:, :, out_part]),
        load(3, qkv_parts, qkv_all.at[:, pack]),
        load(4, tokens_hbm.at[mine], tokens_ref),
    ]
    for one in first_loads:
        one.start()

    def attn_copy(step):
        return to_group(step, groups, attn_send.at[step - 1], attn_grad.at[group], attn_sems)

    def grad_copy(step, block):
        return to_group(
            step, groups, grad_out.at[pl.ds(block * rows, rows)], arrived.at[step - 1], grad_sems
        )

    share = output_out.shape[0]

    def out_copy(step):
        return to_group(
            step, groups, out_send.at[pl.ds(step * share, share)], out_recv.at[step - 1], out_sems
        )

    greet(dp, groups)
    spread = Spread(qkv_all, spread_send, spread_recv, dp)
    lanes = lax.broadcasted_iota(jnp.int32, (rows, span_w), 1) // head_width
    first_loads[3].wait()
    spread.start(0)
    first_loads[0].wait()
    first_loads[1].wait()
    values = tokens_out[...]
    grad_resid, mlp_rows = norm_back(values, mlp_gain[...], back_ref[...].astype(jnp.float32))
    grad_resid = grad_resid + cot_ref[...].astype(jnp.float32) * live_ref[mine]
    tokens_out[...] = grad_resid
    branch_ref[...] = grad_resid.astype(jnp.bfloat16)
    first_loads[2].wait()
    for step in range(1, groups):
        attn_send[step - 1] = times(branch_ref[...], weights[step - 1, :, out_part]).astype(
            jnp.bfloat16
        )
        attn_copy(step).start()
    attn_grad[group] = times_t(branch_ref[...], out_own[...]).astype(jnp.bfloat16)

    def store(start, size, total):
        if start == 0:
            out_total[...] = total[:share]
        out_send[pl.ds(start, size)] = total.astype(jnp.bfloat16)

    scatter = scatter_from(dp, lambda chunk: times(chunk_ref[chunk], branch_ref[...]), store, scatter_refs)
    for place in range(groups):
        turned = (attn_ref[mine] if place == 0 else rows_ref[place - 1]).T
        chunk_ref[:, pl.ds(place * share, share)] = turned.reshape(dp, share, rows)
    scatter.other_chunks()
    scatter.own_chunks()
    for block in range(groups):
        part = pl.ds(block * rows, rows)
        key_t[:, part] = key_ref[part, pl.ds(0, pair)].T[:head_width]
    key_sum[...] = jnp.zeros_like(key_sum)
    value_sum[...] = jnp.zeros_like(value_sum)

    def attend(block):
        part = pl.ds(block * rows, rows)

        @pl.when(block != group)
        def _():
            step = (group - block + groups) % groups
            to_group(step, groups, attn_grad.at[block], attn_grad.at[block], attn_sems).wait_recv()

        query_seg = seg_row[:, part]
        query_place = lax.broadcasted_iota(jnp.int32, (rows, rows), 1) + block * rows

        def wide(entries):
            return jnp.concatenate([entries] * heads, axis=1)

        def span(number, carry):
            columns = pl.ds(pl.multiple_of(number * span_w, span_w), span_w)
            query = query_ref[part, columns]
            grad = attn_grad[block, :, columns]
            weighed = (grad.astype(jnp.float32) * attn_ref[part, columns].astype(jnp.float32)).T
            centres = jnp.sum(weighed.reshape(heads, head_width, rows), axis=1)
            centre = jnp.concatenate([centres[head : head + 1] for head in range(heads)], axis=1)
            logsum = logsum_ref[number * groups + block]
            for head in range(heads):
                place = pl.ds(head * rows, rows)
                query_m[place] = jnp.where(lanes == head, query, 0)
                attn_m[place] = jnp.where(lanes == head, grad, 0)
            query_t[...] = jnp.zeros_like(query_t)

            def keys(piece, carry):
                key_part = pl.ds(pl.multiple_of(piece * rows, rows), rows)
                key_place = lax.broadcasted_iota(jnp.int32, (rows, rows), 0) + piece * rows
                allowed = (seg_column[key_part] == query_seg) & (key_place <= query_place)
                bias = jnp.where(allowed, 0.0, -jnp.inf)
                scores = times_t(key_ref[key_part], query_m[...]) * (scale * LOG2E)
                chance = jnp.exp2(scores - logsum + wide(bias))
                probs = times_t(value_ref[key_part], attn_m[...])
                slope = (chance * (probs - centre)).astype(jnp.bfloat16)
                value_sum[key_part] += times(chance.astype(jnp.bfloat16), attn_m[...])
                key_sum[key_part] += times(slope, query_m[...])
                query_t[...] += times(key_t[:, key_part], slope)
                return carry

            lax.fori_loop(0, block + 1, keys, 0)
            cos, sin = wide(cosine_t[:, part]), wide(sine_t[:, part])
            low, high = query_t[:half] * scale, query_t[half:] * scale
            turned = jnp.concatenate([low * cos + high * sin, high * cos - low * sin], axis=0)
            stacked = jnp.concatenate(
                [turned[:, head * rows : (head + 1) * rows] for head in range(heads)], axis=0
            )
            grad_out[part, columns] = stacked.T.astype(jnp.bfloat16)
            return carry

        lax.fori_loop(0, width // span_w, span, 0)

        def folded(total):
            sums = total[part, pl.ds(0, pair)]
            for step in range(1, span_w // pair):
                sums = sums + total[part, pl.ds(step * pair, pair)]
            return sums + pltpu.roll(sums, head_width, 1)

        grad_k = folded(key_sum) * scale
        grad_k = (
            grad_k * cosine[part]
            - pltpu.roll(grad_k, pair - half, 1) * sine_a[part]
            - pltpu.roll(grad_k, half, 1) * sine_b[part]
        )
        first = lax.broadcasted_iota(jnp.int32, (rows, pair), 1) < head_width
        grad_out[part, pl.ds(width, pair)] = jnp.where(first, grad_k, folded(value_sum)).astype(
            jnp.bfloat16
        )

        @pl.when(block != group)
        def _():
            grad_copy((block - group + groups) % groups, block).start()

    stages = dp.bit_length() - 1
    for block in reversed(range(groups)):
        attend(block)
        if block == groups - 1:
            for stage in range(1, stages - 1):
                scatter.later(stage)
            for stage in range(stages - 1):
                spread.wait_recv(stage)
                if stage < stages - 2:
                    spread.start(stage + 1)
        if block == groups - 2:
            scatter.later(stages - 1)
            spread.start(stages - 1)
            for step in range(1, groups):
                out_copy(step).start()

    spread.wait_recv(stages - 1)
    part_rows = qkv_all.shape[2]
    last_loads = [
        pltpu.make_async_copy(
            qkv_all.at[:, place], weights.at[:, pl.ds(place * part_rows, part_rows)], last_sem.at[place]
        )
        for place in range(dp)
    ]
    for one in last_loads:
        one.start()
    total = out_total[...]
    for step in range(1, groups):
        out_copy(step).wait_recv()
        total = total + out_recv[step - 1].astype(jnp.float32)
    output_out[...] = total
    grad_act = times_t(grad_out[mine, out_part], qkv_own[...])
    grad_act = grad_act + times_t(grad_out[mine, pl.ds(width, pair)], pair_own[...])
    for one in last_loads:
        one.wait()
    for step in range(1, groups):
        to_group(step, groups, arrived.at[step - 1], arrived.at[step - 1], grad_sems).wait_recv()
        grad_act = grad_act + times_t(arrived[step - 1], weights[others - step])
    first_loads[4].wait()
    by_tokens, attn_rows = norm_back(tokens_ref[...].astype(jnp.float32), attn_gain[...], grad_act)
    tokens_out[...] += by_tokens
    columns = gains_out.shape[2]
    for place in range(dp):
        span = slice(place * columns, (place + 1) * columns)
        gains_out[place, 0:1] = mlp_rows[:, span]
        gains_out[place, 1:2] = attn_rows[:, span]
    for step in range(1, groups):
        attn_copy(step).wait_send()
        grad_copy(step, 0).wait_send()
        out_copy(step).wait_send()
    spread.wait_send()
    scatter.finish()


def attention_back(operands, sizes, head_width, collective_id):
    dp, groups = sizes
    others_w, rows_others, query, key, parts = (operands[index] for index in (8, 9, 10, 11, 24))
    rows, width = rows_others.shape[1:]
    features = others_w.shape[1]
    count, span_w = key.shape
    share = width // dp
    stacked = (span_w // head_width) * rows
    columns = width + 2 * head_width
    vmem = pl.BlockSpec(memory_space=pltpu.VMEM)
    any_spec = pl.BlockSpec(memory_space=pl.ANY)
    bf16, f32 = jnp.bfloat16, jnp.float32
    flops = 2 * count * count * width * 10
    return pl.pallas_call(
        functools.partial(attention_back_kernel, dp, groups, head_width),
        out_shape=[
            jax.ShapeDtypeStruct((rows, features), f32),
            jax.ShapeDtypeStruct((dp, 2, features // dp), f32),
            jax.ShapeDtypeStruct((share, features), f32),
            jax.ShapeDtypeStruct((count, columns), bf16),
            jax.ShapeDtypeStruct((groups - 1, dp) + parts.shape[1:], bf16),
        ],
        in_specs=[any_spec if index in (1, 2, 4, 8, 24) else vmem for index in range(25)],
        out_specs=[vmem] * 4 + [any_spec],
        scratch_shapes=[
            pltpu.VMEM((rows, features), bf16),
            pltpu.VMEM((rows, features), bf16),
            pltpu.VMEM((dp, groups * share, rows), bf16),
            pltpu.VMEM((groups - 1, features, columns), bf16),
            pltpu.VMEM((stacked, span_w), bf16),
            pltpu.VMEM((stacked, span_w), bf16),
            pltpu.VMEM((head_width, count), bf16),
            pltpu.VMEM((head_width, stacked), f32),
            pltpu.VMEM((count, span_w), f32),
            pltpu.VMEM((count, span_w), f32),
            pltpu.VMEM((groups - 1, rows, width), bf16),
            pltpu.VMEM((groups, rows, width), bf16),
            pltpu.VMEM((groups - 1, rows, columns), bf16),
            pltpu.VMEM((share, features), f32),
            pltpu.VMEM((groups * share, features), bf16),
            pltpu.VMEM((groups - 1, share, features), bf16),
            pltpu.VMEM((rows, features), bf16),
            pltpu.SemaphoreType.DMA((5,)),
            pltpu.SemaphoreType.DMA((dp,)),
            pltpu.SemaphoreType.DMA((2, groups - 1)),
            pltpu.SemaphoreType.DMA((2, groups - 1)),
            pltpu.SemaphoreType.DMA((2, groups - 1)),
            pltpu.SemaphoreType.DMA((2, dp - 1)),
            pltpu.SemaphoreType.DMA((2, dp - 1)),
        ]
        + scatter_scratch(dp, groups * share, features),
        compiler_params=pltpu.CompilerParams(
            collective_id=collective_id, has_side_effects=True, vmem_limit_bytes=VMEM_LIMIT
        ),
        cost_estimate=pl.CostEstimate(flops=flops, bytes_accessed=40 * 2**20, transcendentals=0),
    )(*operands)


def last_sums_kernel(dp, groups, lhs_ref, rhs_ref, gains_ref, query_out, key_out, value_out, gains_out, near, far, total, near_sems, far_sems, *scatter_refs):
    pack, group = lax.axis_index("dp"), lax.axis_index("kv")

    def store(start, size, value):
        span, width, head_width = pl.ds(start, size), query_out.shape[1], key_out.shape[1]
        query_out[span] = value[:, :width]
        key_out[span] = value[:, width : width + head_width]
        value_out[span] = value[:, width + head_width :]

    scatter = scatter_from(dp, lambda chunk: times(lhs_ref[chunk], rhs_ref[...]), store, scatter_refs)

    def near_copy(step):
        return pltpu.make_async_remote_copy(
            src_ref=gains_ref,
            dst_ref=near.at[step - 1],
            send_sem=near_sems.at[0, step - 1],
            recv_sem=near_sems.at[1, step - 1],
            device_id={"kv": (group + step) % groups},
            device_id_type=MESH,
        )

    def far_copy(step):
        other = (pack + step) % dp
        return pltpu.make_async_remote_copy(
            src_ref=total.at[other],
            dst_ref=far.at[step - 1],
            send_sem=far_sems.at[0, step - 1],
            recv_sem=far_sems.at[1, step - 1],
            device_id={"dp": other},
            device_id_type=MESH,
        )

    barrier = pltpu.get_barrier_semaphore()
    for step in range(1, dp):
        pl.semaphore_signal(
            barrier, inc=1, device_id={"dp": (pack + step) % dp}, device_id_type=MESH
        )
    for step in range(1, groups):
        pl.semaphore_signal(
            barrier, inc=1, device_id={"kv": (group + step) % groups}, device_id_type=MESH
        )
    pl.semaphore_wait(barrier, dp + groups - 2)
    for step in range(1, groups):
        near_copy(step).start()
    scatter.other_chunks()
    value = gains_ref[...]
    for step in range(1, groups):
        near_copy(step).wait_recv()
        value = value + near[step - 1]
    total[...] = value
    for step in range(1, dp):
        far_copy(step).start()
    scatter.own_chunks()
    for stage in range(1, dp.bit_length() - 1):
        scatter.later(stage)
    value = total[pack]
    for step in range(1, dp):
        far_copy(step).wait_recv()
        value = value + far[step - 1]
    gains_out[...] = value
    for step in range(1, groups):
        near_copy(step).wait_send()
    for step in range(1, dp):
        far_copy(step).wait_send()
    scatter.finish()


def last_sums(lhs, rhs, gains, head_width, groups, collective_id):
    dp, rows = lhs.shape[0], lhs.shape[1]
    columns = rhs.shape[1]
    vmem = pl.BlockSpec(memory_space=pltpu.VMEM)
    return pl.pallas_call(
        functools.partial(last_sums_kernel, dp, groups),
        out_shape=[
            jax.ShapeDtypeStruct((rows, columns - 2 * head_width), jnp.float32),
            jax.ShapeDtypeStruct((rows, head_width), jnp.float32),
            jax.ShapeDtypeStruct((rows, head_width), jnp.float32),
            jax.ShapeDtypeStruct(gains.shape[1:], jnp.float32),
        ],
        in_specs=[vmem] * 3,
        out_specs=[vmem] * 4,
        scratch_shapes=[
            pltpu.VMEM((groups - 1,) + gains.shape, jnp.float32),
            pltpu.VMEM((dp - 1,) + gains.shape[1:], jnp.float32),
            pltpu.VMEM(gains.shape, jnp.float32),
            pltpu.SemaphoreType.DMA((2, groups - 1)),
            pltpu.SemaphoreType.DMA((2, dp - 1)),
        ]
        + scatter_scratch(dp, rows, columns),
        compiler_params=pltpu.CompilerParams(
            collective_id=collective_id, has_side_effects=True, vmem_limit_bytes=VMEM_LIMIT
        ),
        cost_estimate=pl.CostEstimate(
            flops=2 * lhs.size * columns, bytes_accessed=2 * lhs.size, transcendentals=0
        ),
    )(lhs, rhs, gains)


def row_chunks(matrix, count):
    chunks = matrix.reshape(count, matrix.shape[0] // count, matrix.shape[1])
    return jnp.pad(chunks, ((0, 0), (0, -chunks.shape[1] % 16), (0, 0)))


def per_device(
    tokens_in,
    attn_gain,
    w_query,
    w_key,
    w_value,
    w_output,
    mlp_gain,
    w_gate,
    w_up,
    w_down,
    counts,
    segments,
    cotangent,
):
    row_count = tokens_in.shape[0]
    head_width = w_key.shape[1]
    pack_count, group_count = lax.axis_size("dp"), lax.axis_size("kv")
    sizes = (pack_count, group_count)
    pack = lax.axis_index("dp")
    share = w_query.shape[0] // pack_count
    w_pair = jnp.concatenate([w_key, w_value], axis=1)

    def own_share(matrix):
        return lax.dynamic_slice_in_dim(matrix, pack * share, share, 0)

    out_part = lax.dynamic_slice_in_dim(w_output[0], pack * share, share, 1).T
    qkv_part = jnp.concatenate([own_share(w_query), own_share(w_pair)], axis=1)
    live_rows = (jnp.arange(row_count) < counts[0]).astype(jnp.float32)[:, None]
    (
        attn_out,
        act_flipped,
        query,
        key,
        value,
        logsums,
        cosine,
        sine_a,
        sine_b,
        cosine_t,
        sine_t,
        out_parts,
    ) = attention(tokens_in, attn_gain[None], w_query, w_pair, segments, out_part, group_count, 5)
    (
        second_flipped,
        hidden_flipped,
        grad_gate,
        grad_up,
        grad_act_two,
        feed_part,
        resid_mine,
        attn_others,
        out_others,
    ) = feed_forward(
        attn_out,
        out_parts,
        w_output[0],
        w_gate,
        w_up,
        w_down[0],
        cotangent,
        live_rows,
        tokens_in,
        mlp_gain[None],
        sizes,
        1,
    )
    second_chunks = row_chunks(second_flipped, pack_count)
    sent_gate, sent_up, sent_down, qkv_parts = product_scatter(
        [
            (second_chunks, grad_gate),
            (second_chunks, grad_up),
            (row_chunks(hidden_flipped, pack_count), cotangent),
        ],
        qkv_part,
        group_count,
        2,
    )
    grad_two_mine = lax.psum_scatter(grad_act_two, "kv", scatter_dimension=0, tiled=True)
    grad_two_mine, feed_part, qkv_parts = lax.optimization_barrier(
        (grad_two_mine, feed_part, qkv_parts)
    )
    grad_tokens, gain_rows, sent_output, grad_qkv, _ = attention_back(
        (
            grad_two_mine,
            resid_mine,
            cotangent,
            live_rows,
            tokens_in,
            attn_gain[None],
            mlp_gain[None],
            w_output[0],
            out_others.reshape(group_count - 1, -1, w_output.shape[1]),
            attn_others,
            query,
            key,
            value,
            logsums,
            attn_out,
            segments[:, None],
            segments[None],
            cosine_t,
            sine_t,
            cosine,
            sine_a,
            sine_b,
            w_query,
            w_pair,
            qkv_parts,
        ),
        sizes,
        head_width,
        3,
    )
    sent_query, sent_key, sent_value, gains = last_sums(
        row_chunks(act_flipped, pack_count), grad_qkv, gain_rows, head_width, group_count, 4
    )
    sent_two, sent_one = gains[0], gains[1]
    sent_output = sent_output[None]
    sent_down = sent_down[: w_down.shape[1] // pack_count][None]
    layer_out = (
        resid_mine
        + lax.psum_scatter(feed_part, "kv", scatter_dimension=0, tiled=True).astype(jnp.float32)
    ).astype(jnp.bfloat16)
    return (
        layer_out,
        grad_tokens,
        sent_one,
        sent_query,
        sent_key,
        sent_value,
        sent_output,
        sent_two,
        sent_gate,
        sent_up,
        sent_down,
    )


def solution(mesh):
    return jax.shard_map(
        per_device,
        mesh=mesh,
        in_specs=(
            P("dp", None),
            P(),
            P(None, "kv"),
            P(None, "kv"),
            P(None, "kv"),
            P("kv", None, None),
            P(),
            P(None, "kv"),
            P(None, "kv"),
            P("kv", None, None),
            P("dp"),
            P("dp"),
            P("dp", None),
        ),
        out_specs=(
            P(("dp", "kv"), None),
            P(("dp", "kv"), None),
            P("dp"),
            P("dp", "kv"),
            P("dp", "kv"),
            P("dp", "kv"),
            P("kv", "dp", None),
            P("dp"),
            P("dp", "kv"),
            P("dp", "kv"),
            P("kv", "dp", None),
        ),
        check_vma=False,
    )
```

```python
import functools

import jax
import jax.numpy as jnp
from jax import lax
from jax.experimental import pallas as pl
from jax.experimental.pallas import tpu as pltpu
from jax.sharding import PartitionSpec as P

EPS = 1e-05
LOG2E = 1.4426950408889634
MESH = pl.DeviceIdType.MESH
VMEM_LIMIT = 60 * 1024 * 1024


def row_halves(rows):
    upper = -(-rows // 32) * 16
    return ((0, upper), (upper, rows - upper))


def times(first, second):
    return jnp.dot(first, second, preferred_element_type=jnp.float32)


def times_t(first, second):
    return lax.dot_general(
        first, second, (((1,), (1,)), ((), ())), preferred_element_type=jnp.float32
    )


def to_group(step, groups, source, target, sems):
    return pltpu.make_async_remote_copy(
        src_ref=source,
        dst_ref=target,
        send_sem=sems.at[0, step - 1],
        recv_sem=sems.at[1, step - 1],
        device_id={"kv": (lax.axis_index("kv") + step) % groups},
        device_id_type=MESH,
    )


class Spread:
    def __init__(self, buffer, send_sem, recv_sem, dp):
        self.buffer, self.send_sem, self.recv_sem = buffer, send_sem, recv_sem
        self.me = lax.axis_index("dp")
        self.bits = dp.bit_length() - 1
        rows = buffer.shape[2]
        self.halves = row_halves(rows)

    def flipped(self, places):
        device = self.me
        for place in places:
            device = device + 2**place * (1 - 2 * ((self.me // 2**place) % 2))
        return device

    def copies(self, stage, arriving):
        result = []
        for half in range(2):
            order = list(range(1, self.bits))
            order = (order if half == 0 else order[::-1]) + [0]
            for subset in range(2**stage):
                places = [order[b] for b in range(stage) if subset >> b & 1]
                if arriving:
                    places = places + [order[stage]]
                part = self.buffer.at[:, self.flipped(places), pl.ds(*self.halves[half])]
                number = 2**stage - 1 + subset
                result.append(
                    pltpu.make_async_remote_copy(
                        src_ref=part,
                        dst_ref=part,
                        send_sem=self.send_sem.at[half, number],
                        recv_sem=self.recv_sem.at[half, number],
                        device_id={"dp": self.flipped([order[stage]])},
                        device_id_type=MESH,
                    )
                )
        return result

    def start(self, stage):
        for copy in self.copies(stage, False):
            copy.start()

    def wait_recv(self, stage):
        for copy in self.copies(stage, True):
            copy.wait_recv()

    def wait_send(self):
        for stage in range(self.bits):
            for copy in self.copies(stage, False):
                copy.wait_send()


def greet(dp, groups):
    pack, group = lax.axis_index("dp"), lax.axis_index("kv")
    bits = dp.bit_length() - 1
    barrier = pltpu.get_barrier_semaphore()
    for place in range(bits):
        other = pack + 2**place * (1 - 2 * ((pack // 2**place) % 2))
        pl.semaphore_signal(barrier, inc=1, device_id={"dp": other}, device_id_type=MESH)
    for step in range(1, groups):
        other = (group + step) % groups
        pl.semaphore_signal(barrier, inc=1, device_id={"kv": other}, device_id_type=MESH)
    pl.semaphore_wait(barrier, bits + groups - 1)


def attention_kernel(groups, head_width, *refs):
    (
        tokens_ref, gain_ref, query_w, pair_w, seg_column, seg_row, frequency, part_hbm,
        attn_out, act_out, query_out, key_out, value_out, logsum_out,
        cosine_out, sine_a_out, sine_b_out, cosine_t_out, sine_t_out, parts_out,
        query_m, value_t, part_sems,
    ) = refs
    rows = tokens_ref.shape[0] // groups
    width, span_w = query_w.shape[1], key_out.shape[1]
    heads, pair, half = span_w // head_width, 2 * head_width, head_width // 2
    scale = head_width**-0.5 * LOG2E

    def part_copy(step):
        return to_group(step, groups, part_hbm, parts_out.at[groups - 1 - step], part_sems)

    greet(1, groups)
    for step in range(1, groups):
        part_copy(step).start()
    lanes = lax.broadcasted_iota(jnp.int32, (rows, pair), 1)
    low_half = lanes % head_width < half
    head_lanes = lax.broadcasted_iota(jnp.int32, (rows, span_w), 1) // head_width

    for block in range(groups):
        part = pl.ds(block * rows, rows)
        values = tokens_ref[part].astype(jnp.float32)
        inverse = lax.rsqrt(jnp.mean(values * values, axis=1, keepdims=True) + EPS)
        act = (values * inverse * gain_ref[...]).astype(jnp.bfloat16)
        act_out[:, part] = act.T
        query_raw = times(act, query_w[...])
        pair_raw = times(act, pair_w[...])
        before = (seg_row[...] < seg_column[part]).astype(jnp.float32)
        places = (
            lax.broadcasted_iota(jnp.int32, (rows, 1), 0) + block * rows
        ).astype(jnp.float32) - jnp.sum(before, axis=1, keepdims=True)
        angles = places * frequency[...]
        cosine, sine = jnp.cos(angles), jnp.sin(angles)
        sine_a, sine_b = jnp.where(low_half, -sine, 0.0), jnp.where(low_half, 0.0, sine)
        cosine_out[part], sine_a_out[part], sine_b_out[part] = cosine, sine_a, sine_b
        cosine_t_out[:, part] = cosine.T[:half]
        sine_t_out[:, part] = sine.T[:half]

        def rotated(vectors):
            return (
                vectors * cosine
                + pltpu.roll(vectors, pair - half, 1) * sine_a
                + pltpu.roll(vectors, half, 1) * sine_b
            ).astype(jnp.bfloat16)

        for start in range(0, width, pair):
            query_out[part, pl.ds(start, pair)] = rotated(query_raw[:, start : start + pair])
        other = pltpu.roll(pair_raw, head_width, 1)
        keys_two = rotated(jnp.where(lanes < head_width, pair_raw, other))
        values_two = jnp.where(lanes < head_width, other, pair_raw)
        key_out[part] = jnp.concatenate([keys_two] * (span_w // pair), axis=1)
        value_out[part] = jnp.concatenate(
            [values_two.astype(jnp.bfloat16)] * (span_w // pair), axis=1
        )
        value_t[:, part] = values_two.T[:head_width].astype(jnp.bfloat16)
        query_seg = seg_row[:, part]
        query_place = lax.broadcasted_iota(jnp.int32, (rows, rows), 1) + block * rows

        def span(number, carry):
            columns = pl.ds(pl.multiple_of(number * span_w, span_w), span_w)
            query = query_out[part, columns]
            for head in range(heads):
                query_m[pl.ds(head * rows, rows)] = jnp.where(head_lanes == head, query, 0)

            def keys(step, carry):
                highest, total, output = carry
                piece = block - step
                key_part = pl.ds(pl.multiple_of(piece * rows, rows), rows)
                key_place = lax.broadcasted_iota(jnp.int32, (rows, rows), 0) + piece * rows
                allowed = (seg_column[key_part] == query_seg) & (key_place <= query_place)
                bias = jnp.where(allowed, 0.0, -jnp.inf)
                scores = times_t(key_out[key_part], query_m[...]) * scale
                scores = scores + jnp.concatenate([bias] * heads, axis=1)
                top = jnp.maximum(highest, jnp.max(scores, axis=0, keepdims=True))
                shrink = jnp.exp2(highest - top)
                chance = jnp.exp2(scores - top)
                total = total * shrink + jnp.sum(chance, axis=0, keepdims=True)
                output = output * shrink + times(value_t[:, key_part], chance.astype(jnp.bfloat16))
                return top, total, output

            first = (
                jnp.full((1, heads * rows), -jnp.inf, jnp.float32),
                jnp.zeros((1, heads * rows), jnp.float32),
                jnp.zeros((head_width, heads * rows), jnp.float32),
            )
            highest, total, output = lax.fori_loop(0, block + 1, keys, first)
            output = output / total
            stacked = jnp.concatenate(
                [output[:, head * rows : (head + 1) * rows] for head in range(heads)], axis=0
            )
            attn_out[part, columns] = stacked.T.astype(jnp.bfloat16)
            logsum_out[number * groups + block] = highest + jnp.log(total) * LOG2E
            return carry

        lax.fori_loop(0, width // span_w, span, 0)
    for step in range(1, groups):
        part_copy(step).wait()


def attention(tokens, gain, query_w, pair_w, segments, part, groups, collective_id):
    count, features = tokens.shape
    width, head_width = query_w.shape[1], pair_w.shape[1] // 2
    span_w = 256
    rows, heads, half = count // groups, span_w // head_width, head_width // 2
    frequency = 10000.0 ** (-(jnp.arange(half, dtype=jnp.float32) * 2.0 / head_width))
    vmem = pl.BlockSpec(memory_space=pltpu.VMEM)
    any_spec = pl.BlockSpec(memory_space=pl.ANY)
    bf16, f32 = jnp.bfloat16, jnp.float32
    return pl.pallas_call(
        functools.partial(attention_kernel, groups, head_width),
        out_shape=[
            jax.ShapeDtypeStruct((count, width), bf16),
            jax.ShapeDtypeStruct((features, count), bf16),
            jax.ShapeDtypeStruct((count, width), bf16),
            jax.ShapeDtypeStruct((count, span_w), bf16),
            jax.ShapeDtypeStruct((count, span_w), bf16),
            jax.ShapeDtypeStruct((width // span_w * groups, 1, heads * rows), f32),
            jax.ShapeDtypeStruct((count, 2 * head_width), f32),
            jax.ShapeDtypeStruct((count, 2 * head_width), f32),
            jax.ShapeDtypeStruct((count, 2 * head_width), f32),
            jax.ShapeDtypeStruct((half, count), f32),
            jax.ShapeDtypeStruct((half, count), f32),
            jax.ShapeDtypeStruct((groups - 1,) + part.shape, bf16),
        ],
        in_specs=[vmem] * 7 + [any_spec],
        out_specs=[vmem] * 11 + [any_spec],
        scratch_shapes=[
            pltpu.VMEM((heads * rows, span_w), bf16),
            pltpu.VMEM((head_width, count), bf16),
            pltpu.SemaphoreType.DMA((2, groups - 1)),
        ],
        compiler_params=pltpu.CompilerParams(
            collective_id=collective_id, has_side_effects=True, vmem_limit_bytes=VMEM_LIMIT
        ),
        cost_estimate=pl.CostEstimate(
            flops=4 * count * features * width, bytes_accessed=8 * tokens.size, transcendentals=0
        ),
    )(
        tokens,
        gain,
        query_w,
        pair_w,
        segments[:, None],
        segments[None],
        jnp.tile(frequency, 4)[None],
        part,
    )


def feed_forward_kernel(dp, groups, *refs):
    (
        attn_hbm, attn_ref, part_ref, own_hbm, gate_hbm, up_hbm, down_hbm, cot_hbm, live_hbm,
        tokens_ref, gain_ref, live_ref,
        act_out, hidden_out, gate_out, up_out, back_out, feed_a_out, feed_b_out, resid_out, rows_out, all_out,
        attn_in, all_ref, own_ref, w_gate, w_up, w_down, cot_ref, live_all, grad_hidden, resid_ref,
        load_sem, send_sem, recv_sem, spread_send, spread_recv, out_sem,
    ) = refs
    block = pl.program_id(0)
    blocks = groups
    group = lax.axis_index("kv")
    pack = lax.axis_index("dp")
    rows = tokens_ref.shape[0]
    others = groups - 1
    spread = Spread(all_ref, spread_send, spread_recv, dp)
    loads = [
        pltpu.make_async_copy(source, target, load_sem.at[index])
        for index, (source, target) in enumerate(
            (
                (down_hbm, w_down),
                (cot_hbm, cot_ref),
                (live_hbm, live_all),
                (own_hbm, own_ref),
                (gate_hbm, w_gate),
                (up_hbm, w_up),
            )
        )
    ]

    def attn_copy(part, step, slot, source, place):
        span = pl.ds(part * rows, rows)
        return pltpu.make_async_remote_copy(
            src_ref=source.at[span],
            dst_ref=attn_in.at[slot, span],
            send_sem=send_sem.at[part, place],
            recv_sem=recv_sem.at[part, slot],
            device_id={"kv": (group + step) % groups},
            device_id_type=MESH,
        )

    def send_rows(part):
        for step in range(1, groups):
            copy = attn_copy(part, step, others - step, attn_hbm, step - 1)
            if step in relayed:
                pl.when((group == 0) | (group == 3))(copy.start)
            else:
                copy.start()

    relayed = (2,) if groups == 4 else ()
    relays = ((1, 0, 3), (2, 2, 1)) if groups == 4 else ()

    def wait_rows(part, slot):
        attn_copy(part, 1, slot, attn_hbm, 0).wait_recv()

    def pass_on(part):
        for holder, slot, step in relays:

            @pl.when(group == holder)
            def _():
                wait_rows(part, slot)
                attn_copy(part, step, 1, attn_in.at[slot], 1).start()

    def wait_block(part):
        for slot in range(others):
            holders = [holder for holder, place, _ in relays if place == slot]
            if holders:

                @pl.when(group != holders[0])
                def _():
                    wait_rows(part, slot)
            else:
                wait_rows(part, slot)

    def hidden_gradient(part):
        span = pl.ds(part * rows, rows)
        masked = (cot_ref[span].astype(jnp.float32) * live_all[span]).astype(jnp.bfloat16)
        grad_hidden[span] = times_t(masked, w_down[...]).astype(jnp.bfloat16)

    @pl.when(block == 0)
    def _():
        for load in loads:
            load.start()
        all_ref[:, pack] = part_ref[...]
        greet(dp, groups)
        send_rows(0)
        spread.start(0)
        for part in range(1, blocks):
            send_rows(part)
        for load in loads[:3]:
            load.wait()
        stages = dp.bit_length() - 1
        for stage in range(stages):
            if stage < blocks:
                hidden_gradient(stage)
            spread.wait_recv(stage)
            if stage + 1 < stages:
                spread.start(stage + 1)
            if stage < 2:
                pass_on(stage)
        for part in range(stages, blocks):
            hidden_gradient(part)
        for load in loads[3:]:
            load.wait()

    wait_block(block)
    span = pl.ds(pl.multiple_of(block * rows, rows), rows)
    width = own_ref.shape[0]
    total = tokens_ref[...].astype(jnp.float32) + times(attn_ref[...], own_ref[...])
    for slot in range(others):
        total = total + times_t(attn_in[slot, span], all_ref[slot].reshape(-1, width))
    resid_ref[...] = total
    inverse = lax.rsqrt(jnp.mean(total * total, axis=1, keepdims=True) + EPS)
    act = (total * inverse * gain_ref[...]).astype(jnp.bfloat16)
    act_out[...] = act.T
    gate = times(act, w_gate[...])
    up = times(act, w_up[...])
    chance = jax.nn.sigmoid(gate)
    swish = gate * chance
    hidden = swish * up
    feed = times(hidden.astype(jnp.bfloat16), w_down[...]).astype(jnp.bfloat16)
    feed_a_out[...] = feed[:, : feed_a_out.shape[1]]
    feed_b_out[...] = feed[:, feed_a_out.shape[1] :]
    hidden_out[...] = (hidden * live_ref[...]).astype(jnp.bfloat16).T
    grad = grad_hidden[span].astype(jnp.float32)
    gate_b = (grad * up * chance * (1.0 + gate * (1.0 - chance))).astype(jnp.bfloat16)
    up_b = (grad * swish).astype(jnp.bfloat16)
    gate_out[...] = gate_b
    up_out[...] = up_b
    back_out[...] = (times_t(gate_b, w_gate[...]) + times_t(up_b, w_up[...])).astype(jnp.bfloat16)

    @pl.when(block == group)
    def _():
        copy = pltpu.make_async_copy(resid_ref, resid_out, out_sem.at[0])
        copy.start()
        copy.wait()

    @pl.when(block < blocks - 2)
    def _():
        pass_on(block + 2)

    @pl.when(block == blocks - 1)
    def _():
        mine = pl.ds(pl.multiple_of(group * rows, rows), rows)
        copies = [
            pltpu.make_async_copy(attn_in.at[:, mine], rows_out, out_sem.at[1]),
            pltpu.make_async_copy(all_ref, all_out, out_sem.at[2]),
        ]
        for copy in copies:
            copy.start()
        for part in range(blocks):
            for place in range(others):
                attn_copy(part, 1, 0, attn_hbm, place).wait_send()
        spread.wait_send()
        for copy in copies:
            copy.wait()


def feed_forward(attn, part, w_own, w_gate, w_up, w_down, cotangent, live, tokens, gain, sizes, collective_id):
    dp, groups = sizes
    count, features = tokens.shape
    rows = count // groups
    width, hidden = w_own.shape[0], w_gate.shape[1]
    share = part.shape[1]
    others = groups - 1
    early = features // 2
    any_spec = pl.BlockSpec(memory_space=pl.ANY)
    by_row = lambda columns: pl.BlockSpec((rows, columns), lambda i: (i, 0))
    by_column = lambda height: pl.BlockSpec((height, rows), lambda i: (0, i))
    flops = 2 * count * features * (groups * width + 6 * hidden)
    return pl.pallas_call(
        functools.partial(feed_forward_kernel, dp, groups),
        grid=(groups,),
        out_shape=[
            jax.ShapeDtypeStruct((features, count), jnp.bfloat16),
            jax.ShapeDtypeStruct((hidden, count), jnp.bfloat16),
            jax.ShapeDtypeStruct((count, hidden), jnp.bfloat16),
            jax.ShapeDtypeStruct((count, hidden), jnp.bfloat16),
            jax.ShapeDtypeStruct((count, features), jnp.bfloat16),
            jax.ShapeDtypeStruct((count, early), jnp.bfloat16),
            jax.ShapeDtypeStruct((count, features - early), jnp.bfloat16),
            jax.ShapeDtypeStruct((rows, features), jnp.float32),
            jax.ShapeDtypeStruct((others, rows, width), jnp.bfloat16),
            jax.ShapeDtypeStruct((others, dp, share, width), jnp.bfloat16),
        ],
        in_specs=[
            any_spec,
            by_row(width),
            pl.BlockSpec(memory_space=pltpu.VMEM),
            any_spec, any_spec, any_spec, any_spec, any_spec, any_spec,
            by_row(features),
            pl.BlockSpec(memory_space=pltpu.VMEM),
            by_row(1),
        ],
        out_specs=[
            by_column(features), by_column(hidden), by_row(hidden), by_row(hidden),
            by_row(features), by_row(early), by_row(features - early), any_spec, any_spec, any_spec,
        ],
        scratch_shapes=[
            pltpu.VMEM((others, count, width), jnp.bfloat16),
            pltpu.VMEM((others, dp, share, width), jnp.bfloat16),
            pltpu.VMEM((width, features), jnp.bfloat16),
            pltpu.VMEM((features, hidden), jnp.bfloat16),
            pltpu.VMEM((features, hidden), jnp.bfloat16),
            pltpu.VMEM((hidden, features), jnp.bfloat16),
            pltpu.VMEM((count, features), jnp.bfloat16),
            pltpu.VMEM((count, 1), jnp.float32),
            pltpu.VMEM((count, hidden), jnp.bfloat16),
            pltpu.VMEM((rows, features), jnp.float32),
            pltpu.SemaphoreType.DMA((6,)),
            pltpu.SemaphoreType.DMA((groups, others)),
            pltpu.SemaphoreType.DMA((groups, others)),
            pltpu.SemaphoreType.DMA((2, dp - 1)),
            pltpu.SemaphoreType.DMA((2, dp - 1)),
            pltpu.SemaphoreType.DMA((3,)),
        ],
        compiler_params=pltpu.CompilerParams(
            collective_id=collective_id, has_side_effects=True, vmem_limit_bytes=VMEM_LIMIT
        ),
        cost_estimate=pl.CostEstimate(flops=flops, bytes_accessed=40 * count * features, transcendentals=0),
    )(attn, attn, part, w_own, w_gate, w_up, w_down, cotangent, live, tokens, gain, live)


class Scatter:
    def __init__(self, dp, product, store, sent, held, late, sems):
        self.product, self.store, self.sent, self.held, self.late = product, store, sent, held, late
        self.first_send, self.first_recv, self.late_send, self.late_recv = sems
        self.me = lax.axis_index("dp")
        self.upper = self.me // 2
        self.bits = dp.bit_length() - 1
        self.slots = dp // 2
        self.halves = row_halves(held.shape[1])

    def bit(self, place):
        return (self.me // 2**place) % 2

    def partner(self, place):
        return self.me + 2**place * (1 - 2 * self.bit(place))

    def first_copy(self, t):
        return pltpu.make_async_remote_copy(
            src_ref=self.sent.at[t],
            dst_ref=self.held.at[t],
            send_sem=self.first_send.at[t],
            recv_sem=self.first_recv.at[t],
            device_id={"dp": self.partner(0)},
            device_id_type=MESH,
        )

    def stage_bit(self, half, stage):
        return stage - 1 if half == 0 else self.bits - 1 - stage

    def slot_of(self, half, stage, index, value):
        if half == 0:
            low = 2 ** (stage - 1)
            return index * 2**stage + value * low + self.upper % low
        top = 2 ** (self.bits - stage)
        return index + value * (top // 2) + (self.upper // top) * top

    def late_copy(self, half, stage, index, slot):
        start, size = self.halves[half]
        buffer = self.slots - 2 ** (self.bits - stage) + index
        return pltpu.make_async_remote_copy(
            src_ref=self.held.at[slot, pl.ds(start, size)],
            dst_ref=self.late[half].at[buffer],
            send_sem=self.late_send.at[half, buffer],
            recv_sem=self.late_recv.at[half, buffer],
            device_id={"dp": self.partner(self.stage_bit(half, stage) + 1)},
            device_id_type=MESH,
        )

    def other_chunks(self):
        def step(t, carry):
            self.sent[t] = self.product(2 * t + 1 - self.bit(0)).astype(jnp.bfloat16)
            self.first_copy(t).start()
            return carry

        lax.fori_loop(0, self.slots, step, 0)

    def own_chunks(self):
        def step(e, carry):
            t = 0
            for place in range(self.bits - 1):
                t = t + 2**place * ((e // 2**place + 1 + self.upper // 2**place) % 2)
            own = self.product(2 * t + self.bit(0))
            self.first_copy(t).wait_recv()
            self.held[t] = (self.held[t].astype(jnp.float32) + own).astype(jnp.bfloat16)

            @pl.when(e % 2 == 0)
            def _():
                self.late_copy(0, 1, t // 2, t).start()

            @pl.when(e < self.slots // 2)
            def _():
                self.late_copy(1, 1, t % (self.slots // 2), t).start()

            return carry

        lax.fori_loop(0, self.slots, step, 0)

    def later(self, stage):
        for half in range(2):
            start, size = self.halves[half]
            keep_bit = self.bit(self.stage_bit(half, stage) + 1)
            for index in range(2 ** (self.bits - 1 - stage)):
                slot = self.slot_of(half, stage, index, keep_bit)
                self.late_copy(half, stage, index, slot).wait_recv()
                buffer = self.slots - 2 ** (self.bits - stage) + index
                total = self.held[slot, pl.ds(start, size)].astype(jnp.float32) + self.late[half][
                    buffer
                ].astype(jnp.float32)
                if stage == self.bits - 1:
                    self.store(start, size, total)
                else:
                    self.held[slot, pl.ds(start, size)] = total.astype(jnp.bfloat16)
            if stage < self.bits - 1:
                follow = self.stage_bit(half, stage + 1) + 1
                for index in range(2 ** (self.bits - 2 - stage)):
                    slot = self.slot_of(half, stage + 1, index, 1 - self.bit(follow))
                    self.late_copy(half, stage + 1, index, slot).start()

    def finish(self):
        for t in range(self.slots):
            self.first_copy(t).wait_send()
        for half in range(2):
            for stage in range(1, self.bits):
                for index in range(2 ** (self.bits - 1 - stage)):
                    self.late_copy(half, stage, index, 0).wait_send()


def scatter_scratch(dp, rows, columns):
    slots = dp // 2
    return (
        [pltpu.VMEM((slots, rows, columns), jnp.bfloat16)] * 2
        + [pltpu.VMEM((slots - 1, size, columns), jnp.bfloat16) for _, size in row_halves(rows)]
        + [pltpu.SemaphoreType.DMA((slots,))] * 2
        + [pltpu.SemaphoreType.DMA((2, slots - 1))] * 2
    )


def scatter_from(dp, product, store, refs):
    return Scatter(dp, product, store, refs[0], refs[1], refs[2:4], refs[4:8])


def product_scatter_kernel(count, dp, groups, *refs):
    lhs, rhs, pass_ref = refs[:count], refs[count : 2 * count], refs[2 * count]
    outs, pass_out = refs[2 * count + 1 : 3 * count + 1], refs[3 * count + 1]
    pass_sems, scratch = refs[3 * count + 2], refs[3 * count + 3 :]

    def pass_copy(step):
        return to_group(step, groups, pass_ref, pass_out.at[groups - 1 - step], pass_sems)

    def member(a):
        def product(chunk):
            return times(lhs[a][chunk], rhs[a][...])

        def store(start, size, total):
            outs[a][pl.ds(start, size)] = total

        return scatter_from(dp, product, store, scratch[8 * a : 8 * a + 8])

    members = [member(a) for a in range(count)]
    stages = dp.bit_length() - 1
    greet(dp, groups)
    for step in range(1, groups):
        pass_copy(step).start()
    pending = []
    for a in range(count):
        members[a].other_chunks()
        members[a].own_chunks()
        pending.append((a, 1))
        if a > 0:
            done, stage = pending.pop(0)
            members[done].later(stage)
            if stage < stages - 1:
                pending.append((done, stage + 1))
    while pending:
        done, stage = pending.pop(0)
        members[done].later(stage)
        if stage < stages - 1:
            pending.append((done, stage + 1))
    for one in members:
        one.finish()
    for step in range(1, groups):
        pass_copy(step).wait()


def product_scatter(pairs, passed, groups, collective_id):
    count = len(pairs)
    dp = pairs[0][0].shape[0]
    dims = [(lhs.shape[1], rhs.shape[1]) for lhs, rhs in pairs]
    flops = sum(2 * lhs.size * rhs.shape[1] for lhs, rhs in pairs)
    moved = sum(2 * (lhs.size + rhs.size) for lhs, rhs in pairs)
    vmem = pl.BlockSpec(memory_space=pltpu.VMEM)
    any_spec = pl.BlockSpec(memory_space=pl.ANY)
    return pl.pallas_call(
        functools.partial(product_scatter_kernel, count, dp, groups),
        out_shape=[jax.ShapeDtypeStruct(dim, jnp.float32) for dim in dims]
        + [jax.ShapeDtypeStruct((groups - 1,) + passed.shape, passed.dtype)],
        in_specs=[vmem] * (2 * count) + [any_spec],
        out_specs=[vmem] * count + [any_spec],
        scratch_shapes=[pltpu.SemaphoreType.DMA((2, groups - 1))]
        + sum([scatter_scratch(dp, *dim) for dim in dims], []),
        compiler_params=pltpu.CompilerParams(
            collective_id=collective_id, has_side_effects=True, vmem_limit_bytes=VMEM_LIMIT
        ),
        cost_estimate=pl.CostEstimate(flops=flops * 3, bytes_accessed=moved, transcendentals=0),
    )(*[lhs for lhs, _ in pairs], *[rhs for _, rhs in pairs], passed)


def norm_back(values, gain, grads):
    inverse = lax.rsqrt(jnp.mean(values * values, axis=1, keepdims=True) + EPS)
    scaled = gain * grads
    mean = jnp.mean(scaled * values, axis=1, keepdims=True)
    by_values = inverse * scaled - values * (inverse * inverse * inverse * mean)
    return by_values, jnp.sum(grads * values * inverse, axis=0, keepdims=True)


def attention_back_kernel(dp, groups, head_width, *refs):
    (
        back_ref, resid_hbm, cot_hbm, live_ref, tokens_hbm, attn_gain, mlp_gain,
        out_own, out_others, rows_ref, query_ref, key_ref, value_ref, logsum_ref, attn_ref,
        seg_column, seg_row, cosine_t, sine_t, cosine, sine_a, sine_b, qkv_own, pair_own, qkv_parts,
        tokens_out, gains_out, output_out, out_send, grad_out, qkv_all,
        cot_ref, tokens_ref, chunk_ref, weights, query_m, attn_m, key_t, query_t, key_sum, value_sum,
        attn_send, attn_grad, arrived, branch_ref,
        load_sem, last_sem, attn_sems, grad_sems, spread_send, spread_recv, *scatter_refs,
    ) = refs
    group, pack, others = lax.axis_index("kv"), lax.axis_index("dp"), groups - 1
    rows = branch_ref.shape[0]
    width = query_ref.shape[1]
    span_w = key_ref.shape[1]
    pair, half, heads = 2 * head_width, head_width // 2, span_w // head_width
    scale = head_width**-0.5
    mine = pl.ds(pl.multiple_of(group * rows, rows), rows)
    out_part = pl.ds(0, width)

    def load(index, source, target):
        return pltpu.make_async_copy(source, target, load_sem.at[index])

    first_loads = [
        load(0, resid_hbm, tokens_out),
        load(1, cot_hbm.at[mine], cot_ref),
        load(2, out_others, weights.at[:, :, out_part]),
        load(3, qkv_parts, qkv_all.at[:, pack]),
        load(4, tokens_hbm.at[mine], tokens_ref),
    ]
    for one in first_loads:
        one.start()

    spans = width // span_w

    def attn_copy(number, step):
        return to_group(
            step, groups, attn_send.at[number, step - 1], attn_grad.at[number, group], attn_sems.at[number]
        )

    def columns_of(number):
        start = number * span_w
        return pl.ds(start, span_w if number < spans - 1 else width + pair - start)

    def grad_copy(number, step, block):
        columns = columns_of(number)
        return to_group(
            step,
            groups,
            grad_out.at[pl.ds(block * rows, rows), columns],
            arrived.at[step - 1, :, columns],
            grad_sems.at[number],
        )

    share = output_out.shape[0]

    greet(dp, groups)
    spread = Spread(qkv_all, spread_send, spread_recv, dp)
    lanes = lax.broadcasted_iota(jnp.int32, (rows, span_w), 1) // head_width
    first_loads[3].wait()
    spread.start(0)
    first_loads[0].wait()
    first_loads[1].wait()
    values = tokens_out[...]
    grad_resid, mlp_rows = norm_back(values, mlp_gain[...], back_ref[...].astype(jnp.float32))
    grad_resid = grad_resid + cot_ref[...].astype(jnp.float32) * live_ref[mine]
    tokens_out[...] = grad_resid
    branch_ref[...] = grad_resid.astype(jnp.bfloat16)
    stages = dp.bit_length() - 1
    first_loads[2].wait()
    for number in range(spans):
        columns = pl.ds(number * span_w, span_w)
        for step in range(1, groups):
            attn_send[number, step - 1] = times(branch_ref[...], weights[step - 1, :, columns]).astype(
                jnp.bfloat16
            )
            attn_copy(number, step).start()
        attn_grad[number, group] = times_t(branch_ref[...], out_own[columns]).astype(jnp.bfloat16)

    spread.wait_recv(0)
    spread.start(1)

    def store(start, size, total):
        if start == 0:
            output_out[...] = total[:share]
        out_send[pl.ds(start, size)] = total.astype(jnp.bfloat16)

    scatter = scatter_from(dp, lambda chunk: times(chunk_ref[chunk], branch_ref[...]), store, scatter_refs)
    for place in range(groups):
        turned = (attn_ref[mine] if place == 0 else rows_ref[place - 1]).T
        chunk_ref[:, pl.ds(place * share, share)] = turned.reshape(dp, share, rows)
    scatter.other_chunks()
    scatter.own_chunks()
    for block in range(groups):
        part = pl.ds(block * rows, rows)
        key_t[:, part] = key_ref[part, pl.ds(0, pair)].T[:head_width]
    key_sum[...] = jnp.zeros_like(key_sum)
    value_sum[...] = jnp.zeros_like(value_sum)

    def attend(number, block):
        part = pl.ds(block * rows, rows)

        @pl.when(block != group)
        def _():
            step = (group - block + groups) % groups
            landed = attn_grad.at[number, block]
            to_group(step, groups, landed, landed, attn_sems.at[number]).wait_recv()

        query_seg = seg_row[:, part]
        query_place = lax.broadcasted_iota(jnp.int32, (rows, rows), 1) + block * rows

        def wide(entries):
            return jnp.concatenate([entries] * heads, axis=1)

        if True:
            columns = pl.ds(number * span_w, span_w)
            query = query_ref[part, columns]
            grad = attn_grad[number, block]
            weighed = (grad.astype(jnp.float32) * attn_ref[part, columns].astype(jnp.float32)).T
            centres = jnp.sum(weighed.reshape(heads, head_width, rows), axis=1)
            centre = jnp.concatenate([centres[head : head + 1] for head in range(heads)], axis=1)
            logsum = logsum_ref[number * groups + block]
            for head in range(heads):
                place = pl.ds(head * rows, rows)
                query_m[place] = jnp.where(lanes == head, query, 0)
                attn_m[place] = jnp.where(lanes == head, grad, 0)
            query_t[...] = jnp.zeros_like(query_t)

            def keys(piece, carry):
                key_part = pl.ds(pl.multiple_of(piece * rows, rows), rows)
                key_place = lax.broadcasted_iota(jnp.int32, (rows, rows), 0) + piece * rows
                allowed = (seg_column[key_part] == query_seg) & (key_place <= query_place)
                bias = jnp.where(allowed, 0.0, -jnp.inf)
                scores = times_t(key_ref[key_part], query_m[...]) * (scale * LOG2E)
                chance = jnp.exp2(scores - logsum + wide(bias))
                probs = times_t(value_ref[key_part], attn_m[...])
                slope = (chance * (probs - centre)).astype(jnp.bfloat16)
                value_sum[key_part] += times(chance.astype(jnp.bfloat16), attn_m[...])
                key_sum[key_part] += times(slope, query_m[...])
                query_t[...] += times(key_t[:, key_part], slope)
                return carry

            lax.fori_loop(0, block + 1, keys, 0)
            cos, sin = wide(cosine_t[:, part]), wide(sine_t[:, part])
            low, high = query_t[:half] * scale, query_t[half:] * scale
            turned = jnp.concatenate([low * cos + high * sin, high * cos - low * sin], axis=0)
            stacked = jnp.concatenate(
                [turned[:, head * rows : (head + 1) * rows] for head in range(heads)], axis=0
            )
            grad_out[part, columns] = stacked.T.astype(jnp.bfloat16)

        def folded(total):
            sums = total[part, pl.ds(0, pair)]
            for step in range(1, span_w // pair):
                sums = sums + total[part, pl.ds(step * pair, pair)]
            return sums + pltpu.roll(sums, head_width, 1)

        if number == spans - 1:
            grad_k = folded(key_sum) * scale
            grad_k = (
                grad_k * cosine[part]
                - pltpu.roll(grad_k, pair - half, 1) * sine_a[part]
                - pltpu.roll(grad_k, half, 1) * sine_b[part]
            )
            first = lax.broadcasted_iota(jnp.int32, (rows, pair), 1) < head_width
            grad_out[part, pl.ds(width, pair)] = jnp.where(
                first, grad_k, folded(value_sum)
            ).astype(jnp.bfloat16)

        @pl.when(block != group)
        def _():
            grad_copy(number, (block - group + groups) % groups, block).start()

    turns = [(number, block) for number in range(spans) for block in reversed(range(groups))]
    for turn, (number, block) in enumerate(turns):
        attend(number, block)
        if turn == 3:
            for stage in range(1, stages - 1):
                spread.wait_recv(stage)
                spread.start(stage + 1)
    for stage in range(1, stages - 1):
        scatter.later(stage)
    spread.wait_recv(stages - 1)
    part_rows = qkv_all.shape[2]
    last_loads = [
        pltpu.make_async_copy(
            qkv_all.at[:, place], weights.at[:, pl.ds(place * part_rows, part_rows)], last_sem.at[place]
        )
        for place in range(dp)
    ]
    for one in last_loads:
        one.start()
    grad_act = times_t(grad_out[mine, out_part], qkv_own[...])
    grad_act = grad_act + times_t(grad_out[mine, pl.ds(width, pair)], pair_own[...])
    for one in last_loads:
        one.wait()
    for number in range(spans):
        columns = columns_of(number)
        for step in range(1, groups):
            landed = arrived.at[step - 1, :, columns]
            to_group(step, groups, landed, landed, grad_sems.at[number]).wait_recv()
            grad_act = grad_act + times_t(
                arrived[step - 1, :, columns], weights[others - step, :, columns]
            )
    first_loads[4].wait()
    by_tokens, attn_rows = norm_back(tokens_ref[...].astype(jnp.float32), attn_gain[...], grad_act)
    tokens_out[...] += by_tokens
    scatter.later(stages - 1)
    columns = gains_out.shape[2]
    for place in range(dp):
        span = slice(place * columns, (place + 1) * columns)
        gains_out[place, 0:1] = mlp_rows[:, span]
        gains_out[place, 1:2] = attn_rows[:, span]
    for step in range(1, groups):
        for number in range(spans):
            attn_copy(number, step).wait_send()
            grad_copy(number, step, 0).wait_send()
    spread.wait_send()
    scatter.finish()


def attention_back(operands, sizes, head_width, collective_id):
    dp, groups = sizes
    others_w, rows_others, query, key, parts = (operands[index] for index in (8, 9, 10, 11, 24))
    rows, width = rows_others.shape[1:]
    features = others_w.shape[1]
    count, span_w = key.shape
    share = width // dp
    stacked = (span_w // head_width) * rows
    columns = width + 2 * head_width
    vmem = pl.BlockSpec(memory_space=pltpu.VMEM)
    any_spec = pl.BlockSpec(memory_space=pl.ANY)
    bf16, f32 = jnp.bfloat16, jnp.float32
    flops = 2 * count * count * width * 10
    return pl.pallas_call(
        functools.partial(attention_back_kernel, dp, groups, head_width),
        out_shape=[
            jax.ShapeDtypeStruct((rows, features), f32),
            jax.ShapeDtypeStruct((dp, 2, features // dp), f32),
            jax.ShapeDtypeStruct((share, features), f32),
            jax.ShapeDtypeStruct((groups * share, features), bf16),
            jax.ShapeDtypeStruct((count, columns), bf16),
            jax.ShapeDtypeStruct((groups - 1, dp) + parts.shape[1:], bf16),
        ],
        in_specs=[any_spec if index in (1, 2, 4, 8, 24) else vmem for index in range(25)],
        out_specs=[vmem] * 5 + [any_spec],
        scratch_shapes=[
            pltpu.VMEM((rows, features), bf16),
            pltpu.VMEM((rows, features), bf16),
            pltpu.VMEM((dp, groups * share, rows), bf16),
            pltpu.VMEM((groups - 1, features, columns), bf16),
            pltpu.VMEM((stacked, span_w), bf16),
            pltpu.VMEM((stacked, span_w), bf16),
            pltpu.VMEM((head_width, count), bf16),
            pltpu.VMEM((head_width, stacked), f32),
            pltpu.VMEM((count, span_w), f32),
            pltpu.VMEM((count, span_w), f32),
            pltpu.VMEM((width // span_w, groups - 1, rows, span_w), bf16),
            pltpu.VMEM((width // span_w, groups, rows, span_w), bf16),
            pltpu.VMEM((groups - 1, rows, columns), bf16),
            pltpu.VMEM((rows, features), bf16),
            pltpu.SemaphoreType.DMA((5,)),
            pltpu.SemaphoreType.DMA((dp,)),
            pltpu.SemaphoreType.DMA((width // span_w, 2, groups - 1)),
            pltpu.SemaphoreType.DMA((width // span_w, 2, groups - 1)),
            pltpu.SemaphoreType.DMA((2, dp - 1)),
            pltpu.SemaphoreType.DMA((2, dp - 1)),
        ]
        + scatter_scratch(dp, groups * share, features),
        compiler_params=pltpu.CompilerParams(
            collective_id=collective_id, has_side_effects=True, vmem_limit_bytes=VMEM_LIMIT
        ),
        cost_estimate=pl.CostEstimate(flops=flops, bytes_accessed=40 * 2**20, transcendentals=0),
    )(*operands)


def last_sums_kernel(dp, groups, lhs_ref, rhs_ref, gains_ref, output_ref, sums_ref, query_out, key_out, value_out, output_out, gains_out, out_recv, out_sems, near, far, total, near_sems, far_sems, *scatter_refs):
    pack, group = lax.axis_index("dp"), lax.axis_index("kv")

    def store(start, size, value):
        span, width, head_width = pl.ds(start, size), query_out.shape[1], key_out.shape[1]
        query_out[span] = value[:, :width]
        key_out[span] = value[:, width : width + head_width]
        value_out[span] = value[:, width + head_width :]

    scatter = scatter_from(dp, lambda chunk: times(lhs_ref[chunk], rhs_ref[...]), store, scatter_refs)

    share = output_out.shape[0]

    def out_copy(step):
        source = sums_ref.at[pl.ds(step * share, share)]
        return to_group(step, groups, source, out_recv.at[step - 1], out_sems)

    def near_copy(step):
        return pltpu.make_async_remote_copy(
            src_ref=gains_ref,
            dst_ref=near.at[step - 1],
            send_sem=near_sems.at[0, step - 1],
            recv_sem=near_sems.at[1, step - 1],
            device_id={"kv": (group + step) % groups},
            device_id_type=MESH,
        )

    def far_copy(step):
        other = (pack + step) % dp
        return pltpu.make_async_remote_copy(
            src_ref=total.at[other],
            dst_ref=far.at[step - 1],
            send_sem=far_sems.at[0, step - 1],
            recv_sem=far_sems.at[1, step - 1],
            device_id={"dp": other},
            device_id_type=MESH,
        )

    barrier = pltpu.get_barrier_semaphore()
    for step in range(1, dp):
        pl.semaphore_signal(
            barrier, inc=1, device_id={"dp": (pack + step) % dp}, device_id_type=MESH
        )
    for step in range(1, groups):
        pl.semaphore_signal(
            barrier, inc=1, device_id={"kv": (group + step) % groups}, device_id_type=MESH
        )
    pl.semaphore_wait(barrier, dp + groups - 2)
    for step in range(1, groups):
        near_copy(step).start()
        out_copy(step).start()
    scatter.other_chunks()
    value = gains_ref[...]
    for step in range(1, groups):
        near_copy(step).wait_recv()
        value = value + near[step - 1]
    total[...] = value
    for step in range(1, dp):
        far_copy(step).start()
    scatter.own_chunks()
    for stage in range(1, dp.bit_length() - 1):
        scatter.later(stage)
    value = total[pack]
    for step in range(1, dp):
        far_copy(step).wait_recv()
        value = value + far[step - 1]
    gains_out[...] = value
    value = output_ref[...]
    for step in range(1, groups):
        out_copy(step).wait_recv()
        value = value + out_recv[step - 1].astype(jnp.float32)
    output_out[...] = value
    for step in range(1, groups):
        near_copy(step).wait_send()
        out_copy(step).wait_send()
    for step in range(1, dp):
        far_copy(step).wait_send()
    scatter.finish()


def last_sums(lhs, rhs, gains, output, sums, head_width, groups, collective_id):
    dp, rows = lhs.shape[0], lhs.shape[1]
    columns = rhs.shape[1]
    vmem = pl.BlockSpec(memory_space=pltpu.VMEM)
    return pl.pallas_call(
        functools.partial(last_sums_kernel, dp, groups),
        out_shape=[
            jax.ShapeDtypeStruct((rows, columns - 2 * head_width), jnp.float32),
            jax.ShapeDtypeStruct((rows, head_width), jnp.float32),
            jax.ShapeDtypeStruct((rows, head_width), jnp.float32),
            jax.ShapeDtypeStruct(output.shape, jnp.float32),
            jax.ShapeDtypeStruct(gains.shape[1:], jnp.float32),
        ],
        in_specs=[vmem] * 5,
        out_specs=[vmem] * 5,
        scratch_shapes=[
            pltpu.VMEM((groups - 1,) + output.shape, jnp.bfloat16),
            pltpu.SemaphoreType.DMA((2, groups - 1)),
            pltpu.VMEM((groups - 1,) + gains.shape, jnp.float32),
            pltpu.VMEM((dp - 1,) + gains.shape[1:], jnp.float32),
            pltpu.VMEM(gains.shape, jnp.float32),
            pltpu.SemaphoreType.DMA((2, groups - 1)),
            pltpu.SemaphoreType.DMA((2, dp - 1)),
        ]
        + scatter_scratch(dp, rows, columns),
        compiler_params=pltpu.CompilerParams(
            collective_id=collective_id, has_side_effects=True, vmem_limit_bytes=VMEM_LIMIT
        ),
        cost_estimate=pl.CostEstimate(
            flops=2 * lhs.size * columns, bytes_accessed=2 * lhs.size, transcendentals=0
        ),
    )(lhs, rhs, gains, output, sums)


def row_chunks(matrix, count):
    chunks = matrix.reshape(count, matrix.shape[0] // count, matrix.shape[1])
    return jnp.pad(chunks, ((0, 0), (0, -chunks.shape[1] % 16), (0, 0)))


def per_device(
    tokens_in,
    attn_gain,
    w_query,
    w_key,
    w_value,
    w_output,
    mlp_gain,
    w_gate,
    w_up,
    w_down,
    counts,
    segments,
    cotangent,
):
    row_count = tokens_in.shape[0]
    head_width = w_key.shape[1]
    pack_count, group_count = lax.axis_size("dp"), lax.axis_size("kv")
    sizes = (pack_count, group_count)
    pack = lax.axis_index("dp")
    share = w_query.shape[0] // pack_count
    w_pair = jnp.concatenate([w_key, w_value], axis=1)

    def own_share(matrix):
        return lax.dynamic_slice_in_dim(matrix, pack * share, share, 0)

    out_part = lax.dynamic_slice_in_dim(w_output[0], pack * share, share, 1).T
    qkv_part = jnp.concatenate([own_share(w_query), own_share(w_pair)], axis=1)
    live_rows = (jnp.arange(row_count) < counts[0]).astype(jnp.float32)[:, None]
    (
        attn_out,
        act_flipped,
        query,
        key,
        value,
        logsums,
        cosine,
        sine_a,
        sine_b,
        cosine_t,
        sine_t,
        out_parts,
    ) = attention(tokens_in, attn_gain[None], w_query, w_pair, segments, out_part, group_count, 5)
    (
        second_flipped,
        hidden_flipped,
        grad_gate,
        grad_up,
        grad_act_two,
        feed_early,
        feed_late,
        resid_mine,
        attn_others,
        out_others,
    ) = feed_forward(
        attn_out,
        out_parts,
        w_output[0],
        w_gate,
        w_up,
        w_down[0],
        cotangent,
        live_rows,
        tokens_in,
        mlp_gain[None],
        sizes,
        1,
    )
    second_chunks = row_chunks(second_flipped, pack_count)
    sent_gate, sent_up, sent_down, qkv_parts = product_scatter(
        [
            (second_chunks, grad_gate),
            (second_chunks, grad_up),
            (row_chunks(hidden_flipped, pack_count), cotangent),
        ],
        qkv_part,
        group_count,
        2,
    )
    grad_two_mine = lax.psum_scatter(grad_act_two, "kv", scatter_dimension=0, tiled=True)
    grad_two_mine, feed_early, qkv_parts = lax.optimization_barrier(
        (grad_two_mine, feed_early, qkv_parts)
    )
    grad_tokens, gain_rows, own_output, output_sums, grad_qkv, _ = attention_back(
        (
            grad_two_mine,
            resid_mine,
            cotangent,
            live_rows,
            tokens_in,
            attn_gain[None],
            mlp_gain[None],
            w_output[0],
            out_others.reshape(group_count - 1, -1, w_output.shape[1]),
            attn_others,
            query,
            key,
            value,
            logsums,
            attn_out,
            segments[:, None],
            segments[None],
            cosine_t,
            sine_t,
            cosine,
            sine_a,
            sine_b,
            w_query,
            w_pair,
            qkv_parts,
        ),
        sizes,
        head_width,
        3,
    )
    early_sum = lax.psum_scatter(feed_early, "kv", scatter_dimension=0, tiled=True)
    early_sum, feed_late, grad_qkv = lax.optimization_barrier((early_sum, feed_late, grad_qkv))
    sent_query, sent_key, sent_value, sent_output, gains = last_sums(
        row_chunks(act_flipped, pack_count),
        grad_qkv,
        gain_rows,
        own_output,
        output_sums,
        head_width,
        group_count,
        4,
    )
    sent_two, sent_one = gains[0], gains[1]
    sent_output = sent_output[None]
    sent_down = sent_down[: w_down.shape[1] // pack_count][None]
    late_sum = lax.psum_scatter(feed_late, "kv", scatter_dimension=0, tiled=True)
    feed_sum = jnp.concatenate([early_sum, late_sum], axis=1).astype(jnp.float32)
    layer_out = (resid_mine + feed_sum).astype(jnp.bfloat16)
    return (
        layer_out,
        grad_tokens,
        sent_one,
        sent_query,
        sent_key,
        sent_value,
        sent_output,
        sent_two,
        sent_gate,
        sent_up,
        sent_down,
    )


def solution(mesh):
    return jax.shard_map(
        per_device,
        mesh=mesh,
        in_specs=(
            P("dp", None),
            P(),
            P(None, "kv"),
            P(None, "kv"),
            P(None, "kv"),
            P("kv", None, None),
            P(),
            P(None, "kv"),
            P(None, "kv"),
            P("kv", None, None),
            P("dp"),
            P("dp"),
            P("dp", None),
        ),
        out_specs=(
            P(("dp", "kv"), None),
            P(("dp", "kv"), None),
            P("dp"),
            P("dp", "kv"),
            P("dp", "kv"),
            P("dp", "kv"),
            P("kv", "dp", None),
            P("dp"),
            P("dp", "kv"),
            P("dp", "kv"),
            P("kv", "dp", None),
        ),
        check_vma=False,
    )
```

```python
import functools

import jax
import jax.numpy as jnp
from jax import lax
from jax.experimental import pallas as pl
from jax.experimental.pallas import tpu as pltpu
from jax.sharding import PartitionSpec as P

EPS = 1e-05
LOG2E = 1.4426950408889634
MESH = pl.DeviceIdType.MESH
VMEM_LIMIT = 60 * 1024 * 1024


def row_halves(rows):
    upper = -(-rows // 32) * 16
    return ((0, upper), (upper, rows - upper))


def times(first, second):
    return jnp.dot(first, second, preferred_element_type=jnp.float32)


def times_t(first, second):
    return lax.dot_general(
        first, second, (((1,), (1,)), ((), ())), preferred_element_type=jnp.float32
    )


def to_group(step, groups, source, target, sems):
    return pltpu.make_async_remote_copy(
        src_ref=source,
        dst_ref=target,
        send_sem=sems.at[0, step - 1],
        recv_sem=sems.at[1, step - 1],
        device_id={"kv": (lax.axis_index("kv") + step) % groups},
        device_id_type=MESH,
    )


class Spread:
    def __init__(self, buffer, send_sem, recv_sem, dp):
        self.buffer, self.send_sem, self.recv_sem = buffer, send_sem, recv_sem
        self.me = lax.axis_index("dp")
        self.bits = dp.bit_length() - 1
        rows = buffer.shape[2]
        self.halves = row_halves(rows)

    def flipped(self, places):
        device = self.me
        for place in places:
            device = device + 2**place * (1 - 2 * ((self.me // 2**place) % 2))
        return device

    def copies(self, stage, arriving):
        result = []
        for half in range(2):
            order = list(range(1, self.bits))
            order = (order if half == 0 else order[::-1]) + [0]
            for subset in range(2**stage):
                places = [order[b] for b in range(stage) if subset >> b & 1]
                if arriving:
                    places = places + [order[stage]]
                part = self.buffer.at[:, self.flipped(places), pl.ds(*self.halves[half])]
                number = 2**stage - 1 + subset
                result.append(
                    pltpu.make_async_remote_copy(
                        src_ref=part,
                        dst_ref=part,
                        send_sem=self.send_sem.at[half, number],
                        recv_sem=self.recv_sem.at[half, number],
                        device_id={"dp": self.flipped([order[stage]])},
                        device_id_type=MESH,
                    )
                )
        return result

    def start(self, stage):
        for copy in self.copies(stage, False):
            copy.start()

    def wait_recv(self, stage):
        for copy in self.copies(stage, True):
            copy.wait_recv()

    def wait_send(self):
        for stage in range(self.bits):
            for copy in self.copies(stage, False):
                copy.wait_send()


def greet(dp, groups):
    pack, group = lax.axis_index("dp"), lax.axis_index("kv")
    bits = dp.bit_length() - 1
    barrier = pltpu.get_barrier_semaphore()
    for place in range(bits):
        other = pack + 2**place * (1 - 2 * ((pack // 2**place) % 2))
        pl.semaphore_signal(barrier, inc=1, device_id={"dp": other}, device_id_type=MESH)
    for step in range(1, groups):
        other = (group + step) % groups
        pl.semaphore_signal(barrier, inc=1, device_id={"kv": other}, device_id_type=MESH)
    pl.semaphore_wait(barrier, bits + groups - 1)


def attention_kernel(groups, head_width, *refs):
    (
        tokens_ref, gain_ref, query_w, pair_w, seg_column, seg_row, frequency, part_hbm,
        attn_out, act_out, query_out, key_out, value_out, logsum_out,
        cosine_out, sine_a_out, sine_b_out, cosine_t_out, sine_t_out, parts_out,
        query_m, value_t, part_sems,
    ) = refs
    rows = tokens_ref.shape[0] // groups
    width, span_w = query_w.shape[1], key_out.shape[1]
    heads, pair, half = span_w // head_width, 2 * head_width, head_width // 2
    scale = head_width**-0.5 * LOG2E

    def part_copy(step):
        return to_group(step, groups, part_hbm, parts_out.at[groups - 1 - step], part_sems)

    greet(1, groups)
    for step in range(1, groups):
        part_copy(step).start()
    lanes = lax.broadcasted_iota(jnp.int32, (rows, pair), 1)
    low_half = lanes % head_width < half
    head_lanes = lax.broadcasted_iota(jnp.int32, (rows, span_w), 1) // head_width

    for block in range(groups):
        part = pl.ds(block * rows, rows)
        values = tokens_ref[part].astype(jnp.float32)
        inverse = lax.rsqrt(jnp.mean(values * values, axis=1, keepdims=True) + EPS)
        act = (values * inverse * gain_ref[...]).astype(jnp.bfloat16)
        act_out[:, part] = act.T
        query_raw = times(act, query_w[...])
        pair_raw = times(act, pair_w[...])
        before = (seg_row[...] < seg_column[part]).astype(jnp.float32)
        places = (
            lax.broadcasted_iota(jnp.int32, (rows, 1), 0) + block * rows
        ).astype(jnp.float32) - jnp.sum(before, axis=1, keepdims=True)
        angles = places * frequency[...]
        cosine, sine = jnp.cos(angles), jnp.sin(angles)
        sine_a, sine_b = jnp.where(low_half, -sine, 0.0), jnp.where(low_half, 0.0, sine)
        cosine_out[part], sine_a_out[part], sine_b_out[part] = cosine, sine_a, sine_b
        cosine_t_out[:, part] = cosine.T[:half]
        sine_t_out[:, part] = sine.T[:half]

        def rotated(vectors):
            return (
                vectors * cosine
                + pltpu.roll(vectors, pair - half, 1) * sine_a
                + pltpu.roll(vectors, half, 1) * sine_b
            ).astype(jnp.bfloat16)

        for start in range(0, width, pair):
            query_out[part, pl.ds(start, pair)] = rotated(query_raw[:, start : start + pair])
        other = pltpu.roll(pair_raw, head_width, 1)
        keys_two = rotated(jnp.where(lanes < head_width, pair_raw, other))
        values_two = jnp.where(lanes < head_width, other, pair_raw)
        key_out[part] = jnp.concatenate([keys_two] * (span_w // pair), axis=1)
        value_out[part] = jnp.concatenate(
            [values_two.astype(jnp.bfloat16)] * (span_w // pair), axis=1
        )
        value_t[:, part] = values_two.T[:head_width].astype(jnp.bfloat16)
        query_seg = seg_row[:, part]
        query_place = lax.broadcasted_iota(jnp.int32, (rows, rows), 1) + block * rows

        def span(number, carry):
            columns = pl.ds(pl.multiple_of(number * span_w, span_w), span_w)
            query = query_out[part, columns]
            for head in range(heads):
                query_m[pl.ds(head * rows, rows)] = jnp.where(head_lanes == head, query, 0)

            def keys(step, carry):
                highest, total, output = carry
                piece = block - step
                key_part = pl.ds(pl.multiple_of(piece * rows, rows), rows)
                key_place = lax.broadcasted_iota(jnp.int32, (rows, rows), 0) + piece * rows
                allowed = (seg_column[key_part] == query_seg) & (key_place <= query_place)
                bias = jnp.where(allowed, 0.0, -jnp.inf)
                scores = times_t(key_out[key_part], query_m[...]) * scale
                scores = scores + jnp.concatenate([bias] * heads, axis=1)
                top = jnp.maximum(highest, jnp.max(scores, axis=0, keepdims=True))
                shrink = jnp.exp2(highest - top)
                chance = jnp.exp2(scores - top)
                total = total * shrink + jnp.sum(chance, axis=0, keepdims=True)
                output = output * shrink + times(value_t[:, key_part], chance.astype(jnp.bfloat16))
                return top, total, output

            first = (
                jnp.full((1, heads * rows), -jnp.inf, jnp.float32),
                jnp.zeros((1, heads * rows), jnp.float32),
                jnp.zeros((head_width, heads * rows), jnp.float32),
            )
            highest, total, output = lax.fori_loop(0, block + 1, keys, first)
            output = output / total
            stacked = jnp.concatenate(
                [output[:, head * rows : (head + 1) * rows] for head in range(heads)], axis=0
            )
            attn_out[part, columns] = stacked.T.astype(jnp.bfloat16)
            logsum_out[number * groups + block] = highest + jnp.log(total) * LOG2E
            return carry

        lax.fori_loop(0, width // span_w, span, 0)
    for step in range(1, groups):
        part_copy(step).wait()


def attention(tokens, gain, query_w, pair_w, segments, part, groups, collective_id):
    count, features = tokens.shape
    width, head_width = query_w.shape[1], pair_w.shape[1] // 2
    span_w = 256
    rows, heads, half = count // groups, span_w // head_width, head_width // 2
    frequency = 10000.0 ** (-(jnp.arange(half, dtype=jnp.float32) * 2.0 / head_width))
    vmem = pl.BlockSpec(memory_space=pltpu.VMEM)
    any_spec = pl.BlockSpec(memory_space=pl.ANY)
    bf16, f32 = jnp.bfloat16, jnp.float32
    return pl.pallas_call(
        functools.partial(attention_kernel, groups, head_width),
        out_shape=[
            jax.ShapeDtypeStruct((count, width), bf16),
            jax.ShapeDtypeStruct((features, count), bf16),
            jax.ShapeDtypeStruct((count, width), bf16),
            jax.ShapeDtypeStruct((count, span_w), bf16),
            jax.ShapeDtypeStruct((count, span_w), bf16),
            jax.ShapeDtypeStruct((width // span_w * groups, 1, heads * rows), f32),
            jax.ShapeDtypeStruct((count, 2 * head_width), f32),
            jax.ShapeDtypeStruct((count, 2 * head_width), f32),
            jax.ShapeDtypeStruct((count, 2 * head_width), f32),
            jax.ShapeDtypeStruct((half, count), f32),
            jax.ShapeDtypeStruct((half, count), f32),
            jax.ShapeDtypeStruct((groups - 1,) + part.shape, bf16),
        ],
        in_specs=[vmem] * 7 + [any_spec],
        out_specs=[vmem] * 11 + [any_spec],
        scratch_shapes=[
            pltpu.VMEM((heads * rows, span_w), bf16),
            pltpu.VMEM((head_width, count), bf16),
            pltpu.SemaphoreType.DMA((2, groups - 1)),
        ],
        compiler_params=pltpu.CompilerParams(
            collective_id=collective_id, has_side_effects=True, vmem_limit_bytes=VMEM_LIMIT
        ),
        cost_estimate=pl.CostEstimate(
            flops=4 * count * features * width, bytes_accessed=8 * tokens.size, transcendentals=0
        ),
    )(
        tokens,
        gain,
        query_w,
        pair_w,
        segments[:, None],
        segments[None],
        jnp.tile(frequency, 4)[None],
        part,
    )


def feed_forward_kernel(dp, groups, *refs):
    (
        attn_hbm, attn_ref, part_ref, own_hbm, gate_hbm, up_hbm, down_hbm, cot_hbm, live_hbm,
        tokens_ref, gain_ref, live_ref, pass_hbm,
        act_out, hidden_out, gate_out, up_out, back_out, feed_a_out, feed_b_out, resid_out, rows_out, all_out, pass_out,
        attn_in, all_ref, own_ref, w_gate, w_up, w_down, cot_ref, live_all, grad_hidden, resid_ref,
        load_sem, send_sem, recv_sem, spread_send, spread_recv, out_sem, pass_sems,
    ) = refs
    block = pl.program_id(0)
    blocks = groups
    group = lax.axis_index("kv")
    pack = lax.axis_index("dp")
    rows = tokens_ref.shape[0]
    others = groups - 1
    spread = Spread(all_ref, spread_send, spread_recv, dp)
    stages = dp.bit_length() - 1
    loads = [
        pltpu.make_async_copy(source, target, load_sem.at[index])
        for index, (source, target) in enumerate(
            (
                (down_hbm, w_down),
                (cot_hbm, cot_ref),
                (live_hbm, live_all),
                (own_hbm, own_ref),
                (gate_hbm, w_gate),
                (up_hbm, w_up),
            )
        )
    ]

    def attn_copy(part, step, slot, source, place):
        span = pl.ds(part * rows, rows)
        return pltpu.make_async_remote_copy(
            src_ref=source.at[span],
            dst_ref=attn_in.at[slot, span],
            send_sem=send_sem.at[part, place],
            recv_sem=recv_sem.at[part, slot],
            device_id={"kv": (group + step) % groups},
            device_id_type=MESH,
        )

    def pass_copy(step):
        return to_group(step, groups, pass_hbm, pass_out.at[others - step], pass_sems)

    line = groups == 4
    inner = (group == 1) | (group == 2)
    direct = (1, 3) if line else tuple(range(1, groups))
    relays = ((0, 3, 1), (2, 1, others)) if line else ()

    def own_copy(part, step):
        return attn_copy(part, step, others - step, attn_hbm, step - 1)

    def send_rows(part):
        for step in direct:
            own_copy(part, step).start()

    def wait_rows(part, slot):
        attn_copy(part, 1, slot, attn_hbm, 0).wait_recv()

    def pass_on(part):
        if line:

            @pl.when(inner)
            def _():
                for slot, step, place in relays:
                    wait_rows(part, slot)
                    attn_copy(part, step, 1, attn_in.at[slot], place).start()

    def wait_block(part):
        for slot in range(others):
            if line and slot != 1:

                @pl.when(jnp.logical_not(inner))
                def _():
                    wait_rows(part, slot)
            else:
                wait_rows(part, slot)

    def hidden_gradient(part):
        span = pl.ds(part * rows, rows)
        masked = (cot_ref[span].astype(jnp.float32) * live_all[span]).astype(jnp.bfloat16)
        grad_hidden[span] = times_t(masked, w_down[...]).astype(jnp.bfloat16)

    @pl.when(block == 0)
    def _():
        for load in loads:
            load.start()
        all_ref[:, pack] = part_ref[...]
        greet(dp, groups)
        send_rows(0)
        spread.start(0)
        for part in range(1, blocks):
            send_rows(part)
        for load in loads[:3]:
            load.wait()
        for stage in range(stages):
            if stage < blocks:
                hidden_gradient(stage)
            spread.wait_recv(stage)
            if stage + 1 < stages:
                spread.start(stage + 1)
            if stage < blocks - 1:
                pass_on(stage)
        for part in range(stages, blocks):
            hidden_gradient(part)
        for load in loads[3:]:
            load.wait()

    wait_block(block)
    span = pl.ds(pl.multiple_of(block * rows, rows), rows)
    width = own_ref.shape[0]
    total = tokens_ref[...].astype(jnp.float32) + times(attn_ref[...], own_ref[...])
    for slot in range(others):
        total = total + times_t(attn_in[slot, span], all_ref[slot].reshape(-1, width))
    resid_ref[...] = total
    inverse = lax.rsqrt(jnp.mean(total * total, axis=1, keepdims=True) + EPS)
    act = (total * inverse * gain_ref[...]).astype(jnp.bfloat16)
    act_out[...] = act.T
    gate = times(act, w_gate[...])
    up = times(act, w_up[...])
    chance = jax.nn.sigmoid(gate)
    swish = gate * chance
    hidden = swish * up
    feed = times(hidden.astype(jnp.bfloat16), w_down[...]).astype(jnp.bfloat16)
    feed_a_out[...] = feed[:, : feed_a_out.shape[1]]
    feed_b_out[...] = feed[:, feed_a_out.shape[1] :]
    hidden_out[...] = (hidden * live_ref[...]).astype(jnp.bfloat16).T
    grad = grad_hidden[span].astype(jnp.float32)
    gate_b = (grad * up * chance * (1.0 + gate * (1.0 - chance))).astype(jnp.bfloat16)
    up_b = (grad * swish).astype(jnp.bfloat16)
    gate_out[...] = gate_b
    up_out[...] = up_b
    back_out[...] = (times_t(gate_b, w_gate[...]) + times_t(up_b, w_up[...])).astype(jnp.bfloat16)

    @pl.when(block == group)
    def _():
        copy = pltpu.make_async_copy(resid_ref, resid_out, out_sem.at[0])
        copy.start()
        copy.wait()

    @pl.when(block == 0)
    def _():
        for part in range(min(stages, blocks - 1), blocks):
            pass_on(part)
        for step in range(1, groups):
            pass_copy(step).start()

    @pl.when(block == blocks - 1)
    def _():
        mine = pl.ds(pl.multiple_of(group * rows, rows), rows)
        copies = [
            pltpu.make_async_copy(attn_in.at[:, mine], rows_out, out_sem.at[1]),
            pltpu.make_async_copy(all_ref, all_out, out_sem.at[2]),
        ]
        for copy in copies:
            copy.start()
        for part in range(blocks):
            for step in direct:
                own_copy(part, step).wait_send()
        if line:

            @pl.when(inner)
            def _():
                for part in range(blocks):
                    for slot, step, place in relays:
                        attn_copy(part, step, 1, attn_in.at[slot], place).wait_send()

        spread.wait_send()
        for step in range(1, groups):
            pass_copy(step).wait()
        for copy in copies:
            copy.wait()


def feed_forward(attn, part, w_own, w_gate, w_up, w_down, cotangent, live, tokens, gain, passed, sizes, collective_id):
    dp, groups = sizes
    count, features = tokens.shape
    rows = count // groups
    width, hidden = w_own.shape[0], w_gate.shape[1]
    share = part.shape[1]
    others = groups - 1
    early = 5 * features // 8
    any_spec = pl.BlockSpec(memory_space=pl.ANY)
    by_row = lambda columns: pl.BlockSpec((rows, columns), lambda i: (i, 0))
    by_column = lambda height: pl.BlockSpec((height, rows), lambda i: (0, i))
    flops = 2 * count * features * (groups * width + 6 * hidden)
    return pl.pallas_call(
        functools.partial(feed_forward_kernel, dp, groups),
        grid=(groups,),
        out_shape=[
            jax.ShapeDtypeStruct((features, count), jnp.bfloat16),
            jax.ShapeDtypeStruct((hidden, count), jnp.bfloat16),
            jax.ShapeDtypeStruct((count, hidden), jnp.bfloat16),
            jax.ShapeDtypeStruct((count, hidden), jnp.bfloat16),
            jax.ShapeDtypeStruct((count, features), jnp.bfloat16),
            jax.ShapeDtypeStruct((count, early), jnp.bfloat16),
            jax.ShapeDtypeStruct((count, features - early), jnp.bfloat16),
            jax.ShapeDtypeStruct((rows, features), jnp.float32),
            jax.ShapeDtypeStruct((others, rows, width), jnp.bfloat16),
            jax.ShapeDtypeStruct((others, dp, share, width), jnp.bfloat16),
            jax.ShapeDtypeStruct((others,) + passed.shape, jnp.bfloat16),
        ],
        in_specs=[
            any_spec,
            by_row(width),
            pl.BlockSpec(memory_space=pltpu.VMEM),
            any_spec, any_spec, any_spec, any_spec, any_spec, any_spec,
            by_row(features),
            pl.BlockSpec(memory_space=pltpu.VMEM),
            by_row(1),
            any_spec,
        ],
        out_specs=[
            by_column(features), by_column(hidden), by_row(hidden), by_row(hidden),
            by_row(features), by_row(early), by_row(features - early), any_spec, any_spec, any_spec, any_spec,
        ],
        scratch_shapes=[
            pltpu.VMEM((others, count, width), jnp.bfloat16),
            pltpu.VMEM((others, dp, share, width), jnp.bfloat16),
            pltpu.VMEM((width, features), jnp.bfloat16),
            pltpu.VMEM((features, hidden), jnp.bfloat16),
            pltpu.VMEM((features, hidden), jnp.bfloat16),
            pltpu.VMEM((hidden, features), jnp.bfloat16),
            pltpu.VMEM((count, features), jnp.bfloat16),
            pltpu.VMEM((count, 1), jnp.float32),
            pltpu.VMEM((count, hidden), jnp.bfloat16),
            pltpu.VMEM((rows, features), jnp.float32),
            pltpu.SemaphoreType.DMA((6,)),
            pltpu.SemaphoreType.DMA((groups, groups)),
            pltpu.SemaphoreType.DMA((groups, others)),
            pltpu.SemaphoreType.DMA((2, dp - 1)),
            pltpu.SemaphoreType.DMA((2, dp - 1)),
            pltpu.SemaphoreType.DMA((3,)),
            pltpu.SemaphoreType.DMA((2, groups - 1)),
        ],
        compiler_params=pltpu.CompilerParams(
            collective_id=collective_id, has_side_effects=True, vmem_limit_bytes=VMEM_LIMIT
        ),
        cost_estimate=pl.CostEstimate(flops=flops, bytes_accessed=40 * count * features, transcendentals=0),
    )(attn, attn, part, w_own, w_gate, w_up, w_down, cotangent, live, tokens, gain, live, passed)


class Scatter:
    def __init__(self, dp, product, store, sent, held, late, sems):
        self.product, self.store, self.sent, self.held, self.late = product, store, sent, held, late
        self.first_send, self.first_recv, self.late_send, self.late_recv = sems
        self.me = lax.axis_index("dp")
        self.upper = self.me // 2
        self.bits = dp.bit_length() - 1
        self.slots = dp // 2
        self.halves = row_halves(held.shape[1])

    def bit(self, place):
        return (self.me // 2**place) % 2

    def partner(self, place):
        return self.me + 2**place * (1 - 2 * self.bit(place))

    def first_copy(self, t):
        return pltpu.make_async_remote_copy(
            src_ref=self.sent.at[t],
            dst_ref=self.held.at[t],
            send_sem=self.first_send.at[t],
            recv_sem=self.first_recv.at[t],
            device_id={"dp": self.partner(0)},
            device_id_type=MESH,
        )

    def stage_bit(self, half, stage):
        return stage - 1 if half == 0 else self.bits - 1 - stage

    def slot_of(self, half, stage, index, value):
        if half == 0:
            low = 2 ** (stage - 1)
            return index * 2**stage + value * low + self.upper % low
        top = 2 ** (self.bits - stage)
        return index + value * (top // 2) + (self.upper // top) * top

    def late_copy(self, half, stage, index, slot):
        start, size = self.halves[half]
        buffer = self.slots - 2 ** (self.bits - stage) + index
        return pltpu.make_async_remote_copy(
            src_ref=self.held.at[slot, pl.ds(start, size)],
            dst_ref=self.late[half].at[buffer],
            send_sem=self.late_send.at[half, buffer],
            recv_sem=self.late_recv.at[half, buffer],
            device_id={"dp": self.partner(self.stage_bit(half, stage) + 1)},
            device_id_type=MESH,
        )

    def other_chunks(self):
        def step(t, carry):
            self.sent[t] = self.product(2 * t + 1 - self.bit(0)).astype(jnp.bfloat16)
            self.first_copy(t).start()
            return carry

        lax.fori_loop(0, self.slots, step, 0)

    def own_chunks(self):
        def step(e, carry):
            t = 0
            for place in range(self.bits - 1):
                t = t + 2**place * ((e // 2**place + 1 + self.upper // 2**place) % 2)
            own = self.product(2 * t + self.bit(0))
            self.first_copy(t).wait_recv()
            self.held[t] = (self.held[t].astype(jnp.float32) + own).astype(jnp.bfloat16)

            @pl.when(e % 2 == 0)
            def _():
                self.late_copy(0, 1, t // 2, t).start()

            @pl.when(e < self.slots // 2)
            def _():
                self.late_copy(1, 1, t % (self.slots // 2), t).start()

            return carry

        lax.fori_loop(0, self.slots, step, 0)

    def later(self, stage):
        for half in range(2):
            start, size = self.halves[half]
            keep_bit = self.bit(self.stage_bit(half, stage) + 1)
            for index in range(2 ** (self.bits - 1 - stage)):
                slot = self.slot_of(half, stage, index, keep_bit)
                self.late_copy(half, stage, index, slot).wait_recv()
                buffer = self.slots - 2 ** (self.bits - stage) + index
                total = self.held[slot, pl.ds(start, size)].astype(jnp.float32) + self.late[half][
                    buffer
                ].astype(jnp.float32)
                if stage == self.bits - 1:
                    self.store(start, size, total)
                else:
                    self.held[slot, pl.ds(start, size)] = total.astype(jnp.bfloat16)
            if stage < self.bits - 1:
                follow = self.stage_bit(half, stage + 1) + 1
                for index in range(2 ** (self.bits - 2 - stage)):
                    slot = self.slot_of(half, stage + 1, index, 1 - self.bit(follow))
                    self.late_copy(half, stage + 1, index, slot).start()

    def finish(self):
        for t in range(self.slots):
            self.first_copy(t).wait_send()
        for half in range(2):
            for stage in range(1, self.bits):
                for index in range(2 ** (self.bits - 1 - stage)):
                    self.late_copy(half, stage, index, 0).wait_send()


def scatter_scratch(dp, rows, columns):
    slots = dp // 2
    return (
        [pltpu.VMEM((slots, rows, columns), jnp.bfloat16)] * 2
        + [pltpu.VMEM((slots - 1, size, columns), jnp.bfloat16) for _, size in row_halves(rows)]
        + [pltpu.SemaphoreType.DMA((slots,))] * 2
        + [pltpu.SemaphoreType.DMA((2, slots - 1))] * 2
    )


def scatter_from(dp, product, store, refs):
    return Scatter(dp, product, store, refs[0], refs[1], refs[2:4], refs[4:8])


def product_scatter_kernel(count, dp, *refs):
    lhs, rhs = refs[:count], refs[count : 2 * count]
    outs, scratch = refs[2 * count : 3 * count], refs[3 * count :]

    def member(a):
        def product(chunk):
            return times(lhs[a][chunk], rhs[a][...])

        def store(start, size, total):
            outs[a][pl.ds(start, size)] = total

        return scatter_from(dp, product, store, scratch[8 * a : 8 * a + 8])

    members = [member(a) for a in range(count)]
    stages = dp.bit_length() - 1
    greet(dp, 1)
    pending = []
    for a in range(count):
        members[a].other_chunks()
        members[a].own_chunks()
        pending.append((a, 1))
        if a > 0:
            done, stage = pending.pop(0)
            members[done].later(stage)
            if stage < stages - 1:
                pending.append((done, stage + 1))
    while pending:
        done, stage = pending.pop(0)
        members[done].later(stage)
        if stage < stages - 1:
            pending.append((done, stage + 1))
    for one in members:
        one.finish()


def product_scatter(pairs, collective_id):
    count = len(pairs)
    dp = pairs[0][0].shape[0]
    dims = [(lhs.shape[1], rhs.shape[1]) for lhs, rhs in pairs]
    flops = sum(2 * lhs.size * rhs.shape[1] for lhs, rhs in pairs)
    moved = sum(2 * (lhs.size + rhs.size) for lhs, rhs in pairs)
    vmem = pl.BlockSpec(memory_space=pltpu.VMEM)
    any_spec = pl.BlockSpec(memory_space=pl.ANY)
    return pl.pallas_call(
        functools.partial(product_scatter_kernel, count, dp),
        out_shape=[jax.ShapeDtypeStruct(dim, jnp.float32) for dim in dims],
        in_specs=[vmem] * (2 * count),
        out_specs=[vmem] * count,
        scratch_shapes=sum([scatter_scratch(dp, *dim) for dim in dims], []),
        compiler_params=pltpu.CompilerParams(
            collective_id=collective_id, has_side_effects=True, vmem_limit_bytes=VMEM_LIMIT
        ),
        cost_estimate=pl.CostEstimate(flops=flops * 3, bytes_accessed=moved, transcendentals=0),
    )(*[lhs for lhs, _ in pairs], *[rhs for _, rhs in pairs])


def norm_back(values, gain, grads):
    inverse = lax.rsqrt(jnp.mean(values * values, axis=1, keepdims=True) + EPS)
    scaled = gain * grads
    mean = jnp.mean(scaled * values, axis=1, keepdims=True)
    by_values = inverse * scaled - values * (inverse * inverse * inverse * mean)
    return by_values, jnp.sum(grads * values * inverse, axis=0, keepdims=True)


def attention_back_kernel(dp, groups, head_width, *refs):
    (
        back_ref, resid_hbm, cot_hbm, live_ref, tokens_hbm, attn_gain, mlp_gain,
        out_own, out_others, rows_ref, query_ref, key_ref, value_ref, logsum_ref, attn_ref,
        seg_column, seg_row, cosine_t, sine_t, cosine, sine_a, sine_b, qkv_own, pair_own, qkv_parts,
        tokens_out, gains_out, output_out, out_send, grad_out, qkv_all,
        cot_ref, tokens_ref, chunk_ref, weights, query_m, attn_m, key_t, query_t, key_sum, value_sum,
        attn_send, attn_grad, arrived, branch_ref,
        load_sem, last_sem, attn_sems, grad_sems, spread_send, spread_recv, *scatter_refs,
    ) = refs
    group, pack, others = lax.axis_index("kv"), lax.axis_index("dp"), groups - 1
    rows = branch_ref.shape[0]
    width = query_ref.shape[1]
    span_w = key_ref.shape[1]
    pair, half, heads = 2 * head_width, head_width // 2, span_w // head_width
    scale = head_width**-0.5
    mine = pl.ds(pl.multiple_of(group * rows, rows), rows)
    out_part = pl.ds(0, width)

    def load(index, source, target):
        return pltpu.make_async_copy(source, target, load_sem.at[index])

    first_loads = [
        load(0, resid_hbm, tokens_out),
        load(1, cot_hbm.at[mine], cot_ref),
        load(2, out_others, weights.at[:, :, out_part]),
        load(3, qkv_parts, qkv_all.at[:, pack]),
        load(4, tokens_hbm.at[mine], tokens_ref),
    ]
    for one in first_loads:
        one.start()

    spans = width // span_w

    def attn_copy(number, step):
        return to_group(
            step, groups, attn_send.at[number, step - 1], attn_grad.at[number, group], attn_sems.at[number]
        )

    def columns_of(number):
        start = number * span_w
        return pl.ds(start, span_w if number < spans - 1 else width + pair - start)

    def grad_copy(number, step, block):
        columns = columns_of(number)
        return to_group(
            step,
            groups,
            grad_out.at[pl.ds(block * rows, rows), columns],
            arrived.at[step - 1, :, columns],
            grad_sems.at[number],
        )

    share = output_out.shape[0]

    greet(dp, groups)
    spread = Spread(qkv_all, spread_send, spread_recv, dp)
    lanes = lax.broadcasted_iota(jnp.int32, (rows, span_w), 1) // head_width
    first_loads[3].wait()
    spread.start(0)
    first_loads[0].wait()
    first_loads[1].wait()
    values = tokens_out[...]
    grad_resid, mlp_rows = norm_back(values, mlp_gain[...], back_ref[...].astype(jnp.float32))
    grad_resid = grad_resid + cot_ref[...].astype(jnp.float32) * live_ref[mine]
    tokens_out[...] = grad_resid
    branch_ref[...] = grad_resid.astype(jnp.bfloat16)
    stages = dp.bit_length() - 1
    first_loads[2].wait()
    for number in range(spans):
        columns = pl.ds(number * span_w, span_w)
        for step in range(1, groups):
            attn_send[number, step - 1] = times(branch_ref[...], weights[step - 1, :, columns]).astype(
                jnp.bfloat16
            )
            attn_copy(number, step).start()
        attn_grad[number, group] = times_t(branch_ref[...], out_own[columns]).astype(jnp.bfloat16)

    spread.wait_recv(0)
    spread.start(1)

    def store(start, size, total):
        if start == 0:
            output_out[...] = total[:share]
        out_send[pl.ds(start, size)] = total.astype(jnp.bfloat16)

    scatter = scatter_from(dp, lambda chunk: times(chunk_ref[chunk], branch_ref[...]), store, scatter_refs)
    for place in range(groups):
        turned = (attn_ref[mine] if place == 0 else rows_ref[place - 1]).T
        chunk_ref[:, pl.ds(place * share, share)] = turned.reshape(dp, share, rows)
    scatter.other_chunks()
    scatter.own_chunks()
    for block in range(groups):
        part = pl.ds(block * rows, rows)
        key_t[:, part] = key_ref[part, pl.ds(0, pair)].T[:head_width]
    key_sum[...] = jnp.zeros_like(key_sum)
    value_sum[...] = jnp.zeros_like(value_sum)

    def attend(number, block):
        part = pl.ds(block * rows, rows)

        @pl.when(block != group)
        def _():
            step = (group - block + groups) % groups
            landed = attn_grad.at[number, block]
            to_group(step, groups, landed, landed, attn_sems.at[number]).wait_recv()

        query_seg = seg_row[:, part]
        query_place = lax.broadcasted_iota(jnp.int32, (rows, rows), 1) + block * rows

        def wide(entries):
            return jnp.concatenate([entries] * heads, axis=1)

        if True:
            columns = pl.ds(number * span_w, span_w)
            query = query_ref[part, columns]
            grad = attn_grad[number, block]
            weighed = (grad.astype(jnp.float32) * attn_ref[part, columns].astype(jnp.float32)).T
            centres = jnp.sum(weighed.reshape(heads, head_width, rows), axis=1)
            centre = jnp.concatenate([centres[head : head + 1] for head in range(heads)], axis=1)
            logsum = logsum_ref[number * groups + block]
            for head in range(heads):
                place = pl.ds(head * rows, rows)
                query_m[place] = jnp.where(lanes == head, query, 0)
                attn_m[place] = jnp.where(lanes == head, grad, 0)
            query_t[...] = jnp.zeros_like(query_t)

            def keys(piece, carry):
                key_part = pl.ds(pl.multiple_of(piece * rows, rows), rows)
                key_place = lax.broadcasted_iota(jnp.int32, (rows, rows), 0) + piece * rows
                allowed = (seg_column[key_part] == query_seg) & (key_place <= query_place)
                bias = jnp.where(allowed, 0.0, -jnp.inf)
                scores = times_t(key_ref[key_part], query_m[...]) * (scale * LOG2E)
                chance = jnp.exp2(scores - logsum + wide(bias))
                probs = times_t(value_ref[key_part], attn_m[...])
                slope = (chance * (probs - centre)).astype(jnp.bfloat16)
                value_sum[key_part] += times(chance.astype(jnp.bfloat16), attn_m[...])
                key_sum[key_part] += times(slope, query_m[...])
                query_t[...] += times(key_t[:, key_part], slope)
                return carry

            lax.fori_loop(0, block + 1, keys, 0)
            cos, sin = wide(cosine_t[:, part]), wide(sine_t[:, part])
            low, high = query_t[:half] * scale, query_t[half:] * scale
            turned = jnp.concatenate([low * cos + high * sin, high * cos - low * sin], axis=0)
            stacked = jnp.concatenate(
                [turned[:, head * rows : (head + 1) * rows] for head in range(heads)], axis=0
            )
            grad_out[part, columns] = stacked.T.astype(jnp.bfloat16)

        def folded(total):
            sums = total[part, pl.ds(0, pair)]
            for step in range(1, span_w // pair):
                sums = sums + total[part, pl.ds(step * pair, pair)]
            return sums + pltpu.roll(sums, head_width, 1)

        if number == spans - 1:
            grad_k = folded(key_sum) * scale
            grad_k = (
                grad_k * cosine[part]
                - pltpu.roll(grad_k, pair - half, 1) * sine_a[part]
                - pltpu.roll(grad_k, half, 1) * sine_b[part]
            )
            first = lax.broadcasted_iota(jnp.int32, (rows, pair), 1) < head_width
            grad_out[part, pl.ds(width, pair)] = jnp.where(
                first, grad_k, folded(value_sum)
            ).astype(jnp.bfloat16)

        @pl.when(block != group)
        def _():
            grad_copy(number, (block - group + groups) % groups, block).start()

    turns = [(number, block) for number in range(spans) for block in reversed(range(groups))]
    for turn, (number, block) in enumerate(turns):
        attend(number, block)
        if turn == 3:
            for stage in range(1, stages - 1):
                spread.wait_recv(stage)
                spread.start(stage + 1)
    for stage in range(1, stages - 1):
        scatter.later(stage)
    spread.wait_recv(stages - 1)
    part_rows = qkv_all.shape[2]
    last_loads = [
        pltpu.make_async_copy(
            qkv_all.at[:, place], weights.at[:, pl.ds(place * part_rows, part_rows)], last_sem.at[place]
        )
        for place in range(dp)
    ]
    for one in last_loads:
        one.start()
    grad_act = times_t(grad_out[mine, out_part], qkv_own[...])
    grad_act = grad_act + times_t(grad_out[mine, pl.ds(width, pair)], pair_own[...])
    for one in last_loads:
        one.wait()
    for number in range(spans):
        columns = columns_of(number)
        for step in range(1, groups):
            landed = arrived.at[step - 1, :, columns]
            to_group(step, groups, landed, landed, grad_sems.at[number]).wait_recv()
            grad_act = grad_act + times_t(
                arrived[step - 1, :, columns], weights[others - step, :, columns]
            )
    first_loads[4].wait()
    by_tokens, attn_rows = norm_back(tokens_ref[...].astype(jnp.float32), attn_gain[...], grad_act)
    tokens_out[...] += by_tokens
    scatter.later(stages - 1)
    columns = gains_out.shape[2]
    for place in range(dp):
        span = slice(place * columns, (place + 1) * columns)
        gains_out[place, 0:1] = mlp_rows[:, span]
        gains_out[place, 1:2] = attn_rows[:, span]
    for step in range(1, groups):
        for number in range(spans):
            attn_copy(number, step).wait_send()
            grad_copy(number, step, 0).wait_send()
    spread.wait_send()
    scatter.finish()


def attention_back(operands, sizes, head_width, collective_id):
    dp, groups = sizes
    others_w, rows_others, query, key, parts = (operands[index] for index in (8, 9, 10, 11, 24))
    rows, width = rows_others.shape[1:]
    features = others_w.shape[1]
    count, span_w = key.shape
    share = width // dp
    stacked = (span_w // head_width) * rows
    columns = width + 2 * head_width
    vmem = pl.BlockSpec(memory_space=pltpu.VMEM)
    any_spec = pl.BlockSpec(memory_space=pl.ANY)
    bf16, f32 = jnp.bfloat16, jnp.float32
    flops = 2 * count * count * width * 10
    return pl.pallas_call(
        functools.partial(attention_back_kernel, dp, groups, head_width),
        out_shape=[
            jax.ShapeDtypeStruct((rows, features), f32),
            jax.ShapeDtypeStruct((dp, 2, features // dp), f32),
            jax.ShapeDtypeStruct((share, features), f32),
            jax.ShapeDtypeStruct((groups * share, features), bf16),
            jax.ShapeDtypeStruct((count, columns), bf16),
            jax.ShapeDtypeStruct((groups - 1, dp) + parts.shape[1:], bf16),
        ],
        in_specs=[any_spec if index in (1, 2, 4, 8, 24) else vmem for index in range(25)],
        out_specs=[vmem] * 5 + [any_spec],
        scratch_shapes=[
            pltpu.VMEM((rows, features), bf16),
            pltpu.VMEM((rows, features), bf16),
            pltpu.VMEM((dp, groups * share, rows), bf16),
            pltpu.VMEM((groups - 1, features, columns), bf16),
            pltpu.VMEM((stacked, span_w), bf16),
            pltpu.VMEM((stacked, span_w), bf16),
            pltpu.VMEM((head_width, count), bf16),
            pltpu.VMEM((head_width, stacked), f32),
            pltpu.VMEM((count, span_w), f32),
            pltpu.VMEM((count, span_w), f32),
            pltpu.VMEM((width // span_w, groups - 1, rows, span_w), bf16),
            pltpu.VMEM((width // span_w, groups, rows, span_w), bf16),
            pltpu.VMEM((groups - 1, rows, columns), bf16),
            pltpu.VMEM((rows, features), bf16),
            pltpu.SemaphoreType.DMA((5,)),
            pltpu.SemaphoreType.DMA((dp,)),
            pltpu.SemaphoreType.DMA((width // span_w, 2, groups - 1)),
            pltpu.SemaphoreType.DMA((width // span_w, 2, groups - 1)),
            pltpu.SemaphoreType.DMA((2, dp - 1)),
            pltpu.SemaphoreType.DMA((2, dp - 1)),
        ]
        + scatter_scratch(dp, groups * share, features),
        compiler_params=pltpu.CompilerParams(
            collective_id=collective_id, has_side_effects=True, vmem_limit_bytes=VMEM_LIMIT
        ),
        cost_estimate=pl.CostEstimate(flops=flops, bytes_accessed=40 * 2**20, transcendentals=0),
    )(*operands)


def last_sums_kernel(dp, groups, lhs_ref, rhs_ref, gains_ref, output_ref, sums_ref, query_out, key_out, value_out, output_out, gains_out, out_recv, out_sems, near, far, total, near_sems, far_sems, *scatter_refs):
    pack, group = lax.axis_index("dp"), lax.axis_index("kv")

    def store(start, size, value):
        span, width, head_width = pl.ds(start, size), query_out.shape[1], key_out.shape[1]
        query_out[span] = value[:, :width]
        key_out[span] = value[:, width : width + head_width]
        value_out[span] = value[:, width + head_width :]

    scatter = scatter_from(dp, lambda chunk: times(lhs_ref[chunk], rhs_ref[...]), store, scatter_refs)

    share = output_out.shape[0]

    def out_copy(step):
        source = sums_ref.at[pl.ds(step * share, share)]
        return to_group(step, groups, source, out_recv.at[step - 1], out_sems)

    def near_copy(step):
        return pltpu.make_async_remote_copy(
            src_ref=gains_ref,
            dst_ref=near.at[step - 1],
            send_sem=near_sems.at[0, step - 1],
            recv_sem=near_sems.at[1, step - 1],
            device_id={"kv": (group + step) % groups},
            device_id_type=MESH,
        )

    def far_copy(step):
        other = (pack + step) % dp
        return pltpu.make_async_remote_copy(
            src_ref=total.at[other],
            dst_ref=far.at[step - 1],
            send_sem=far_sems.at[0, step - 1],
            recv_sem=far_sems.at[1, step - 1],
            device_id={"dp": other},
            device_id_type=MESH,
        )

    barrier = pltpu.get_barrier_semaphore()
    for step in range(1, dp):
        pl.semaphore_signal(
            barrier, inc=1, device_id={"dp": (pack + step) % dp}, device_id_type=MESH
        )
    for step in range(1, groups):
        pl.semaphore_signal(
            barrier, inc=1, device_id={"kv": (group + step) % groups}, device_id_type=MESH
        )
    pl.semaphore_wait(barrier, dp + groups - 2)
    for step in range(1, groups):
        near_copy(step).start()
        out_copy(step).start()
    scatter.other_chunks()
    value = gains_ref[...]
    for step in range(1, groups):
        near_copy(step).wait_recv()
        value = value + near[step - 1]
    total[...] = value
    for step in range(1, dp):
        far_copy(step).start()
    scatter.own_chunks()
    for stage in range(1, dp.bit_length() - 1):
        scatter.later(stage)
    value = total[pack]
    for step in range(1, dp):
        far_copy(step).wait_recv()
        value = value + far[step - 1]
    gains_out[...] = value
    value = output_ref[...]
    for step in range(1, groups):
        out_copy(step).wait_recv()
        value = value + out_recv[step - 1].astype(jnp.float32)
    output_out[...] = value
    for step in range(1, groups):
        near_copy(step).wait_send()
        out_copy(step).wait_send()
    for step in range(1, dp):
        far_copy(step).wait_send()
    scatter.finish()


def last_sums(lhs, rhs, gains, output, sums, head_width, groups, collective_id):
    dp, rows = lhs.shape[0], lhs.shape[1]
    columns = rhs.shape[1]
    vmem = pl.BlockSpec(memory_space=pltpu.VMEM)
    return pl.pallas_call(
        functools.partial(last_sums_kernel, dp, groups),
        out_shape=[
            jax.ShapeDtypeStruct((rows, columns - 2 * head_width), jnp.float32),
            jax.ShapeDtypeStruct((rows, head_width), jnp.float32),
            jax.ShapeDtypeStruct((rows, head_width), jnp.float32),
            jax.ShapeDtypeStruct(output.shape, jnp.float32),
            jax.ShapeDtypeStruct(gains.shape[1:], jnp.float32),
        ],
        in_specs=[vmem] * 5,
        out_specs=[vmem] * 5,
        scratch_shapes=[
            pltpu.VMEM((groups - 1,) + output.shape, jnp.bfloat16),
            pltpu.SemaphoreType.DMA((2, groups - 1)),
            pltpu.VMEM((groups - 1,) + gains.shape, jnp.float32),
            pltpu.VMEM((dp - 1,) + gains.shape[1:], jnp.float32),
            pltpu.VMEM(gains.shape, jnp.float32),
            pltpu.SemaphoreType.DMA((2, groups - 1)),
            pltpu.SemaphoreType.DMA((2, dp - 1)),
        ]
        + scatter_scratch(dp, rows, columns),
        compiler_params=pltpu.CompilerParams(
            collective_id=collective_id, has_side_effects=True, vmem_limit_bytes=VMEM_LIMIT
        ),
        cost_estimate=pl.CostEstimate(
            flops=2 * lhs.size * columns, bytes_accessed=2 * lhs.size, transcendentals=0
        ),
    )(lhs, rhs, gains, output, sums)


def row_chunks(matrix, count):
    chunks = matrix.reshape(count, matrix.shape[0] // count, matrix.shape[1])
    return jnp.pad(chunks, ((0, 0), (0, -chunks.shape[1] % 16), (0, 0)))


def per_device(
    tokens_in,
    attn_gain,
    w_query,
    w_key,
    w_value,
    w_output,
    mlp_gain,
    w_gate,
    w_up,
    w_down,
    counts,
    segments,
    cotangent,
):
    row_count = tokens_in.shape[0]
    head_width = w_key.shape[1]
    pack_count, group_count = lax.axis_size("dp"), lax.axis_size("kv")
    sizes = (pack_count, group_count)
    pack = lax.axis_index("dp")
    share = w_query.shape[0] // pack_count
    w_pair = jnp.concatenate([w_key, w_value], axis=1)

    def own_share(matrix):
        return lax.dynamic_slice_in_dim(matrix, pack * share, share, 0)

    out_part = lax.dynamic_slice_in_dim(w_output[0], pack * share, share, 1).T
    qkv_part = jnp.concatenate([own_share(w_query), own_share(w_pair)], axis=1)
    live_rows = (jnp.arange(row_count) < counts[0]).astype(jnp.float32)[:, None]
    (
        attn_out,
        act_flipped,
        query,
        key,
        value,
        logsums,
        cosine,
        sine_a,
        sine_b,
        cosine_t,
        sine_t,
        out_parts,
    ) = attention(tokens_in, attn_gain[None], w_query, w_pair, segments, out_part, group_count, 5)
    (
        second_flipped,
        hidden_flipped,
        grad_gate,
        grad_up,
        grad_act_two,
        feed_early,
        feed_late,
        resid_mine,
        attn_others,
        out_others,
        qkv_parts,
    ) = feed_forward(
        attn_out,
        out_parts,
        w_output[0],
        w_gate,
        w_up,
        w_down[0],
        cotangent,
        live_rows,
        tokens_in,
        mlp_gain[None],
        qkv_part,
        sizes,
        1,
    )
    second_chunks = row_chunks(second_flipped, pack_count)
    sent_gate, sent_up, sent_down = product_scatter(
        [
            (second_chunks, grad_gate),
            (second_chunks, grad_up),
            (row_chunks(hidden_flipped, pack_count), cotangent),
        ],
        2,
    )
    grad_two_mine = lax.psum_scatter(grad_act_two, "kv", scatter_dimension=0, tiled=True)
    grad_two_mine, feed_early, sent_down = lax.optimization_barrier(
        (grad_two_mine, feed_early, sent_down)
    )
    grad_tokens, gain_rows, own_output, output_sums, grad_qkv, _ = attention_back(
        (
            grad_two_mine,
            resid_mine,
            cotangent,
            live_rows,
            tokens_in,
            attn_gain[None],
            mlp_gain[None],
            w_output[0],
            out_others.reshape(group_count - 1, -1, w_output.shape[1]),
            attn_others,
            query,
            key,
            value,
            logsums,
            attn_out,
            segments[:, None],
            segments[None],
            cosine_t,
            sine_t,
            cosine,
            sine_a,
            sine_b,
            w_query,
            w_pair,
            qkv_parts,
        ),
        sizes,
        head_width,
        3,
    )
    early_sum = lax.psum_scatter(feed_early, "kv", scatter_dimension=0, tiled=True)
    early_sum, feed_late, grad_qkv = lax.optimization_barrier((early_sum, feed_late, grad_qkv))
    sent_query, sent_key, sent_value, sent_output, gains = last_sums(
        row_chunks(act_flipped, pack_count),
        grad_qkv,
        gain_rows,
        own_output,
        output_sums,
        head_width,
        group_count,
        4,
    )
    sent_two, sent_one = gains[0], gains[1]
    sent_output = sent_output[None]
    sent_down = sent_down[: w_down.shape[1] // pack_count][None]
    late_sum = lax.psum_scatter(feed_late, "kv", scatter_dimension=0, tiled=True)
    feed_sum = jnp.concatenate([early_sum, late_sum], axis=1).astype(jnp.float32)
    layer_out = (resid_mine + feed_sum).astype(jnp.bfloat16)
    return (
        layer_out,
        grad_tokens,
        sent_one,
        sent_query,
        sent_key,
        sent_value,
        sent_output,
        sent_two,
        sent_gate,
        sent_up,
        sent_down,
    )


def solution(mesh):
    return jax.shard_map(
        per_device,
        mesh=mesh,
        in_specs=(
            P("dp", None),
            P(),
            P(None, "kv"),
            P(None, "kv"),
            P(None, "kv"),
            P("kv", None, None),
            P(),
            P(None, "kv"),
            P(None, "kv"),
            P("kv", None, None),
            P("dp"),
            P("dp"),
            P("dp", None),
        ),
        out_specs=(
            P(("dp", "kv"), None),
            P(("dp", "kv"), None),
            P("dp"),
            P("dp", "kv"),
            P("dp", "kv"),
            P("dp", "kv"),
            P("kv", "dp", None),
            P("dp"),
            P("dp", "kv"),
            P("dp", "kv"),
            P("kv", "dp", None),
        ),
        check_vma=False,
    )
```

```python
import functools

import jax
import jax.numpy as jnp
from jax import lax
from jax.experimental import pallas as pl
from jax.experimental.pallas import tpu as pltpu
from jax.sharding import PartitionSpec as P

EPS = 1e-05
LOG2E = 1.4426950408889634
MESH = pl.DeviceIdType.MESH
VMEM_LIMIT = 60 * 1024 * 1024


def row_halves(rows):
    upper = -(-rows // 32) * 16
    return ((0, upper), (upper, rows - upper))


def times(first, second):
    return jnp.dot(first, second, preferred_element_type=jnp.float32)


def times_t(first, second):
    return lax.dot_general(
        first, second, (((1,), (1,)), ((), ())), preferred_element_type=jnp.float32
    )


def to_group(step, groups, source, target, sems):
    return pltpu.make_async_remote_copy(
        src_ref=source,
        dst_ref=target,
        send_sem=sems.at[0, step - 1],
        recv_sem=sems.at[1, step - 1],
        device_id={"kv": (lax.axis_index("kv") + step) % groups},
        device_id_type=MESH,
    )


class Spread:
    def __init__(self, buffer, send_sem, recv_sem, dp):
        self.buffer, self.send_sem, self.recv_sem = buffer, send_sem, recv_sem
        self.me = lax.axis_index("dp")
        self.bits = dp.bit_length() - 1
        rows = buffer.shape[2]
        self.halves = row_halves(rows)

    def flipped(self, places):
        device = self.me
        for place in places:
            device = device + 2**place * (1 - 2 * ((self.me // 2**place) % 2))
        return device

    def copies(self, stage, arriving):
        result = []
        for half in range(2):
            order = list(range(1, self.bits))
            order = (order if half == 0 else order[::-1]) + [0]
            for subset in range(2**stage):
                places = [order[b] for b in range(stage) if subset >> b & 1]
                if arriving:
                    places = places + [order[stage]]
                part = self.buffer.at[:, self.flipped(places), pl.ds(*self.halves[half])]
                number = 2**stage - 1 + subset
                result.append(
                    pltpu.make_async_remote_copy(
                        src_ref=part,
                        dst_ref=part,
                        send_sem=self.send_sem.at[half, number],
                        recv_sem=self.recv_sem.at[half, number],
                        device_id={"dp": self.flipped([order[stage]])},
                        device_id_type=MESH,
                    )
                )
        return result

    def start(self, stage):
        for copy in self.copies(stage, False):
            copy.start()

    def wait_recv(self, stage):
        for copy in self.copies(stage, True):
            copy.wait_recv()

    def wait_send(self):
        for stage in range(self.bits):
            for copy in self.copies(stage, False):
                copy.wait_send()


def greet(dp, groups):
    pack, group = lax.axis_index("dp"), lax.axis_index("kv")
    bits = dp.bit_length() - 1
    barrier = pltpu.get_barrier_semaphore()
    for place in range(bits):
        other = pack + 2**place * (1 - 2 * ((pack // 2**place) % 2))
        pl.semaphore_signal(barrier, inc=1, device_id={"dp": other}, device_id_type=MESH)
    for step in range(1, groups):
        other = (group + step) % groups
        pl.semaphore_signal(barrier, inc=1, device_id={"kv": other}, device_id_type=MESH)
    pl.semaphore_wait(barrier, bits + groups - 1)


def attention_kernel(groups, head_width, *refs):
    (
        tokens_ref, gain_ref, query_w, pair_w, seg_column, seg_row, frequency, part_hbm,
        attn_out, act_out, query_out, key_out, value_out, logsum_out,
        cosine_out, sine_a_out, sine_b_out, cosine_t_out, sine_t_out, parts_out,
        query_m, value_t, part_sems,
    ) = refs
    rows = tokens_ref.shape[0] // groups
    width, span_w = query_w.shape[1], key_out.shape[1]
    heads, pair, half = span_w // head_width, 2 * head_width, head_width // 2
    scale = head_width**-0.5 * LOG2E

    def part_copy(step):
        return to_group(step, groups, part_hbm, parts_out.at[groups - 1 - step], part_sems)

    greet(1, groups)
    for step in range(1, groups):
        part_copy(step).start()
    lanes = lax.broadcasted_iota(jnp.int32, (rows, pair), 1)
    low_half = lanes % head_width < half
    head_lanes = lax.broadcasted_iota(jnp.int32, (rows, span_w), 1) // head_width

    for block in range(groups):
        part = pl.ds(block * rows, rows)
        values = tokens_ref[part].astype(jnp.float32)
        inverse = lax.rsqrt(jnp.mean(values * values, axis=1, keepdims=True) + EPS)
        act = (values * inverse * gain_ref[...]).astype(jnp.bfloat16)
        act_out[:, part] = act.T
        query_raw = times(act, query_w[...])
        pair_raw = times(act, pair_w[...])
        before = (seg_row[...] < seg_column[part]).astype(jnp.float32)
        places = (
            lax.broadcasted_iota(jnp.int32, (rows, 1), 0) + block * rows
        ).astype(jnp.float32) - jnp.sum(before, axis=1, keepdims=True)
        angles = places * frequency[...]
        cosine, sine = jnp.cos(angles), jnp.sin(angles)
        sine_a, sine_b = jnp.where(low_half, -sine, 0.0), jnp.where(low_half, 0.0, sine)
        cosine_out[part], sine_a_out[part], sine_b_out[part] = cosine, sine_a, sine_b
        cosine_t_out[:, part] = cosine.T[:half]
        sine_t_out[:, part] = sine.T[:half]

        def rotated(vectors):
            return (
                vectors * cosine
                + pltpu.roll(vectors, pair - half, 1) * sine_a
                + pltpu.roll(vectors, half, 1) * sine_b
            ).astype(jnp.bfloat16)

        for start in range(0, width, pair):
            query_out[part, pl.ds(start, pair)] = rotated(query_raw[:, start : start + pair])
        other = pltpu.roll(pair_raw, head_width, 1)
        keys_two = rotated(jnp.where(lanes < head_width, pair_raw, other))
        values_two = jnp.where(lanes < head_width, other, pair_raw)
        key_out[part] = jnp.concatenate([keys_two] * (span_w // pair), axis=1)
        value_out[part] = jnp.concatenate(
            [values_two.astype(jnp.bfloat16)] * (span_w // pair), axis=1
        )
        value_t[:, part] = values_two.T[:head_width].astype(jnp.bfloat16)
        query_seg = seg_row[:, part]
        query_place = lax.broadcasted_iota(jnp.int32, (rows, rows), 1) + block * rows

        def span(number, carry):
            columns = pl.ds(pl.multiple_of(number * span_w, span_w), span_w)
            query = query_out[part, columns]
            for head in range(heads):
                query_m[pl.ds(head * rows, rows)] = jnp.where(head_lanes == head, query, 0)

            def keys(step, carry):
                highest, total, output = carry
                piece = block - step
                key_part = pl.ds(pl.multiple_of(piece * rows, rows), rows)
                key_place = lax.broadcasted_iota(jnp.int32, (rows, rows), 0) + piece * rows
                allowed = (seg_column[key_part] == query_seg) & (key_place <= query_place)
                bias = jnp.where(allowed, 0.0, -jnp.inf)
                scores = times_t(key_out[key_part], query_m[...]) * scale
                scores = scores + jnp.concatenate([bias] * heads, axis=1)
                top = jnp.maximum(highest, jnp.max(scores, axis=0, keepdims=True))
                shrink = jnp.exp2(highest - top)
                chance = jnp.exp2(scores - top)
                total = total * shrink + jnp.sum(chance, axis=0, keepdims=True)
                output = output * shrink + times(value_t[:, key_part], chance.astype(jnp.bfloat16))
                return top, total, output

            first = (
                jnp.full((1, heads * rows), -jnp.inf, jnp.float32),
                jnp.zeros((1, heads * rows), jnp.float32),
                jnp.zeros((head_width, heads * rows), jnp.float32),
            )
            highest, total, output = lax.fori_loop(0, block + 1, keys, first)
            output = output / total
            stacked = jnp.concatenate(
                [output[:, head * rows : (head + 1) * rows] for head in range(heads)], axis=0
            )
            attn_out[part, columns] = stacked.T.astype(jnp.bfloat16)
            logsum_out[number * groups + block] = highest + jnp.log(total) * LOG2E
            return carry

        lax.fori_loop(0, width // span_w, span, 0)
    for step in range(1, groups):
        part_copy(step).wait()


def attention(tokens, gain, query_w, pair_w, segments, part, groups, collective_id):
    count, features = tokens.shape
    width, head_width = query_w.shape[1], pair_w.shape[1] // 2
    span_w = 256
    rows, heads, half = count // groups, span_w // head_width, head_width // 2
    frequency = 10000.0 ** (-(jnp.arange(half, dtype=jnp.float32) * 2.0 / head_width))
    vmem = pl.BlockSpec(memory_space=pltpu.VMEM)
    any_spec = pl.BlockSpec(memory_space=pl.ANY)
    bf16, f32 = jnp.bfloat16, jnp.float32
    return pl.pallas_call(
        functools.partial(attention_kernel, groups, head_width),
        out_shape=[
            jax.ShapeDtypeStruct((count, width), bf16),
            jax.ShapeDtypeStruct((features, count), bf16),
            jax.ShapeDtypeStruct((count, width), bf16),
            jax.ShapeDtypeStruct((count, span_w), bf16),
            jax.ShapeDtypeStruct((count, span_w), bf16),
            jax.ShapeDtypeStruct((width // span_w * groups, 1, heads * rows), f32),
            jax.ShapeDtypeStruct((count, 2 * head_width), f32),
            jax.ShapeDtypeStruct((count, 2 * head_width), f32),
            jax.ShapeDtypeStruct((count, 2 * head_width), f32),
            jax.ShapeDtypeStruct((half, count), f32),
            jax.ShapeDtypeStruct((half, count), f32),
            jax.ShapeDtypeStruct((groups - 1,) + part.shape, bf16),
        ],
        in_specs=[vmem] * 7 + [any_spec],
        out_specs=[vmem] * 11 + [any_spec],
        scratch_shapes=[
            pltpu.VMEM((heads * rows, span_w), bf16),
            pltpu.VMEM((head_width, count), bf16),
            pltpu.SemaphoreType.DMA((2, groups - 1)),
        ],
        compiler_params=pltpu.CompilerParams(
            collective_id=collective_id, has_side_effects=True, vmem_limit_bytes=VMEM_LIMIT
        ),
        cost_estimate=pl.CostEstimate(
            flops=4 * count * features * width, bytes_accessed=8 * tokens.size, transcendentals=0
        ),
    )(
        tokens,
        gain,
        query_w,
        pair_w,
        segments[:, None],
        segments[None],
        jnp.tile(frequency, 4)[None],
        part,
    )


def feed_forward_kernel(dp, groups, *refs):
    (
        attn_hbm, attn_ref, part_ref, own_hbm, gate_hbm, up_hbm, down_hbm, cot_hbm, live_hbm,
        tokens_ref, gain_ref, live_ref, pass_hbm,
        act_out, hidden_out, gate_out, up_out, back_out, feed_a_out, feed_b_out, resid_out, rows_out, all_out, pass_out,
        attn_in, all_ref, own_ref, w_gate, w_up, w_down, cot_ref, live_all, grad_hidden, resid_ref,
        load_sem, send_sem, recv_sem, spread_send, spread_recv, out_sem, pass_sems,
    ) = refs
    block = pl.program_id(0)
    blocks = groups
    group = lax.axis_index("kv")
    pack = lax.axis_index("dp")
    rows = tokens_ref.shape[0]
    others = groups - 1
    spread = Spread(all_ref, spread_send, spread_recv, dp)
    stages = dp.bit_length() - 1
    loads = [
        pltpu.make_async_copy(source, target, load_sem.at[index])
        for index, (source, target) in enumerate(
            (
                (down_hbm, w_down),
                (cot_hbm, cot_ref),
                (live_hbm, live_all),
                (own_hbm, own_ref),
                (gate_hbm, w_gate),
                (up_hbm, w_up),
            )
        )
    ]

    def attn_copy(part, step, slot, source, place):
        span = pl.ds(part * rows, rows)
        return pltpu.make_async_remote_copy(
            src_ref=source.at[span],
            dst_ref=attn_in.at[slot, span],
            send_sem=send_sem.at[part, place],
            recv_sem=recv_sem.at[part, slot],
            device_id={"kv": (group + step) % groups},
            device_id_type=MESH,
        )

    def pass_copy(step):
        return to_group(step, groups, pass_hbm, pass_out.at[others - step], pass_sems)

    line = groups == 4
    inner = (group == 1) | (group == 2)
    direct = (1, 3) if line else tuple(range(1, groups))
    relays = ((0, 3, 1), (2, 1, others)) if line else ()

    def own_copy(part, step):
        return attn_copy(part, step, others - step, attn_hbm, step - 1)

    def send_rows(part):
        for step in direct:
            own_copy(part, step).start()

    def wait_rows(part, slot):
        attn_copy(part, 1, slot, attn_hbm, 0).wait_recv()

    def pass_on(part):
        if line:

            @pl.when(inner)
            def _():
                for slot, step, place in relays:
                    wait_rows(part, slot)
                    attn_copy(part, step, 1, attn_in.at[slot], place).start()

    def wait_block(part):
        for slot in range(others):
            if line and slot != 1:

                @pl.when(jnp.logical_not(inner))
                def _():
                    wait_rows(part, slot)
            else:
                wait_rows(part, slot)

    def hidden_gradient(part):
        span = pl.ds(part * rows, rows)
        masked = (cot_ref[span].astype(jnp.float32) * live_all[span]).astype(jnp.bfloat16)
        grad_hidden[span] = times_t(masked, w_down[...]).astype(jnp.bfloat16)

    @pl.when(block == 0)
    def _():
        for load in loads:
            load.start()
        all_ref[:, pack] = part_ref[...]
        greet(dp, groups)
        send_rows(0)
        spread.start(0)
        for part in range(1, blocks):
            send_rows(part)
        for load in loads[:3]:
            load.wait()
        for stage in range(stages):
            if stage < blocks:
                hidden_gradient(stage)
            spread.wait_recv(stage)
            if stage + 1 < stages:
                spread.start(stage + 1)
            if stage < blocks - 1:
                pass_on(stage)
        for part in range(stages, blocks):
            hidden_gradient(part)
        for load in loads[3:]:
            load.wait()

    wait_block(block)
    span = pl.ds(pl.multiple_of(block * rows, rows), rows)
    width = own_ref.shape[0]
    total = tokens_ref[...].astype(jnp.float32) + times(attn_ref[...], own_ref[...])
    for slot in range(others):
        total = total + times_t(attn_in[slot, span], all_ref[slot].reshape(-1, width))
    resid_ref[...] = total
    inverse = lax.rsqrt(jnp.mean(total * total, axis=1, keepdims=True) + EPS)
    act = (total * inverse * gain_ref[...]).astype(jnp.bfloat16)
    act_out[...] = act.T
    gate = times(act, w_gate[...])
    up = times(act, w_up[...])
    chance = jax.nn.sigmoid(gate)
    swish = gate * chance
    hidden = swish * up
    feed = times(hidden.astype(jnp.bfloat16), w_down[...]).astype(jnp.bfloat16)
    feed_a_out[...] = feed[:, : feed_a_out.shape[1]]
    feed_b_out[...] = feed[:, feed_a_out.shape[1] :]
    hidden_out[...] = (hidden * live_ref[...]).astype(jnp.bfloat16).T
    grad = grad_hidden[span].astype(jnp.float32)
    gate_b = (grad * up * chance * (1.0 + gate * (1.0 - chance))).astype(jnp.bfloat16)
    up_b = (grad * swish).astype(jnp.bfloat16)
    gate_out[...] = gate_b
    up_out[...] = up_b
    back_out[...] = (times_t(gate_b, w_gate[...]) + times_t(up_b, w_up[...])).astype(jnp.bfloat16)

    @pl.when(block == group)
    def _():
        copy = pltpu.make_async_copy(resid_ref, resid_out, out_sem.at[0])
        copy.start()
        copy.wait()

    @pl.when(block == 0)
    def _():
        for part in range(min(stages, blocks - 1), blocks):
            pass_on(part)

    @pl.when(block == 1)
    def _():
        for step in range(1, groups):
            pass_copy(step).start()

    @pl.when(block == blocks - 1)
    def _():
        mine = pl.ds(pl.multiple_of(group * rows, rows), rows)
        copies = [
            pltpu.make_async_copy(attn_in.at[:, mine], rows_out, out_sem.at[1]),
            pltpu.make_async_copy(all_ref, all_out, out_sem.at[2]),
        ]
        for copy in copies:
            copy.start()
        for part in range(blocks):
            for step in direct:
                own_copy(part, step).wait_send()
        if line:

            @pl.when(inner)
            def _():
                for part in range(blocks):
                    for slot, step, place in relays:
                        attn_copy(part, step, 1, attn_in.at[slot], place).wait_send()

        spread.wait_send()
        for step in range(1, groups):
            pass_copy(step).wait()
        for copy in copies:
            copy.wait()


def feed_forward(attn, part, w_own, w_gate, w_up, w_down, cotangent, live, tokens, gain, passed, sizes, collective_id):
    dp, groups = sizes
    count, features = tokens.shape
    rows = count // groups
    width, hidden = w_own.shape[0], w_gate.shape[1]
    share = part.shape[1]
    others = groups - 1
    early = 5 * features // 8
    any_spec = pl.BlockSpec(memory_space=pl.ANY)
    by_row = lambda columns: pl.BlockSpec((rows, columns), lambda i: (i, 0))
    by_column = lambda height: pl.BlockSpec((height, rows), lambda i: (0, i))
    flops = 2 * count * features * (groups * width + 6 * hidden)
    return pl.pallas_call(
        functools.partial(feed_forward_kernel, dp, groups),
        grid=(groups,),
        out_shape=[
            jax.ShapeDtypeStruct((features, count), jnp.bfloat16),
            jax.ShapeDtypeStruct((hidden, count), jnp.bfloat16),
            jax.ShapeDtypeStruct((count, hidden), jnp.bfloat16),
            jax.ShapeDtypeStruct((count, hidden), jnp.bfloat16),
            jax.ShapeDtypeStruct((count, features), jnp.bfloat16),
            jax.ShapeDtypeStruct((count, early), jnp.bfloat16),
            jax.ShapeDtypeStruct((count, features - early), jnp.bfloat16),
            jax.ShapeDtypeStruct((rows, features), jnp.float32),
            jax.ShapeDtypeStruct((others, rows, width), jnp.bfloat16),
            jax.ShapeDtypeStruct((others, dp, share, width), jnp.bfloat16),
            jax.ShapeDtypeStruct((others,) + passed.shape, jnp.bfloat16),
        ],
        in_specs=[
            any_spec,
            by_row(width),
            pl.BlockSpec(memory_space=pltpu.VMEM),
            any_spec, any_spec, any_spec, any_spec, any_spec, any_spec,
            by_row(features),
            pl.BlockSpec(memory_space=pltpu.VMEM),
            by_row(1),
            any_spec,
        ],
        out_specs=[
            by_column(features), by_column(hidden), by_row(hidden), by_row(hidden),
            by_row(features), by_row(early), by_row(features - early), any_spec, any_spec, any_spec, any_spec,
        ],
        scratch_shapes=[
            pltpu.VMEM((others, count, width), jnp.bfloat16),
            pltpu.VMEM((others, dp, share, width), jnp.bfloat16),
            pltpu.VMEM((width, features), jnp.bfloat16),
            pltpu.VMEM((features, hidden), jnp.bfloat16),
            pltpu.VMEM((features, hidden), jnp.bfloat16),
            pltpu.VMEM((hidden, features), jnp.bfloat16),
            pltpu.VMEM((count, features), jnp.bfloat16),
            pltpu.VMEM((count, 1), jnp.float32),
            pltpu.VMEM((count, hidden), jnp.bfloat16),
            pltpu.VMEM((rows, features), jnp.float32),
            pltpu.SemaphoreType.DMA((6,)),
            pltpu.SemaphoreType.DMA((groups, groups)),
            pltpu.SemaphoreType.DMA((groups, others)),
            pltpu.SemaphoreType.DMA((2, dp - 1)),
            pltpu.SemaphoreType.DMA((2, dp - 1)),
            pltpu.SemaphoreType.DMA((3,)),
            pltpu.SemaphoreType.DMA((2, groups - 1)),
        ],
        compiler_params=pltpu.CompilerParams(
            collective_id=collective_id, has_side_effects=True, vmem_limit_bytes=VMEM_LIMIT
        ),
        cost_estimate=pl.CostEstimate(flops=flops, bytes_accessed=40 * count * features, transcendentals=0),
    )(attn, attn, part, w_own, w_gate, w_up, w_down, cotangent, live, tokens, gain, live, passed)


class Scatter:
    def __init__(self, dp, product, store, sent, held, late, sems):
        self.product, self.store, self.sent, self.held, self.late = product, store, sent, held, late
        self.first_send, self.first_recv, self.late_send, self.late_recv = sems
        self.me = lax.axis_index("dp")
        self.upper = self.me // 2
        self.bits = dp.bit_length() - 1
        self.slots = dp // 2
        self.halves = row_halves(held.shape[1])

    def bit(self, place):
        return (self.me // 2**place) % 2

    def partner(self, place):
        return self.me + 2**place * (1 - 2 * self.bit(place))

    def first_copy(self, t):
        return pltpu.make_async_remote_copy(
            src_ref=self.sent.at[t],
            dst_ref=self.held.at[t],
            send_sem=self.first_send.at[t],
            recv_sem=self.first_recv.at[t],
            device_id={"dp": self.partner(0)},
            device_id_type=MESH,
        )

    def stage_bit(self, half, stage):
        return stage - 1 if half == 0 else self.bits - 1 - stage

    def slot_of(self, half, stage, index, value):
        if half == 0:
            low = 2 ** (stage - 1)
            return index * 2**stage + value * low + self.upper % low
        top = 2 ** (self.bits - stage)
        return index + value * (top // 2) + (self.upper // top) * top

    def late_copy(self, half, stage, index, slot):
        start, size = self.halves[half]
        buffer = self.slots - 2 ** (self.bits - stage) + index
        return pltpu.make_async_remote_copy(
            src_ref=self.held.at[slot, pl.ds(start, size)],
            dst_ref=self.late[half].at[buffer],
            send_sem=self.late_send.at[half, buffer],
            recv_sem=self.late_recv.at[half, buffer],
            device_id={"dp": self.partner(self.stage_bit(half, stage) + 1)},
            device_id_type=MESH,
        )

    def other_chunks(self):
        def step(t, carry):
            self.sent[t] = self.product(2 * t + 1 - self.bit(0)).astype(jnp.bfloat16)
            self.first_copy(t).start()
            return carry

        lax.fori_loop(0, self.slots, step, 0)

    def slot_at(self, e):
        t = 0
        for place in range(self.bits - 1):
            t = t + 2**place * ((e // 2**place + 1 + self.upper // 2**place) % 2)
        return t

    def own_chunks(self, others_too=False):
        def other(t):
            self.sent[t] = self.product(2 * t + 1 - self.bit(0)).astype(jnp.bfloat16)
            self.first_copy(t).start()

        if others_too:
            other(self.slot_at(0))

        def step(e, carry):
            if others_too:
                pl.when(e + 1 < self.slots)(lambda: other(self.slot_at(e + 1)))
            t = self.slot_at(e)
            own = self.product(2 * t + self.bit(0))
            self.first_copy(t).wait_recv()
            self.held[t] = (self.held[t].astype(jnp.float32) + own).astype(jnp.bfloat16)

            @pl.when(e % 2 == 0)
            def _():
                self.late_copy(0, 1, t // 2, t).start()

            @pl.when(e < self.slots // 2)
            def _():
                self.late_copy(1, 1, t % (self.slots // 2), t).start()

            return carry

        lax.fori_loop(0, self.slots, step, 0)

    def later(self, stage):
        for half in range(2):
            start, size = self.halves[half]
            keep_bit = self.bit(self.stage_bit(half, stage) + 1)
            for index in range(2 ** (self.bits - 1 - stage)):
                slot = self.slot_of(half, stage, index, keep_bit)
                self.late_copy(half, stage, index, slot).wait_recv()
                buffer = self.slots - 2 ** (self.bits - stage) + index
                total = self.held[slot, pl.ds(start, size)].astype(jnp.float32) + self.late[half][
                    buffer
                ].astype(jnp.float32)
                if stage == self.bits - 1:
                    self.store(start, size, total)
                else:
                    self.held[slot, pl.ds(start, size)] = total.astype(jnp.bfloat16)
            if stage < self.bits - 1:
                follow = self.stage_bit(half, stage + 1) + 1
                for index in range(2 ** (self.bits - 2 - stage)):
                    slot = self.slot_of(half, stage + 1, index, 1 - self.bit(follow))
                    self.late_copy(half, stage + 1, index, slot).start()

    def finish(self):
        for t in range(self.slots):
            self.first_copy(t).wait_send()
        for half in range(2):
            for stage in range(1, self.bits):
                for index in range(2 ** (self.bits - 1 - stage)):
                    self.late_copy(half, stage, index, 0).wait_send()


def scatter_scratch(dp, rows, columns):
    slots = dp // 2
    return (
        [pltpu.VMEM((slots, rows, columns), jnp.bfloat16)] * 2
        + [pltpu.VMEM((slots - 1, size, columns), jnp.bfloat16) for _, size in row_halves(rows)]
        + [pltpu.SemaphoreType.DMA((slots,))] * 2
        + [pltpu.SemaphoreType.DMA((2, slots - 1))] * 2
    )


def scatter_from(dp, product, store, refs):
    return Scatter(dp, product, store, refs[0], refs[1], refs[2:4], refs[4:8])


def product_scatter_kernel(count, dp, *refs):
    lhs, rhs = refs[:count], refs[count : 2 * count]
    outs, scratch = refs[2 * count : 3 * count], refs[3 * count :]

    def member(a):
        def product(chunk):
            return times(lhs[a][chunk], rhs[a][...])

        def store(start, size, total):
            outs[a][pl.ds(start, size)] = total

        return scatter_from(dp, product, store, scratch[8 * a : 8 * a + 8])

    members = [member(a) for a in range(count)]
    stages = dp.bit_length() - 1
    greet(dp, 1)
    pending = []
    for a in range(count):
        members[a].own_chunks(others_too=True)
        pending.append((a, 1))
        if a > 0:
            done, stage = pending.pop(0)
            members[done].later(stage)
            if stage < stages - 1:
                pending.append((done, stage + 1))
    while pending:
        done, stage = pending.pop(0)
        members[done].later(stage)
        if stage < stages - 1:
            pending.append((done, stage + 1))
    for one in members:
        one.finish()


def product_scatter(pairs, collective_id):
    count = len(pairs)
    dp = pairs[0][0].shape[0]
    dims = [(lhs.shape[1], rhs.shape[1]) for lhs, rhs in pairs]
    flops = sum(2 * lhs.size * rhs.shape[1] for lhs, rhs in pairs)
    moved = sum(2 * (lhs.size + rhs.size) for lhs, rhs in pairs)
    vmem = pl.BlockSpec(memory_space=pltpu.VMEM)
    any_spec = pl.BlockSpec(memory_space=pl.ANY)
    return pl.pallas_call(
        functools.partial(product_scatter_kernel, count, dp),
        out_shape=[jax.ShapeDtypeStruct(dim, jnp.float32) for dim in dims],
        in_specs=[vmem] * (2 * count),
        out_specs=[vmem] * count,
        scratch_shapes=sum([scatter_scratch(dp, *dim) for dim in dims], []),
        compiler_params=pltpu.CompilerParams(
            collective_id=collective_id, has_side_effects=True, vmem_limit_bytes=VMEM_LIMIT
        ),
        cost_estimate=pl.CostEstimate(flops=flops * 3, bytes_accessed=moved, transcendentals=0),
    )(*[lhs for lhs, _ in pairs], *[rhs for _, rhs in pairs])


def norm_back(values, gain, grads):
    inverse = lax.rsqrt(jnp.mean(values * values, axis=1, keepdims=True) + EPS)
    scaled = gain * grads
    mean = jnp.mean(scaled * values, axis=1, keepdims=True)
    by_values = inverse * scaled - values * (inverse * inverse * inverse * mean)
    return by_values, jnp.sum(grads * values * inverse, axis=0, keepdims=True)


def attention_back_kernel(dp, groups, head_width, *refs):
    (
        back_ref, resid_hbm, cot_hbm, live_ref, tokens_hbm, attn_gain, mlp_gain,
        out_own, out_others, rows_ref, query_ref, key_ref, value_ref, logsum_ref, attn_ref,
        seg_column, seg_row, cosine_t, sine_t, cosine, sine_a, sine_b, qkv_own, pair_own, qkv_parts,
        tokens_out, gains_out, output_out, out_send, grad_out, qkv_all,
        cot_ref, tokens_ref, chunk_ref, weights, query_m, attn_m, key_t, query_t, key_sum, value_sum,
        attn_send, attn_grad, arrived, branch_ref,
        load_sem, last_sem, attn_sems, grad_sems, spread_send, spread_recv, *scatter_refs,
    ) = refs
    group, pack, others = lax.axis_index("kv"), lax.axis_index("dp"), groups - 1
    rows = branch_ref.shape[0]
    width = query_ref.shape[1]
    span_w = key_ref.shape[1]
    pair, half, heads = 2 * head_width, head_width // 2, span_w // head_width
    scale = head_width**-0.5
    mine = pl.ds(pl.multiple_of(group * rows, rows), rows)
    out_part = pl.ds(0, width)

    def load(index, source, target):
        return pltpu.make_async_copy(source, target, load_sem.at[index])

    first_loads = [
        load(0, resid_hbm, tokens_out),
        load(1, cot_hbm.at[mine], cot_ref),
        load(2, out_others, weights.at[:, :, out_part]),
        load(3, qkv_parts, qkv_all.at[:, pack]),
        load(4, tokens_hbm.at[mine], tokens_ref),
    ]
    for one in first_loads:
        one.start()

    spans = width // span_w

    def attn_copy(number, step):
        return to_group(
            step, groups, attn_send.at[number, step - 1], attn_grad.at[number, group], attn_sems.at[number]
        )

    def columns_of(number):
        start = number * span_w
        return pl.ds(start, span_w if number < spans - 1 else width + pair - start)

    def grad_copy(number, step, block):
        columns = columns_of(number)
        return to_group(
            step,
            groups,
            grad_out.at[pl.ds(block * rows, rows), columns],
            arrived.at[step - 1, :, columns],
            grad_sems.at[number],
        )

    share = output_out.shape[0]

    greet(dp, groups)
    spread = Spread(qkv_all, spread_send, spread_recv, dp)
    lanes = lax.broadcasted_iota(jnp.int32, (rows, span_w), 1) // head_width
    first_loads[3].wait()
    spread.start(0)
    first_loads[0].wait()
    first_loads[1].wait()
    values = tokens_out[...]
    grad_resid, mlp_rows = norm_back(values, mlp_gain[...], back_ref[...].astype(jnp.float32))
    grad_resid = grad_resid + cot_ref[...].astype(jnp.float32) * live_ref[mine]
    tokens_out[...] = grad_resid
    branch_ref[...] = grad_resid.astype(jnp.bfloat16)
    stages = dp.bit_length() - 1
    first_loads[2].wait()
    for number in range(spans):
        columns = pl.ds(number * span_w, span_w)
        for step in range(1, groups):
            attn_send[number, step - 1] = times(branch_ref[...], weights[step - 1, :, columns]).astype(
                jnp.bfloat16
            )
            attn_copy(number, step).start()
        attn_grad[number, group] = times_t(branch_ref[...], out_own[columns]).astype(jnp.bfloat16)

    spread.wait_recv(0)
    spread.start(1)

    def store(start, size, total):
        if start == 0:
            output_out[...] = total[:share]
        out_send[pl.ds(start, size)] = total.astype(jnp.bfloat16)

    scatter = scatter_from(dp, lambda chunk: times(chunk_ref[chunk], branch_ref[...]), store, scatter_refs)
    for place in range(groups):
        turned = (attn_ref[mine] if place == 0 else rows_ref[place - 1]).T
        chunk_ref[:, pl.ds(place * share, share)] = turned.reshape(dp, share, rows)
    scatter.other_chunks()
    scatter.own_chunks()
    for block in range(groups):
        part = pl.ds(block * rows, rows)
        key_t[:, part] = key_ref[part, pl.ds(0, pair)].T[:head_width]
    key_sum[...] = jnp.zeros_like(key_sum)
    value_sum[...] = jnp.zeros_like(value_sum)

    def attend(number, block):
        part = pl.ds(block * rows, rows)

        @pl.when(block != group)
        def _():
            step = (group - block + groups) % groups
            landed = attn_grad.at[number, block]
            to_group(step, groups, landed, landed, attn_sems.at[number]).wait_recv()

        query_seg = seg_row[:, part]
        query_place = lax.broadcasted_iota(jnp.int32, (rows, rows), 1) + block * rows

        def wide(entries):
            return jnp.concatenate([entries] * heads, axis=1)

        if True:
            columns = pl.ds(number * span_w, span_w)
            query = query_ref[part, columns]
            grad = attn_grad[number, block]
            weighed = (grad.astype(jnp.float32) * attn_ref[part, columns].astype(jnp.float32)).T
            centres = jnp.sum(weighed.reshape(heads, head_width, rows), axis=1)
            centre = jnp.concatenate([centres[head : head + 1] for head in range(heads)], axis=1)
            logsum = logsum_ref[number * groups + block]
            for head in range(heads):
                place = pl.ds(head * rows, rows)
                query_m[place] = jnp.where(lanes == head, query, 0)
                attn_m[place] = jnp.where(lanes == head, grad, 0)
            query_t[...] = jnp.zeros_like(query_t)

            def keys(piece, carry):
                key_part = pl.ds(pl.multiple_of(piece * rows, rows), rows)
                key_place = lax.broadcasted_iota(jnp.int32, (rows, rows), 0) + piece * rows
                allowed = (seg_column[key_part] == query_seg) & (key_place <= query_place)
                bias = jnp.where(allowed, 0.0, -jnp.inf)
                scores = times_t(key_ref[key_part], query_m[...]) * (scale * LOG2E)
                chance = jnp.exp2(scores - logsum + wide(bias))
                probs = times_t(value_ref[key_part], attn_m[...])
                slope = (chance * (probs - centre)).astype(jnp.bfloat16)
                value_sum[key_part] += times(chance.astype(jnp.bfloat16), attn_m[...])
                key_sum[key_part] += times(slope, query_m[...])
                query_t[...] += times(key_t[:, key_part], slope)
                return carry

            lax.fori_loop(0, block + 1, keys, 0)
            cos, sin = wide(cosine_t[:, part]), wide(sine_t[:, part])
            low, high = query_t[:half] * scale, query_t[half:] * scale
            turned = jnp.concatenate([low * cos + high * sin, high * cos - low * sin], axis=0)
            stacked = jnp.concatenate(
                [turned[:, head * rows : (head + 1) * rows] for head in range(heads)], axis=0
            )
            grad_out[part, columns] = stacked.T.astype(jnp.bfloat16)

        def folded(total):
            sums = total[part, pl.ds(0, pair)]
            for step in range(1, span_w // pair):
                sums = sums + total[part, pl.ds(step * pair, pair)]
            return sums + pltpu.roll(sums, head_width, 1)

        if number == spans - 1:
            grad_k = folded(key_sum) * scale
            grad_k = (
                grad_k * cosine[part]
                - pltpu.roll(grad_k, pair - half, 1) * sine_a[part]
                - pltpu.roll(grad_k, half, 1) * sine_b[part]
            )
            first = lax.broadcasted_iota(jnp.int32, (rows, pair), 1) < head_width
            grad_out[part, pl.ds(width, pair)] = jnp.where(
                first, grad_k, folded(value_sum)
            ).astype(jnp.bfloat16)

        @pl.when(block != group)
        def _():
            grad_copy(number, (block - group + groups) % groups, block).start()

    turns = [(number, block) for number in range(spans) for block in reversed(range(groups))]
    for turn, (number, block) in enumerate(turns):
        attend(number, block)
        if turn == 3:
            for stage in range(1, stages - 1):
                spread.wait_recv(stage)
                spread.start(stage + 1)
    for stage in range(1, stages - 1):
        scatter.later(stage)
    spread.wait_recv(stages - 1)
    part_rows = qkv_all.shape[2]
    last_loads = [
        pltpu.make_async_copy(
            qkv_all.at[:, place], weights.at[:, pl.ds(place * part_rows, part_rows)], last_sem.at[place]
        )
        for place in range(dp)
    ]
    for one in last_loads:
        one.start()
    grad_act = times_t(grad_out[mine, out_part], qkv_own[...])
    grad_act = grad_act + times_t(grad_out[mine, pl.ds(width, pair)], pair_own[...])
    for one in last_loads:
        one.wait()
    for number in range(spans):
        columns = columns_of(number)
        for step in range(1, groups):
            landed = arrived.at[step - 1, :, columns]
            to_group(step, groups, landed, landed, grad_sems.at[number]).wait_recv()
            grad_act = grad_act + times_t(
                arrived[step - 1, :, columns], weights[others - step, :, columns]
            )
    first_loads[4].wait()
    by_tokens, attn_rows = norm_back(tokens_ref[...].astype(jnp.float32), attn_gain[...], grad_act)
    tokens_out[...] += by_tokens
    scatter.later(stages - 1)
    columns = gains_out.shape[2]
    for place in range(dp):
        span = slice(place * columns, (place + 1) * columns)
        gains_out[place, 0:1] = mlp_rows[:, span]
        gains_out[place, 1:2] = attn_rows[:, span]
    for step in range(1, groups):
        for number in range(spans):
            attn_copy(number, step).wait_send()
            grad_copy(number, step, 0).wait_send()
    spread.wait_send()
    scatter.finish()


def attention_back(operands, sizes, head_width, collective_id):
    dp, groups = sizes
    others_w, rows_others, query, key, parts = (operands[index] for index in (8, 9, 10, 11, 24))
    rows, width = rows_others.shape[1:]
    features = others_w.shape[1]
    count, span_w = key.shape
    share = width // dp
    stacked = (span_w // head_width) * rows
    columns = width + 2 * head_width
    vmem = pl.BlockSpec(memory_space=pltpu.VMEM)
    any_spec = pl.BlockSpec(memory_space=pl.ANY)
    bf16, f32 = jnp.bfloat16, jnp.float32
    flops = 2 * count * count * width * 10
    return pl.pallas_call(
        functools.partial(attention_back_kernel, dp, groups, head_width),
        out_shape=[
            jax.ShapeDtypeStruct((rows, features), f32),
            jax.ShapeDtypeStruct((dp, 2, features // dp), f32),
            jax.ShapeDtypeStruct((share, features), f32),
            jax.ShapeDtypeStruct((groups * share, features), bf16),
            jax.ShapeDtypeStruct((count, columns), bf16),
            jax.ShapeDtypeStruct((groups - 1, dp) + parts.shape[1:], bf16),
        ],
        in_specs=[any_spec if index in (1, 2, 4, 8, 24) else vmem for index in range(25)],
        out_specs=[vmem] * 5 + [any_spec],
        scratch_shapes=[
            pltpu.VMEM((rows, features), bf16),
            pltpu.VMEM((rows, features), bf16),
            pltpu.VMEM((dp, groups * share, rows), bf16),
            pltpu.VMEM((groups - 1, features, columns), bf16),
            pltpu.VMEM((stacked, span_w), bf16),
            pltpu.VMEM((stacked, span_w), bf16),
            pltpu.VMEM((head_width, count), bf16),
            pltpu.VMEM((head_width, stacked), f32),
            pltpu.VMEM((count, span_w), f32),
            pltpu.VMEM((count, span_w), f32),
            pltpu.VMEM((width // span_w, groups - 1, rows, span_w), bf16),
            pltpu.VMEM((width // span_w, groups, rows, span_w), bf16),
            pltpu.VMEM((groups - 1, rows, columns), bf16),
            pltpu.VMEM((rows, features), bf16),
            pltpu.SemaphoreType.DMA((5,)),
            pltpu.SemaphoreType.DMA((dp,)),
            pltpu.SemaphoreType.DMA((width // span_w, 2, groups - 1)),
            pltpu.SemaphoreType.DMA((width // span_w, 2, groups - 1)),
            pltpu.SemaphoreType.DMA((2, dp - 1)),
            pltpu.SemaphoreType.DMA((2, dp - 1)),
        ]
        + scatter_scratch(dp, groups * share, features),
        compiler_params=pltpu.CompilerParams(
            collective_id=collective_id, has_side_effects=True, vmem_limit_bytes=VMEM_LIMIT
        ),
        cost_estimate=pl.CostEstimate(flops=flops, bytes_accessed=40 * 2**20, transcendentals=0),
    )(*operands)


def last_sums_kernel(dp, groups, lhs_ref, rhs_ref, gains_ref, output_ref, sums_ref, query_out, key_out, value_out, output_out, gains_out, out_recv, out_sems, near, far, total, near_sems, far_sems, *scatter_refs):
    pack, group = lax.axis_index("dp"), lax.axis_index("kv")

    def store(start, size, value):
        span, width, head_width = pl.ds(start, size), query_out.shape[1], key_out.shape[1]
        query_out[span] = value[:, :width]
        key_out[span] = value[:, width : width + head_width]
        value_out[span] = value[:, width + head_width :]

    scatter = scatter_from(dp, lambda chunk: times(lhs_ref[chunk], rhs_ref[...]), store, scatter_refs)

    share = output_out.shape[0]

    def out_copy(step):
        source = sums_ref.at[pl.ds(step * share, share)]
        return to_group(step, groups, source, out_recv.at[step - 1], out_sems)

    def near_copy(step):
        return pltpu.make_async_remote_copy(
            src_ref=gains_ref,
            dst_ref=near.at[step - 1],
            send_sem=near_sems.at[0, step - 1],
            recv_sem=near_sems.at[1, step - 1],
            device_id={"kv": (group + step) % groups},
            device_id_type=MESH,
        )

    def far_copy(step):
        other = (pack + step) % dp
        return pltpu.make_async_remote_copy(
            src_ref=total.at[other],
            dst_ref=far.at[step - 1],
            send_sem=far_sems.at[0, step - 1],
            recv_sem=far_sems.at[1, step - 1],
            device_id={"dp": other},
            device_id_type=MESH,
        )

    barrier = pltpu.get_barrier_semaphore()
    for step in range(1, dp):
        pl.semaphore_signal(
            barrier, inc=1, device_id={"dp": (pack + step) % dp}, device_id_type=MESH
        )
    for step in range(1, groups):
        pl.semaphore_signal(
            barrier, inc=1, device_id={"kv": (group + step) % groups}, device_id_type=MESH
        )
    pl.semaphore_wait(barrier, dp + groups - 2)
    for step in range(1, groups):
        near_copy(step).start()
        out_copy(step).start()
    scatter.other_chunks()
    value = gains_ref[...]
    for step in range(1, groups):
        near_copy(step).wait_recv()
        value = value + near[step - 1]
    total[...] = value
    for step in range(1, dp):
        far_copy(step).start()
    scatter.own_chunks()
    for stage in range(1, dp.bit_length() - 1):
        scatter.later(stage)
    value = total[pack]
    for step in range(1, dp):
        far_copy(step).wait_recv()
        value = value + far[step - 1]
    gains_out[...] = value
    value = output_ref[...]
    for step in range(1, groups):
        out_copy(step).wait_recv()
        value = value + out_recv[step - 1].astype(jnp.float32)
    output_out[...] = value
    for step in range(1, groups):
        near_copy(step).wait_send()
        out_copy(step).wait_send()
    for step in range(1, dp):
        far_copy(step).wait_send()
    scatter.finish()


def last_sums(lhs, rhs, gains, output, sums, head_width, groups, collective_id):
    dp, rows = lhs.shape[0], lhs.shape[1]
    columns = rhs.shape[1]
    vmem = pl.BlockSpec(memory_space=pltpu.VMEM)
    return pl.pallas_call(
        functools.partial(last_sums_kernel, dp, groups),
        out_shape=[
            jax.ShapeDtypeStruct((rows, columns - 2 * head_width), jnp.float32),
            jax.ShapeDtypeStruct((rows, head_width), jnp.float32),
            jax.ShapeDtypeStruct((rows, head_width), jnp.float32),
            jax.ShapeDtypeStruct(output.shape, jnp.float32),
            jax.ShapeDtypeStruct(gains.shape[1:], jnp.float32),
        ],
        in_specs=[vmem] * 5,
        out_specs=[vmem] * 5,
        scratch_shapes=[
            pltpu.VMEM((groups - 1,) + output.shape, jnp.bfloat16),
            pltpu.SemaphoreType.DMA((2, groups - 1)),
            pltpu.VMEM((groups - 1,) + gains.shape, jnp.float32),
            pltpu.VMEM((dp - 1,) + gains.shape[1:], jnp.float32),
            pltpu.VMEM(gains.shape, jnp.float32),
            pltpu.SemaphoreType.DMA((2, groups - 1)),
            pltpu.SemaphoreType.DMA((2, dp - 1)),
        ]
        + scatter_scratch(dp, rows, columns),
        compiler_params=pltpu.CompilerParams(
            collective_id=collective_id, has_side_effects=True, vmem_limit_bytes=VMEM_LIMIT
        ),
        cost_estimate=pl.CostEstimate(
            flops=2 * lhs.size * columns, bytes_accessed=2 * lhs.size, transcendentals=0
        ),
    )(lhs, rhs, gains, output, sums)


def row_chunks(matrix, count):
    chunks = matrix.reshape(count, matrix.shape[0] // count, matrix.shape[1])
    return jnp.pad(chunks, ((0, 0), (0, -chunks.shape[1] % 16), (0, 0)))


def per_device(
    tokens_in,
    attn_gain,
    w_query,
    w_key,
    w_value,
    w_output,
    mlp_gain,
    w_gate,
    w_up,
    w_down,
    counts,
    segments,
    cotangent,
):
    row_count = tokens_in.shape[0]
    head_width = w_key.shape[1]
    pack_count, group_count = lax.axis_size("dp"), lax.axis_size("kv")
    sizes = (pack_count, group_count)
    pack = lax.axis_index("dp")
    share = w_query.shape[0] // pack_count
    w_pair = jnp.concatenate([w_key, w_value], axis=1)

    def own_share(matrix):
        return lax.dynamic_slice_in_dim(matrix, pack * share, share, 0)

    out_part = lax.dynamic_slice_in_dim(w_output[0], pack * share, share, 1).T
    qkv_part = jnp.concatenate([own_share(w_query), own_share(w_pair)], axis=1)
    live_rows = (jnp.arange(row_count) < counts[0]).astype(jnp.float32)[:, None]
    (
        attn_out,
        act_flipped,
        query,
        key,
        value,
        logsums,
        cosine,
        sine_a,
        sine_b,
        cosine_t,
        sine_t,
        out_parts,
    ) = attention(tokens_in, attn_gain[None], w_query, w_pair, segments, out_part, group_count, 5)
    (
        second_flipped,
        hidden_flipped,
        grad_gate,
        grad_up,
        grad_act_two,
        feed_early,
        feed_late,
        resid_mine,
        attn_others,
        out_others,
        qkv_parts,
    ) = feed_forward(
        attn_out,
        out_parts,
        w_output[0],
        w_gate,
        w_up,
        w_down[0],
        cotangent,
        live_rows,
        tokens_in,
        mlp_gain[None],
        qkv_part,
        sizes,
        1,
    )
    second_chunks = row_chunks(second_flipped, pack_count)
    sent_gate, sent_up, sent_down = product_scatter(
        [
            (second_chunks, grad_gate),
            (second_chunks, grad_up),
            (row_chunks(hidden_flipped, pack_count), cotangent),
        ],
        2,
    )
    grad_two_mine = lax.psum_scatter(grad_act_two, "kv", scatter_dimension=0, tiled=True)
    grad_two_mine, feed_early, sent_down = lax.optimization_barrier(
        (grad_two_mine, feed_early, sent_down)
    )
    grad_tokens, gain_rows, own_output, output_sums, grad_qkv, _ = attention_back(
        (
            grad_two_mine,
            resid_mine,
            cotangent,
            live_rows,
            tokens_in,
            attn_gain[None],
            mlp_gain[None],
            w_output[0],
            out_others.reshape(group_count - 1, -1, w_output.shape[1]),
            attn_others,
            query,
            key,
            value,
            logsums,
            attn_out,
            segments[:, None],
            segments[None],
            cosine_t,
            sine_t,
            cosine,
            sine_a,
            sine_b,
            w_query,
            w_pair,
            qkv_parts,
        ),
        sizes,
        head_width,
        3,
    )
    early_sum = lax.psum_scatter(feed_early, "kv", scatter_dimension=0, tiled=True)
    early_sum, feed_late, grad_qkv = lax.optimization_barrier((early_sum, feed_late, grad_qkv))
    sent_query, sent_key, sent_value, sent_output, gains = last_sums(
        row_chunks(act_flipped, pack_count),
        grad_qkv,
        gain_rows,
        own_output,
        output_sums,
        head_width,
        group_count,
        4,
    )
    sent_two, sent_one = gains[0], gains[1]
    sent_output = sent_output[None]
    sent_down = sent_down[: w_down.shape[1] // pack_count][None]
    late_sum = lax.psum_scatter(feed_late, "kv", scatter_dimension=0, tiled=True)
    feed_sum = jnp.concatenate([early_sum, late_sum], axis=1).astype(jnp.float32)
    layer_out = (resid_mine + feed_sum).astype(jnp.bfloat16)
    return (
        layer_out,
        grad_tokens,
        sent_one,
        sent_query,
        sent_key,
        sent_value,
        sent_output,
        sent_two,
        sent_gate,
        sent_up,
        sent_down,
    )


def solution(mesh):
    return jax.shard_map(
        per_device,
        mesh=mesh,
        in_specs=(
            P("dp", None),
            P(),
            P(None, "kv"),
            P(None, "kv"),
            P(None, "kv"),
            P("kv", None, None),
            P(),
            P(None, "kv"),
            P(None, "kv"),
            P("kv", None, None),
            P("dp"),
            P("dp"),
            P("dp", None),
        ),
        out_specs=(
            P(("dp", "kv"), None),
            P(("dp", "kv"), None),
            P("dp"),
            P("dp", "kv"),
            P("dp", "kv"),
            P("dp", "kv"),
            P("kv", "dp", None),
            P("dp"),
            P("dp", "kv"),
            P("dp", "kv"),
            P("kv", "dp", None),
        ),
        check_vma=False,
    )
```

```python
import functools

import jax
import jax.numpy as jnp
from jax import lax
from jax.experimental import pallas as pl
from jax.experimental.pallas import tpu as pltpu
from jax.sharding import PartitionSpec as P

EPS = 1e-05
LOG2E = 1.4426950408889634
MESH = pl.DeviceIdType.MESH
VMEM_LIMIT = 60 * 1024 * 1024


def row_halves(rows):
    upper = -(-rows // 32) * 16
    return ((0, upper), (upper, rows - upper))


def times(first, second):
    return jnp.dot(first, second, preferred_element_type=jnp.float32)


def times_t(first, second):
    return lax.dot_general(
        first, second, (((1,), (1,)), ((), ())), preferred_element_type=jnp.float32
    )


def to_group(step, groups, source, target, sems):
    return pltpu.make_async_remote_copy(
        src_ref=source,
        dst_ref=target,
        send_sem=sems.at[0, step - 1],
        recv_sem=sems.at[1, step - 1],
        device_id={"kv": (lax.axis_index("kv") + step) % groups},
        device_id_type=MESH,
    )


class Spread:
    def __init__(self, buffer, send_sem, recv_sem, dp):
        self.buffer, self.send_sem, self.recv_sem = buffer, send_sem, recv_sem
        self.me = lax.axis_index("dp")
        self.bits = dp.bit_length() - 1
        rows = buffer.shape[2]
        self.halves = row_halves(rows)

    def flipped(self, places):
        device = self.me
        for place in places:
            device = device + 2**place * (1 - 2 * ((self.me // 2**place) % 2))
        return device

    def copies(self, stage, arriving):
        result = []
        for half in range(2):
            order = list(range(1, self.bits))
            order = (order if half == 0 else order[::-1]) + [0]
            for subset in range(2**stage):
                places = [order[b] for b in range(stage) if subset >> b & 1]
                if arriving:
                    places = places + [order[stage]]
                part = self.buffer.at[:, self.flipped(places), pl.ds(*self.halves[half])]
                number = 2**stage - 1 + subset
                result.append(
                    pltpu.make_async_remote_copy(
                        src_ref=part,
                        dst_ref=part,
                        send_sem=self.send_sem.at[half, number],
                        recv_sem=self.recv_sem.at[half, number],
                        device_id={"dp": self.flipped([order[stage]])},
                        device_id_type=MESH,
                    )
                )
        return result

    def start(self, stage):
        for copy in self.copies(stage, False):
            copy.start()

    def wait_recv(self, stage):
        for copy in self.copies(stage, True):
            copy.wait_recv()

    def wait_send(self):
        for stage in range(self.bits):
            for copy in self.copies(stage, False):
                copy.wait_send()


def greet(dp, groups):
    pack, group = lax.axis_index("dp"), lax.axis_index("kv")
    bits = dp.bit_length() - 1
    barrier = pltpu.get_barrier_semaphore()
    for place in range(bits):
        other = pack + 2**place * (1 - 2 * ((pack // 2**place) % 2))
        pl.semaphore_signal(barrier, inc=1, device_id={"dp": other}, device_id_type=MESH)
    for step in range(1, groups):
        other = (group + step) % groups
        pl.semaphore_signal(barrier, inc=1, device_id={"kv": other}, device_id_type=MESH)
    pl.semaphore_wait(barrier, bits + groups - 1)


def attention_kernel(groups, head_width, *refs):
    (
        tokens_ref, gain_ref, query_w, pair_w, seg_column, seg_row, frequency, part_hbm,
        attn_out, act_out, query_out, key_out, value_out, logsum_out,
        cosine_out, sine_a_out, sine_b_out, cosine_t_out, sine_t_out, parts_out,
        query_m, value_t, part_sems,
    ) = refs
    rows = tokens_ref.shape[0] // groups
    width, span_w = query_w.shape[1], key_out.shape[1]
    heads, pair, half = span_w // head_width, 2 * head_width, head_width // 2
    scale = head_width**-0.5 * LOG2E

    def part_copy(step):
        return to_group(step, groups, part_hbm, parts_out.at[groups - 1 - step], part_sems)

    greet(1, groups)
    for step in range(1, groups):
        part_copy(step).start()
    lanes = lax.broadcasted_iota(jnp.int32, (rows, pair), 1)
    low_half = lanes % head_width < half
    head_lanes = lax.broadcasted_iota(jnp.int32, (rows, span_w), 1) // head_width

    for block in range(groups):
        part = pl.ds(block * rows, rows)
        values = tokens_ref[part].astype(jnp.float32)
        inverse = lax.rsqrt(jnp.mean(values * values, axis=1, keepdims=True) + EPS)
        act = (values * inverse * gain_ref[...]).astype(jnp.bfloat16)
        act_out[:, part] = act.T
        query_raw = times(act, query_w[...])
        pair_raw = times(act, pair_w[...])
        before = (seg_row[...] < seg_column[part]).astype(jnp.float32)
        places = (
            lax.broadcasted_iota(jnp.int32, (rows, 1), 0) + block * rows
        ).astype(jnp.float32) - jnp.sum(before, axis=1, keepdims=True)
        angles = places * frequency[...]
        cosine, sine = jnp.cos(angles), jnp.sin(angles)
        sine_a, sine_b = jnp.where(low_half, -sine, 0.0), jnp.where(low_half, 0.0, sine)
        cosine_out[part], sine_a_out[part], sine_b_out[part] = cosine, sine_a, sine_b
        cosine_t_out[:, part] = cosine.T[:half]
        sine_t_out[:, part] = sine.T[:half]

        def rotated(vectors):
            return (
                vectors * cosine
                + pltpu.roll(vectors, pair - half, 1) * sine_a
                + pltpu.roll(vectors, half, 1) * sine_b
            ).astype(jnp.bfloat16)

        for start in range(0, width, pair):
            query_out[part, pl.ds(start, pair)] = rotated(query_raw[:, start : start + pair])
        other = pltpu.roll(pair_raw, head_width, 1)
        keys_two = rotated(jnp.where(lanes < head_width, pair_raw, other))
        values_two = jnp.where(lanes < head_width, other, pair_raw)
        key_out[part] = jnp.concatenate([keys_two] * (span_w // pair), axis=1)
        value_out[part] = jnp.concatenate(
            [values_two.astype(jnp.bfloat16)] * (span_w // pair), axis=1
        )
        value_t[:, part] = values_two.T[:head_width].astype(jnp.bfloat16)
        query_seg = seg_row[:, part]
        query_place = lax.broadcasted_iota(jnp.int32, (rows, rows), 1) + block * rows

        def span(number, carry):
            columns = pl.ds(pl.multiple_of(number * span_w, span_w), span_w)
            query = query_out[part, columns]
            for head in range(heads):
                query_m[pl.ds(head * rows, rows)] = jnp.where(head_lanes == head, query, 0)

            def keys(step, carry):
                highest, total, output = carry
                piece = block - step
                key_part = pl.ds(pl.multiple_of(piece * rows, rows), rows)
                key_place = lax.broadcasted_iota(jnp.int32, (rows, rows), 0) + piece * rows
                allowed = (seg_column[key_part] == query_seg) & (key_place <= query_place)
                bias = jnp.where(allowed, 0.0, -jnp.inf)
                scores = times_t(key_out[key_part], query_m[...]) * scale
                scores = scores + jnp.concatenate([bias] * heads, axis=1)
                top = jnp.maximum(highest, jnp.max(scores, axis=0, keepdims=True))
                shrink = jnp.exp2(highest - top)
                chance = jnp.exp2(scores - top)
                total = total * shrink + jnp.sum(chance, axis=0, keepdims=True)
                output = output * shrink + times(value_t[:, key_part], chance.astype(jnp.bfloat16))
                return top, total, output

            first = (
                jnp.full((1, heads * rows), -jnp.inf, jnp.float32),
                jnp.zeros((1, heads * rows), jnp.float32),
                jnp.zeros((head_width, heads * rows), jnp.float32),
            )
            highest, total, output = lax.fori_loop(0, block + 1, keys, first)
            output = output / total
            stacked = jnp.concatenate(
                [output[:, head * rows : (head + 1) * rows] for head in range(heads)], axis=0
            )
            attn_out[part, columns] = stacked.T.astype(jnp.bfloat16)
            logsum_out[number * groups + block] = highest + jnp.log(total) * LOG2E
            return carry

        lax.fori_loop(0, width // span_w, span, 0)
    for step in range(1, groups):
        part_copy(step).wait()


def attention(tokens, gain, query_w, pair_w, segments, part, groups, collective_id):
    count, features = tokens.shape
    width, head_width = query_w.shape[1], pair_w.shape[1] // 2
    span_w = 256
    rows, heads, half = count // groups, span_w // head_width, head_width // 2
    frequency = 10000.0 ** (-(jnp.arange(half, dtype=jnp.float32) * 2.0 / head_width))
    vmem = pl.BlockSpec(memory_space=pltpu.VMEM)
    any_spec = pl.BlockSpec(memory_space=pl.ANY)
    bf16, f32 = jnp.bfloat16, jnp.float32
    return pl.pallas_call(
        functools.partial(attention_kernel, groups, head_width),
        out_shape=[
            jax.ShapeDtypeStruct((count, width), bf16),
            jax.ShapeDtypeStruct((features, count), bf16),
            jax.ShapeDtypeStruct((count, width), bf16),
            jax.ShapeDtypeStruct((count, span_w), bf16),
            jax.ShapeDtypeStruct((count, span_w), bf16),
            jax.ShapeDtypeStruct((width // span_w * groups, 1, heads * rows), f32),
            jax.ShapeDtypeStruct((count, 2 * head_width), f32),
            jax.ShapeDtypeStruct((count, 2 * head_width), f32),
            jax.ShapeDtypeStruct((count, 2 * head_width), f32),
            jax.ShapeDtypeStruct((half, count), f32),
            jax.ShapeDtypeStruct((half, count), f32),
            jax.ShapeDtypeStruct((groups - 1,) + part.shape, bf16),
        ],
        in_specs=[vmem] * 7 + [any_spec],
        out_specs=[vmem] * 11 + [any_spec],
        scratch_shapes=[
            pltpu.VMEM((heads * rows, span_w), bf16),
            pltpu.VMEM((head_width, count), bf16),
            pltpu.SemaphoreType.DMA((2, groups - 1)),
        ],
        compiler_params=pltpu.CompilerParams(
            collective_id=collective_id, has_side_effects=True, vmem_limit_bytes=VMEM_LIMIT
        ),
        cost_estimate=pl.CostEstimate(
            flops=4 * count * features * width, bytes_accessed=8 * tokens.size, transcendentals=0
        ),
    )(
        tokens,
        gain,
        query_w,
        pair_w,
        segments[:, None],
        segments[None],
        jnp.tile(frequency, 4)[None],
        part,
    )


def feed_forward_kernel(dp, groups, *refs):
    (
        attn_hbm, attn_ref, part_ref, own_hbm, gate_hbm, up_hbm, down_hbm, cot_hbm, live_hbm,
        tokens_ref, gain_ref, live_ref, pass_hbm,
        act_out, hidden_out, gate_out, up_out, back_out, feed_a_out, feed_b_out, resid_out, rows_out, all_out, pass_out,
        attn_in, all_ref, own_ref, w_gate, w_up, w_down, cot_ref, live_all, grad_hidden, resid_ref,
        load_sem, send_sem, recv_sem, spread_send, spread_recv, out_sem, pass_sems,
    ) = refs
    block = pl.program_id(0)
    blocks = groups
    group = lax.axis_index("kv")
    pack = lax.axis_index("dp")
    rows = tokens_ref.shape[0]
    others = groups - 1
    spread = Spread(all_ref, spread_send, spread_recv, dp)
    stages = dp.bit_length() - 1
    loads = [
        pltpu.make_async_copy(source, target, load_sem.at[index])
        for index, (source, target) in enumerate(
            (
                (down_hbm, w_down),
                (cot_hbm, cot_ref),
                (live_hbm, live_all),
                (own_hbm, own_ref),
                (gate_hbm, w_gate),
                (up_hbm, w_up),
            )
        )
    ]

    def attn_copy(part, step, slot, source, place):
        span = pl.ds(part * rows, rows)
        return pltpu.make_async_remote_copy(
            src_ref=source.at[span],
            dst_ref=attn_in.at[slot, span],
            send_sem=send_sem.at[part, place],
            recv_sem=recv_sem.at[part, slot],
            device_id={"kv": (group + step) % groups},
            device_id_type=MESH,
        )

    def pass_copy(step):
        return to_group(step, groups, pass_hbm, pass_out.at[others - step], pass_sems)

    line = groups == 4
    inner = (group == 1) | (group == 2)
    direct = (1, 3) if line else tuple(range(1, groups))
    relays = ((0, 3, 1), (2, 1, others)) if line else ()

    def own_copy(part, step):
        return attn_copy(part, step, others - step, attn_hbm, step - 1)

    def send_rows(part):
        for step in direct:
            own_copy(part, step).start()

    def wait_rows(part, slot):
        attn_copy(part, 1, slot, attn_hbm, 0).wait_recv()

    def pass_on(part):
        if line:

            @pl.when(inner)
            def _():
                for slot, step, place in relays:
                    wait_rows(part, slot)
                    attn_copy(part, step, 1, attn_in.at[slot], place).start()

    def wait_block(part):
        for slot in range(others):
            if line and slot != 1:

                @pl.when(jnp.logical_not(inner))
                def _():
                    wait_rows(part, slot)
            else:
                wait_rows(part, slot)

    def hidden_gradient(part):
        span = pl.ds(part * rows, rows)
        masked = (cot_ref[span].astype(jnp.float32) * live_all[span]).astype(jnp.bfloat16)
        grad_hidden[span] = times_t(masked, w_down[...]).astype(jnp.bfloat16)

    @pl.when(block == 0)
    def _():
        for load in loads:
            load.start()
        all_ref[:, pack] = part_ref[...]
        greet(dp, groups)
        send_rows(0)
        spread.start(0)
        for part in range(1, blocks):
            send_rows(part)
        for load in loads[:3]:
            load.wait()
        for stage in range(stages):
            if stage < blocks:
                hidden_gradient(stage)
            spread.wait_recv(stage)
            if stage + 1 < stages:
                spread.start(stage + 1)
            if stage < blocks - 1:
                pass_on(stage)
        for part in range(stages, blocks):
            hidden_gradient(part)
        for load in loads[3:]:
            load.wait()

    wait_block(block)
    span = pl.ds(pl.multiple_of(block * rows, rows), rows)
    width = own_ref.shape[0]
    total = tokens_ref[...].astype(jnp.float32) + times(attn_ref[...], own_ref[...])
    for slot in range(others):
        total = total + times_t(attn_in[slot, span], all_ref[slot].reshape(-1, width))
    resid_ref[...] = total
    inverse = lax.rsqrt(jnp.mean(total * total, axis=1, keepdims=True) + EPS)
    act = (total * inverse * gain_ref[...]).astype(jnp.bfloat16)
    act_out[...] = act.T
    gate = times(act, w_gate[...])
    up = times(act, w_up[...])
    chance = jax.nn.sigmoid(gate)
    swish = gate * chance
    hidden = swish * up
    feed = times(hidden.astype(jnp.bfloat16), w_down[...]).astype(jnp.bfloat16)
    feed_a_out[...] = feed[:, : feed_a_out.shape[1]]
    feed_b_out[...] = feed[:, feed_a_out.shape[1] :]
    hidden_out[...] = (hidden * live_ref[...]).astype(jnp.bfloat16).T
    grad = grad_hidden[span].astype(jnp.float32)
    gate_b = (grad * up * chance * (1.0 + gate * (1.0 - chance))).astype(jnp.bfloat16)
    up_b = (grad * swish).astype(jnp.bfloat16)
    gate_out[...] = gate_b
    up_out[...] = up_b
    back_out[...] = (times_t(gate_b, w_gate[...]) + times_t(up_b, w_up[...])).astype(jnp.bfloat16)

    @pl.when(block == group)
    def _():
        copy = pltpu.make_async_copy(resid_ref, resid_out, out_sem.at[0])
        copy.start()
        copy.wait()

    @pl.when(block == 0)
    def _():
        for part in range(min(stages, blocks - 1), blocks):
            pass_on(part)

    @pl.when(block == 1)
    def _():
        for step in range(1, groups):
            pass_copy(step).start()

    @pl.when(block == blocks - 1)
    def _():
        mine = pl.ds(pl.multiple_of(group * rows, rows), rows)
        copies = [
            pltpu.make_async_copy(attn_in.at[:, mine], rows_out, out_sem.at[1]),
            pltpu.make_async_copy(all_ref, all_out, out_sem.at[2]),
        ]
        for copy in copies:
            copy.start()
        for part in range(blocks):
            for step in direct:
                own_copy(part, step).wait_send()
        if line:

            @pl.when(inner)
            def _():
                for part in range(blocks):
                    for slot, step, place in relays:
                        attn_copy(part, step, 1, attn_in.at[slot], place).wait_send()

        spread.wait_send()
        for step in range(1, groups):
            pass_copy(step).wait()
        for copy in copies:
            copy.wait()


def feed_forward(attn, part, w_own, w_gate, w_up, w_down, cotangent, live, tokens, gain, passed, sizes, collective_id):
    dp, groups = sizes
    count, features = tokens.shape
    rows = count // groups
    width, hidden = w_own.shape[0], w_gate.shape[1]
    share = part.shape[1]
    others = groups - 1
    early = 11 * features // 16
    any_spec = pl.BlockSpec(memory_space=pl.ANY)
    by_row = lambda columns: pl.BlockSpec((rows, columns), lambda i: (i, 0))
    by_column = lambda height: pl.BlockSpec((height, rows), lambda i: (0, i))
    flops = 2 * count * features * (groups * width + 6 * hidden)
    return pl.pallas_call(
        functools.partial(feed_forward_kernel, dp, groups),
        grid=(groups,),
        out_shape=[
            jax.ShapeDtypeStruct((features, count), jnp.bfloat16),
            jax.ShapeDtypeStruct((hidden, count), jnp.bfloat16),
            jax.ShapeDtypeStruct((count, hidden), jnp.bfloat16),
            jax.ShapeDtypeStruct((count, hidden), jnp.bfloat16),
            jax.ShapeDtypeStruct((count, features), jnp.bfloat16),
            jax.ShapeDtypeStruct((count, early), jnp.bfloat16),
            jax.ShapeDtypeStruct((count, features - early), jnp.bfloat16),
            jax.ShapeDtypeStruct((rows, features), jnp.float32),
            jax.ShapeDtypeStruct((others, rows, width), jnp.bfloat16),
            jax.ShapeDtypeStruct((others, dp, share, width), jnp.bfloat16),
            jax.ShapeDtypeStruct((others,) + passed.shape, jnp.bfloat16),
        ],
        in_specs=[
            any_spec,
            by_row(width),
            pl.BlockSpec(memory_space=pltpu.VMEM),
            any_spec, any_spec, any_spec, any_spec, any_spec, any_spec,
            by_row(features),
            pl.BlockSpec(memory_space=pltpu.VMEM),
            by_row(1),
            any_spec,
        ],
        out_specs=[
            by_column(features), by_column(hidden), by_row(hidden), by_row(hidden),
            by_row(features), by_row(early), by_row(features - early), any_spec, any_spec, any_spec, any_spec,
        ],
        scratch_shapes=[
            pltpu.VMEM((others, count, width), jnp.bfloat16),
            pltpu.VMEM((others, dp, share, width), jnp.bfloat16),
            pltpu.VMEM((width, features), jnp.bfloat16),
            pltpu.VMEM((features, hidden), jnp.bfloat16),
            pltpu.VMEM((features, hidden), jnp.bfloat16),
            pltpu.VMEM((hidden, features), jnp.bfloat16),
            pltpu.VMEM((count, features), jnp.bfloat16),
            pltpu.VMEM((count, 1), jnp.float32),
            pltpu.VMEM((count, hidden), jnp.bfloat16),
            pltpu.VMEM((rows, features), jnp.float32),
            pltpu.SemaphoreType.DMA((6,)),
            pltpu.SemaphoreType.DMA((groups, groups)),
            pltpu.SemaphoreType.DMA((groups, others)),
            pltpu.SemaphoreType.DMA((2, dp - 1)),
            pltpu.SemaphoreType.DMA((2, dp - 1)),
            pltpu.SemaphoreType.DMA((3,)),
            pltpu.SemaphoreType.DMA((2, groups - 1)),
        ],
        compiler_params=pltpu.CompilerParams(
            collective_id=collective_id, has_side_effects=True, vmem_limit_bytes=VMEM_LIMIT
        ),
        cost_estimate=pl.CostEstimate(flops=flops, bytes_accessed=40 * count * features, transcendentals=0),
    )(attn, attn, part, w_own, w_gate, w_up, w_down, cotangent, live, tokens, gain, live, passed)


class Scatter:
    def __init__(self, dp, product, store, sent, held, late, sems):
        self.product, self.store, self.sent, self.held, self.late = product, store, sent, held, late
        self.first_send, self.first_recv, self.late_send, self.late_recv = sems
        self.me = lax.axis_index("dp")
        self.upper = self.me // 2
        self.bits = dp.bit_length() - 1
        self.slots = dp // 2
        self.halves = row_halves(held.shape[1])

    def bit(self, place):
        return (self.me // 2**place) % 2

    def partner(self, place):
        return self.me + 2**place * (1 - 2 * self.bit(place))

    def first_copy(self, t):
        return pltpu.make_async_remote_copy(
            src_ref=self.sent.at[t],
            dst_ref=self.held.at[t],
            send_sem=self.first_send.at[t],
            recv_sem=self.first_recv.at[t],
            device_id={"dp": self.partner(0)},
            device_id_type=MESH,
        )

    def stage_bit(self, half, stage):
        return stage - 1 if half == 0 else self.bits - 1 - stage

    def slot_of(self, half, stage, index, value):
        if half == 0:
            low = 2 ** (stage - 1)
            return index * 2**stage + value * low + self.upper % low
        top = 2 ** (self.bits - stage)
        return index + value * (top // 2) + (self.upper // top) * top

    def late_copy(self, half, stage, index, slot):
        start, size = self.halves[half]
        buffer = self.slots - 2 ** (self.bits - stage) + index
        return pltpu.make_async_remote_copy(
            src_ref=self.held.at[slot, pl.ds(start, size)],
            dst_ref=self.late[half].at[buffer],
            send_sem=self.late_send.at[half, buffer],
            recv_sem=self.late_recv.at[half, buffer],
            device_id={"dp": self.partner(self.stage_bit(half, stage) + 1)},
            device_id_type=MESH,
        )

    def other_chunks(self):
        def step(t, carry):
            self.sent[t] = self.product(2 * t + 1 - self.bit(0)).astype(jnp.bfloat16)
            self.first_copy(t).start()
            return carry

        lax.fori_loop(0, self.slots, step, 0)

    def slot_at(self, e):
        t = 0
        for place in range(self.bits - 1):
            t = t + 2**place * ((e // 2**place + 1 + self.upper // 2**place) % 2)
        return t

    def own_chunks(self, others_too=False):
        def other(t):
            self.sent[t] = self.product(2 * t + 1 - self.bit(0)).astype(jnp.bfloat16)
            self.first_copy(t).start()

        if others_too:
            other(self.slot_at(0))

        def step(e, carry):
            if others_too:
                pl.when(e + 1 < self.slots)(lambda: other(self.slot_at(e + 1)))
            t = self.slot_at(e)
            own = self.product(2 * t + self.bit(0))
            self.first_copy(t).wait_recv()
            self.held[t] = (self.held[t].astype(jnp.float32) + own).astype(jnp.bfloat16)

            @pl.when(e % 2 == 0)
            def _():
                self.late_copy(0, 1, t // 2, t).start()

            @pl.when(e < self.slots // 2)
            def _():
                self.late_copy(1, 1, t % (self.slots // 2), t).start()

            return carry

        lax.fori_loop(0, self.slots, step, 0)

    def later(self, stage):
        for half in range(2):
            start, size = self.halves[half]
            keep_bit = self.bit(self.stage_bit(half, stage) + 1)
            for index in range(2 ** (self.bits - 1 - stage)):
                slot = self.slot_of(half, stage, index, keep_bit)
                self.late_copy(half, stage, index, slot).wait_recv()
                buffer = self.slots - 2 ** (self.bits - stage) + index
                total = self.held[slot, pl.ds(start, size)].astype(jnp.float32) + self.late[half][
                    buffer
                ].astype(jnp.float32)
                if stage == self.bits - 1:
                    self.store(start, size, total)
                else:
                    self.held[slot, pl.ds(start, size)] = total.astype(jnp.bfloat16)
            if stage < self.bits - 1:
                follow = self.stage_bit(half, stage + 1) + 1
                for index in range(2 ** (self.bits - 2 - stage)):
                    slot = self.slot_of(half, stage + 1, index, 1 - self.bit(follow))
                    self.late_copy(half, stage + 1, index, slot).start()

    def finish(self):
        for t in range(self.slots):
            self.first_copy(t).wait_send()
        for half in range(2):
            for stage in range(1, self.bits):
                for index in range(2 ** (self.bits - 1 - stage)):
                    self.late_copy(half, stage, index, 0).wait_send()


def scatter_scratch(dp, rows, columns):
    slots = dp // 2
    return (
        [pltpu.VMEM((slots, rows, columns), jnp.bfloat16)] * 2
        + [pltpu.VMEM((slots - 1, size, columns), jnp.bfloat16) for _, size in row_halves(rows)]
        + [pltpu.SemaphoreType.DMA((slots,))] * 2
        + [pltpu.SemaphoreType.DMA((2, slots - 1))] * 2
    )


def scatter_from(dp, product, store, refs):
    return Scatter(dp, product, store, refs[0], refs[1], refs[2:4], refs[4:8])


def product_scatter_kernel(count, dp, *refs):
    lhs, rhs = refs[:count], refs[count : 2 * count]
    outs, scratch = refs[2 * count : 3 * count], refs[3 * count :]

    def member(a):
        def product(chunk):
            return times(lhs[a][chunk], rhs[a][...])

        def store(start, size, total):
            outs[a][pl.ds(start, size)] = total

        return scatter_from(dp, product, store, scratch[8 * a : 8 * a + 8])

    members = [member(a) for a in range(count)]
    stages = dp.bit_length() - 1
    greet(dp, 1)
    pending = []
    for a in range(count):
        members[a].own_chunks(others_too=True)
        pending.append((a, 1))
        if a > 0:
            done, stage = pending.pop(0)
            members[done].later(stage)
            if stage < stages - 1:
                pending.append((done, stage + 1))
    while pending:
        done, stage = pending.pop(0)
        members[done].later(stage)
        if stage < stages - 1:
            pending.append((done, stage + 1))
    for one in members:
        one.finish()


def product_scatter(pairs, collective_id):
    count = len(pairs)
    dp = pairs[0][0].shape[0]
    dims = [(lhs.shape[1], rhs.shape[1]) for lhs, rhs in pairs]
    flops = sum(2 * lhs.size * rhs.shape[1] for lhs, rhs in pairs)
    moved = sum(2 * (lhs.size + rhs.size) for lhs, rhs in pairs)
    vmem = pl.BlockSpec(memory_space=pltpu.VMEM)
    any_spec = pl.BlockSpec(memory_space=pl.ANY)
    return pl.pallas_call(
        functools.partial(product_scatter_kernel, count, dp),
        out_shape=[jax.ShapeDtypeStruct(dim, jnp.float32) for dim in dims],
        in_specs=[vmem] * (2 * count),
        out_specs=[vmem] * count,
        scratch_shapes=sum([scatter_scratch(dp, *dim) for dim in dims], []),
        compiler_params=pltpu.CompilerParams(
            collective_id=collective_id, has_side_effects=True, vmem_limit_bytes=VMEM_LIMIT
        ),
        cost_estimate=pl.CostEstimate(flops=flops * 3, bytes_accessed=moved, transcendentals=0),
    )(*[lhs for lhs, _ in pairs], *[rhs for _, rhs in pairs])


def norm_back(values, gain, grads):
    inverse = lax.rsqrt(jnp.mean(values * values, axis=1, keepdims=True) + EPS)
    scaled = gain * grads
    mean = jnp.mean(scaled * values, axis=1, keepdims=True)
    by_values = inverse * scaled - values * (inverse * inverse * inverse * mean)
    return by_values, jnp.sum(grads * values * inverse, axis=0, keepdims=True)


def attention_back_kernel(dp, groups, head_width, *refs):
    (
        back_ref, resid_hbm, cot_hbm, live_ref, tokens_hbm, attn_gain, mlp_gain,
        out_own, out_others, rows_ref, query_ref, key_ref, value_ref, logsum_ref, attn_ref,
        seg_column, seg_row, cosine_t, sine_t, cosine, sine_a, sine_b, qkv_own, pair_own, qkv_parts,
        tokens_out, gains_out, output_out, out_send, grad_out, qkv_all,
        cot_ref, tokens_ref, chunk_ref, weights, query_m, attn_m, key_t, query_t, key_sum, value_sum,
        attn_send, attn_grad, arrived, branch_ref,
        load_sem, last_sem, attn_sems, grad_sems, spread_send, spread_recv, *scatter_refs,
    ) = refs
    group, pack, others = lax.axis_index("kv"), lax.axis_index("dp"), groups - 1
    rows = branch_ref.shape[0]
    width = query_ref.shape[1]
    span_w = key_ref.shape[1]
    pair, half, heads = 2 * head_width, head_width // 2, span_w // head_width
    scale = head_width**-0.5
    mine = pl.ds(pl.multiple_of(group * rows, rows), rows)
    out_part = pl.ds(0, width)

    def load(index, source, target):
        return pltpu.make_async_copy(source, target, load_sem.at[index])

    first_loads = [
        load(0, resid_hbm, tokens_out),
        load(1, cot_hbm.at[mine], cot_ref),
        load(2, out_others, weights.at[:, :, out_part]),
        load(3, qkv_parts, qkv_all.at[:, pack]),
        load(4, tokens_hbm.at[mine], tokens_ref),
    ]
    for one in first_loads:
        one.start()

    spans = width // span_w

    def attn_copy(number, step):
        return to_group(
            step, groups, attn_send.at[number, step - 1], attn_grad.at[number, group], attn_sems.at[number]
        )

    def columns_of(number):
        start = number * span_w
        return pl.ds(start, span_w if number < spans - 1 else width + pair - start)

    def grad_copy(number, step, block):
        columns = columns_of(number)
        return to_group(
            step,
            groups,
            grad_out.at[pl.ds(block * rows, rows), columns],
            arrived.at[step - 1, :, columns],
            grad_sems.at[number],
        )

    share = output_out.shape[0]

    greet(dp, groups)
    spread = Spread(qkv_all, spread_send, spread_recv, dp)
    lanes = lax.broadcasted_iota(jnp.int32, (rows, span_w), 1) // head_width
    first_loads[3].wait()
    spread.start(0)
    first_loads[0].wait()
    first_loads[1].wait()
    values = tokens_out[...]
    grad_resid, mlp_rows = norm_back(values, mlp_gain[...], back_ref[...].astype(jnp.float32))
    grad_resid = grad_resid + cot_ref[...].astype(jnp.float32) * live_ref[mine]
    tokens_out[...] = grad_resid
    branch_ref[...] = grad_resid.astype(jnp.bfloat16)
    stages = dp.bit_length() - 1
    first_loads[2].wait()
    for number in range(spans):
        columns = pl.ds(number * span_w, span_w)
        for step in range(1, groups):
            attn_send[number, step - 1] = times(branch_ref[...], weights[step - 1, :, columns]).astype(
                jnp.bfloat16
            )
            attn_copy(number, step).start()
        attn_grad[number, group] = times_t(branch_ref[...], out_own[columns]).astype(jnp.bfloat16)

    spread.wait_recv(0)
    spread.start(1)

    def store(start, size, total):
        if start == 0:
            output_out[...] = total[:share]
        out_send[pl.ds(start, size)] = total.astype(jnp.bfloat16)

    scatter = scatter_from(dp, lambda chunk: times(chunk_ref[chunk], branch_ref[...]), store, scatter_refs)
    for place in range(groups):
        turned = (attn_ref[mine] if place == 0 else rows_ref[place - 1]).T
        chunk_ref[:, pl.ds(place * share, share)] = turned.reshape(dp, share, rows)
    scatter.other_chunks()
    scatter.own_chunks()
    for block in range(groups):
        part = pl.ds(block * rows, rows)
        key_t[:, part] = key_ref[part, pl.ds(0, pair)].T[:head_width]
    key_sum[...] = jnp.zeros_like(key_sum)
    value_sum[...] = jnp.zeros_like(value_sum)

    def attend(number, block):
        part = pl.ds(block * rows, rows)

        @pl.when(block != group)
        def _():
            step = (group - block + groups) % groups
            landed = attn_grad.at[number, block]
            to_group(step, groups, landed, landed, attn_sems.at[number]).wait_recv()

        query_seg = seg_row[:, part]
        query_place = lax.broadcasted_iota(jnp.int32, (rows, rows), 1) + block * rows

        def wide(entries):
            return jnp.concatenate([entries] * heads, axis=1)

        if True:
            columns = pl.ds(number * span_w, span_w)
            query = query_ref[part, columns]
            grad = attn_grad[number, block]
            weighed = (grad.astype(jnp.float32) * attn_ref[part, columns].astype(jnp.float32)).T
            centres = jnp.sum(weighed.reshape(heads, head_width, rows), axis=1)
            centre = jnp.concatenate([centres[head : head + 1] for head in range(heads)], axis=1)
            logsum = logsum_ref[number * groups + block]
            for head in range(heads):
                place = pl.ds(head * rows, rows)
                query_m[place] = jnp.where(lanes == head, query, 0)
                attn_m[place] = jnp.where(lanes == head, grad, 0)
            query_t[...] = jnp.zeros_like(query_t)

            def keys(piece, carry):
                key_part = pl.ds(pl.multiple_of(piece * rows, rows), rows)
                key_place = lax.broadcasted_iota(jnp.int32, (rows, rows), 0) + piece * rows
                allowed = (seg_column[key_part] == query_seg) & (key_place <= query_place)
                bias = jnp.where(allowed, 0.0, -jnp.inf)
                scores = times_t(key_ref[key_part], query_m[...]) * (scale * LOG2E)
                chance = jnp.exp2(scores - logsum + wide(bias))
                probs = times_t(value_ref[key_part], attn_m[...])
                slope = (chance * (probs - centre)).astype(jnp.bfloat16)
                value_sum[key_part] += times(chance.astype(jnp.bfloat16), attn_m[...])
                key_sum[key_part] += times(slope, query_m[...])
                query_t[...] += times(key_t[:, key_part], slope)
                return carry

            lax.fori_loop(0, block + 1, keys, 0)
            cos, sin = wide(cosine_t[:, part]), wide(sine_t[:, part])
            low, high = query_t[:half] * scale, query_t[half:] * scale
            turned = jnp.concatenate([low * cos + high * sin, high * cos - low * sin], axis=0)
            stacked = jnp.concatenate(
                [turned[:, head * rows : (head + 1) * rows] for head in range(heads)], axis=0
            )
            grad_out[part, columns] = stacked.T.astype(jnp.bfloat16)

        def folded(total):
            sums = total[part, pl.ds(0, pair)]
            for step in range(1, span_w // pair):
                sums = sums + total[part, pl.ds(step * pair, pair)]
            return sums + pltpu.roll(sums, head_width, 1)

        if number == spans - 1:
            grad_k = folded(key_sum) * scale
            grad_k = (
                grad_k * cosine[part]
                - pltpu.roll(grad_k, pair - half, 1) * sine_a[part]
                - pltpu.roll(grad_k, half, 1) * sine_b[part]
            )
            first = lax.broadcasted_iota(jnp.int32, (rows, pair), 1) < head_width
            grad_out[part, pl.ds(width, pair)] = jnp.where(
                first, grad_k, folded(value_sum)
            ).astype(jnp.bfloat16)

        @pl.when(block != group)
        def _():
            grad_copy(number, (block - group + groups) % groups, block).start()

    turns = [(number, block) for number in range(spans) for block in reversed(range(groups))]
    for turn, (number, block) in enumerate(turns):
        attend(number, block)
        if turn == 3:
            for stage in range(1, stages - 1):
                spread.wait_recv(stage)
                spread.start(stage + 1)
    for stage in range(1, stages - 1):
        scatter.later(stage)
    spread.wait_recv(stages - 1)
    part_rows = qkv_all.shape[2]
    last_loads = [
        pltpu.make_async_copy(
            qkv_all.at[:, place], weights.at[:, pl.ds(place * part_rows, part_rows)], last_sem.at[place]
        )
        for place in range(dp)
    ]
    for one in last_loads:
        one.start()
    grad_act = times_t(grad_out[mine, out_part], qkv_own[...])
    grad_act = grad_act + times_t(grad_out[mine, pl.ds(width, pair)], pair_own[...])
    for one in last_loads:
        one.wait()
    for number in range(spans):
        columns = columns_of(number)
        for step in range(1, groups):
            landed = arrived.at[step - 1, :, columns]
            to_group(step, groups, landed, landed, grad_sems.at[number]).wait_recv()
            grad_act = grad_act + times_t(
                arrived[step - 1, :, columns], weights[others - step, :, columns]
            )
    first_loads[4].wait()
    by_tokens, attn_rows = norm_back(tokens_ref[...].astype(jnp.float32), attn_gain[...], grad_act)
    tokens_out[...] += by_tokens
    scatter.later(stages - 1)
    columns = gains_out.shape[2]
    for place in range(dp):
        span = slice(place * columns, (place + 1) * columns)
        gains_out[place, 0:1] = mlp_rows[:, span]
        gains_out[place, 1:2] = attn_rows[:, span]
    for step in range(1, groups):
        for number in range(spans):
            attn_copy(number, step).wait_send()
            grad_copy(number, step, 0).wait_send()
    spread.wait_send()
    scatter.finish()


def attention_back(operands, sizes, head_width, collective_id):
    dp, groups = sizes
    others_w, rows_others, query, key, parts = (operands[index] for index in (8, 9, 10, 11, 24))
    rows, width = rows_others.shape[1:]
    features = others_w.shape[1]
    count, span_w = key.shape
    share = width // dp
    stacked = (span_w // head_width) * rows
    columns = width + 2 * head_width
    vmem = pl.BlockSpec(memory_space=pltpu.VMEM)
    any_spec = pl.BlockSpec(memory_space=pl.ANY)
    bf16, f32 = jnp.bfloat16, jnp.float32
    flops = 2 * count * count * width * 10
    return pl.pallas_call(
        functools.partial(attention_back_kernel, dp, groups, head_width),
        out_shape=[
            jax.ShapeDtypeStruct((rows, features), f32),
            jax.ShapeDtypeStruct((dp, 2, features // dp), f32),
            jax.ShapeDtypeStruct((share, features), f32),
            jax.ShapeDtypeStruct((groups * share, features), bf16),
            jax.ShapeDtypeStruct((count, columns), bf16),
            jax.ShapeDtypeStruct((groups - 1, dp) + parts.shape[1:], bf16),
        ],
        in_specs=[any_spec if index in (1, 2, 4, 8, 24) else vmem for index in range(25)],
        out_specs=[vmem] * 5 + [any_spec],
        scratch_shapes=[
            pltpu.VMEM((rows, features), bf16),
            pltpu.VMEM((rows, features), bf16),
            pltpu.VMEM((dp, groups * share, rows), bf16),
            pltpu.VMEM((groups - 1, features, columns), bf16),
            pltpu.VMEM((stacked, span_w), bf16),
            pltpu.VMEM((stacked, span_w), bf16),
            pltpu.VMEM((head_width, count), bf16),
            pltpu.VMEM((head_width, stacked), f32),
            pltpu.VMEM((count, span_w), f32),
            pltpu.VMEM((count, span_w), f32),
            pltpu.VMEM((width // span_w, groups - 1, rows, span_w), bf16),
            pltpu.VMEM((width // span_w, groups, rows, span_w), bf16),
            pltpu.VMEM((groups - 1, rows, columns), bf16),
            pltpu.VMEM((rows, features), bf16),
            pltpu.SemaphoreType.DMA((5,)),
            pltpu.SemaphoreType.DMA((dp,)),
            pltpu.SemaphoreType.DMA((width // span_w, 2, groups - 1)),
            pltpu.SemaphoreType.DMA((width // span_w, 2, groups - 1)),
            pltpu.SemaphoreType.DMA((2, dp - 1)),
            pltpu.SemaphoreType.DMA((2, dp - 1)),
        ]
        + scatter_scratch(dp, groups * share, features),
        compiler_params=pltpu.CompilerParams(
            collective_id=collective_id, has_side_effects=True, vmem_limit_bytes=VMEM_LIMIT
        ),
        cost_estimate=pl.CostEstimate(flops=flops, bytes_accessed=40 * 2**20, transcendentals=0),
    )(*operands)


def last_sums_kernel(dp, groups, lhs_ref, rhs_ref, gains_ref, output_ref, sums_ref, query_out, key_out, value_out, output_out, gains_out, out_recv, out_sems, near, far, total, near_sems, far_sems, *scatter_refs):
    pack, group = lax.axis_index("dp"), lax.axis_index("kv")

    def store(start, size, value):
        span, width, head_width = pl.ds(start, size), query_out.shape[1], key_out.shape[1]
        query_out[span] = value[:, :width]
        key_out[span] = value[:, width : width + head_width]
        value_out[span] = value[:, width + head_width :]

    scatter = scatter_from(dp, lambda chunk: times(lhs_ref[chunk], rhs_ref[...]), store, scatter_refs)

    share = output_out.shape[0]

    def out_copy(step):
        source = sums_ref.at[pl.ds(step * share, share)]
        return to_group(step, groups, source, out_recv.at[step - 1], out_sems)

    def near_copy(step):
        return pltpu.make_async_remote_copy(
            src_ref=gains_ref,
            dst_ref=near.at[step - 1],
            send_sem=near_sems.at[0, step - 1],
            recv_sem=near_sems.at[1, step - 1],
            device_id={"kv": (group + step) % groups},
            device_id_type=MESH,
        )

    def far_copy(step):
        other = (pack + step) % dp
        return pltpu.make_async_remote_copy(
            src_ref=total.at[other],
            dst_ref=far.at[step - 1],
            send_sem=far_sems.at[0, step - 1],
            recv_sem=far_sems.at[1, step - 1],
            device_id={"dp": other},
            device_id_type=MESH,
        )

    barrier = pltpu.get_barrier_semaphore()
    for step in range(1, dp):
        pl.semaphore_signal(
            barrier, inc=1, device_id={"dp": (pack + step) % dp}, device_id_type=MESH
        )
    for step in range(1, groups):
        pl.semaphore_signal(
            barrier, inc=1, device_id={"kv": (group + step) % groups}, device_id_type=MESH
        )
    pl.semaphore_wait(barrier, dp + groups - 2)
    for step in range(1, groups):
        near_copy(step).start()
        out_copy(step).start()
    scatter.own_chunks(others_too=True)
    value = gains_ref[...]
    for step in range(1, groups):
        near_copy(step).wait_recv()
        value = value + near[step - 1]
    total[...] = value
    for step in range(1, dp):
        far_copy(step).start()
    for stage in range(1, dp.bit_length() - 1):
        scatter.later(stage)
    value = total[pack]
    for step in range(1, dp):
        far_copy(step).wait_recv()
        value = value + far[step - 1]
    gains_out[...] = value
    value = output_ref[...]
    for step in range(1, groups):
        out_copy(step).wait_recv()
        value = value + out_recv[step - 1].astype(jnp.float32)
    output_out[...] = value
    for step in range(1, groups):
        near_copy(step).wait_send()
        out_copy(step).wait_send()
    for step in range(1, dp):
        far_copy(step).wait_send()
    scatter.finish()


def last_sums(lhs, rhs, gains, output, sums, head_width, groups, collective_id):
    dp, rows = lhs.shape[0], lhs.shape[1]
    columns = rhs.shape[1]
    vmem = pl.BlockSpec(memory_space=pltpu.VMEM)
    return pl.pallas_call(
        functools.partial(last_sums_kernel, dp, groups),
        out_shape=[
            jax.ShapeDtypeStruct((rows, columns - 2 * head_width), jnp.float32),
            jax.ShapeDtypeStruct((rows, head_width), jnp.float32),
            jax.ShapeDtypeStruct((rows, head_width), jnp.float32),
            jax.ShapeDtypeStruct(output.shape, jnp.float32),
            jax.ShapeDtypeStruct(gains.shape[1:], jnp.float32),
        ],
        in_specs=[vmem] * 5,
        out_specs=[vmem] * 5,
        scratch_shapes=[
            pltpu.VMEM((groups - 1,) + output.shape, jnp.bfloat16),
            pltpu.SemaphoreType.DMA((2, groups - 1)),
            pltpu.VMEM((groups - 1,) + gains.shape, jnp.float32),
            pltpu.VMEM((dp - 1,) + gains.shape[1:], jnp.float32),
            pltpu.VMEM(gains.shape, jnp.float32),
            pltpu.SemaphoreType.DMA((2, groups - 1)),
            pltpu.SemaphoreType.DMA((2, dp - 1)),
        ]
        + scatter_scratch(dp, rows, columns),
        compiler_params=pltpu.CompilerParams(
            collective_id=collective_id, has_side_effects=True, vmem_limit_bytes=VMEM_LIMIT
        ),
        cost_estimate=pl.CostEstimate(
            flops=2 * lhs.size * columns, bytes_accessed=2 * lhs.size, transcendentals=0
        ),
    )(lhs, rhs, gains, output, sums)


def row_chunks(matrix, count):
    chunks = matrix.reshape(count, matrix.shape[0] // count, matrix.shape[1])
    return jnp.pad(chunks, ((0, 0), (0, -chunks.shape[1] % 16), (0, 0)))


def per_device(
    tokens_in,
    attn_gain,
    w_query,
    w_key,
    w_value,
    w_output,
    mlp_gain,
    w_gate,
    w_up,
    w_down,
    counts,
    segments,
    cotangent,
):
    row_count = tokens_in.shape[0]
    head_width = w_key.shape[1]
    pack_count, group_count = lax.axis_size("dp"), lax.axis_size("kv")
    sizes = (pack_count, group_count)
    pack = lax.axis_index("dp")
    share = w_query.shape[0] // pack_count
    w_pair = jnp.concatenate([w_key, w_value], axis=1)

    def own_share(matrix):
        return lax.dynamic_slice_in_dim(matrix, pack * share, share, 0)

    out_part = lax.dynamic_slice_in_dim(w_output[0], pack * share, share, 1).T
    qkv_part = jnp.concatenate([own_share(w_query), own_share(w_pair)], axis=1)
    live_rows = (jnp.arange(row_count) < counts[0]).astype(jnp.float32)[:, None]
    (
        attn_out,
        act_flipped,
        query,
        key,
        value,
        logsums,
        cosine,
        sine_a,
        sine_b,
        cosine_t,
        sine_t,
        out_parts,
    ) = attention(tokens_in, attn_gain[None], w_query, w_pair, segments, out_part, group_count, 5)
    (
        second_flipped,
        hidden_flipped,
        grad_gate,
        grad_up,
        grad_act_two,
        feed_early,
        feed_late,
        resid_mine,
        attn_others,
        out_others,
        qkv_parts,
    ) = feed_forward(
        attn_out,
        out_parts,
        w_output[0],
        w_gate,
        w_up,
        w_down[0],
        cotangent,
        live_rows,
        tokens_in,
        mlp_gain[None],
        qkv_part,
        sizes,
        1,
    )
    second_chunks = row_chunks(second_flipped, pack_count)
    sent_gate, sent_up, sent_down = product_scatter(
        [
            (second_chunks, grad_gate),
            (second_chunks, grad_up),
            (row_chunks(hidden_flipped, pack_count), cotangent),
        ],
        2,
    )
    grad_two_mine = lax.psum_scatter(grad_act_two, "kv", scatter_dimension=0, tiled=True)
    grad_two_mine, feed_early, sent_down = lax.optimization_barrier(
        (grad_two_mine, feed_early, sent_down)
    )
    grad_tokens, gain_rows, own_output, output_sums, grad_qkv, _ = attention_back(
        (
            grad_two_mine,
            resid_mine,
            cotangent,
            live_rows,
            tokens_in,
            attn_gain[None],
            mlp_gain[None],
            w_output[0],
            out_others.reshape(group_count - 1, -1, w_output.shape[1]),
            attn_others,
            query,
            key,
            value,
            logsums,
            attn_out,
            segments[:, None],
            segments[None],
            cosine_t,
            sine_t,
            cosine,
            sine_a,
            sine_b,
            w_query,
            w_pair,
            qkv_parts,
        ),
        sizes,
        head_width,
        3,
    )
    early_sum = lax.psum_scatter(feed_early, "kv", scatter_dimension=0, tiled=True)
    early_sum, feed_late, grad_qkv = lax.optimization_barrier((early_sum, feed_late, grad_qkv))
    sent_query, sent_key, sent_value, sent_output, gains = last_sums(
        row_chunks(act_flipped, pack_count),
        grad_qkv,
        gain_rows,
        own_output,
        output_sums,
        head_width,
        group_count,
        4,
    )
    sent_two, sent_one = gains[0], gains[1]
    sent_output = sent_output[None]
    sent_down = sent_down[: w_down.shape[1] // pack_count][None]
    late_sum = lax.psum_scatter(feed_late, "kv", scatter_dimension=0, tiled=True)
    feed_sum = jnp.concatenate([early_sum, late_sum], axis=1).astype(jnp.float32)
    layer_out = (resid_mine + feed_sum).astype(jnp.bfloat16)
    return (
        layer_out,
        grad_tokens,
        sent_one,
        sent_query,
        sent_key,
        sent_value,
        sent_output,
        sent_two,
        sent_gate,
        sent_up,
        sent_down,
    )


def solution(mesh):
    return jax.shard_map(
        per_device,
        mesh=mesh,
        in_specs=(
            P("dp", None),
            P(),
            P(None, "kv"),
            P(None, "kv"),
            P(None, "kv"),
            P("kv", None, None),
            P(),
            P(None, "kv"),
            P(None, "kv"),
            P("kv", None, None),
            P("dp"),
            P("dp"),
            P("dp", None),
        ),
        out_specs=(
            P(("dp", "kv"), None),
            P(("dp", "kv"), None),
            P("dp"),
            P("dp", "kv"),
            P("dp", "kv"),
            P("dp", "kv"),
            P("kv", "dp", None),
            P("dp"),
            P("dp", "kv"),
            P("dp", "kv"),
            P("kv", "dp", None),
        ),
        check_vma=False,
    )
```
